32 devices in a mesh: dp: 8 (over z, y), mp: 4 (over x, core).
Axes of the slice: x: 2, y: 2, z: 4, core: 2. Of those that a mesh axis runs over, the one named last changes fastest.
Arguments:
- layer_input: bfloat16 [1024, 16, 1024], P('dp'), may hold values from -6 to 6
- frame_mask: int32 [1024], P('dp'), may hold values 0 or 1
- gain_attn: bfloat16 [2, 1024], P(None, 'dp'), may hold values from 0.099609375 to 1.8984375
- w_query: bfloat16 [2, 1024, 1024], P(None, 'dp', 'mp'), may hold values from -0.1875 to 0.1875
- w_key: bfloat16 [2, 1024, 1024], P(None, 'dp', 'mp'), may hold values from -0.1875 to 0.1875
- w_value: bfloat16 [2, 1024, 1024], P(None, 'dp', 'mp'), may hold values from -0.1875 to 0.1875
- w_out: bfloat16 [2, 1024, 1024], P(None, 'mp', 'dp'), may hold values from -0.375 to 0.375
- gain_ffn: bfloat16 [2, 1024], P(None, 'dp'), may hold values from 0.099609375 to 1.8984375
- w_gate: bfloat16 [2, 1024, 4096], P(None, 'dp', 'mp'), may hold values from -0.1875 to 0.1875
- w_up: bfloat16 [2, 1024, 4096], P(None, 'dp', 'mp'), may hold values from -0.1875 to 0.1875
- w_down: bfloat16 [2, 4096, 1024], P(None, 'mp', 'dp'), may hold values from -0.09375 to 0.09375
- cotangent: bfloat16 [1024, 16, 1024], P('dp'), may hold values from -6 to 6
Outputs:
- output: bfloat16 [1024, 16, 1024], P('dp')
- grad_input: bfloat16 [1024, 16, 1024], P('dp')
- grad_gain_attn: float32 [2, 1024], P(None, 'dp')
- grad_w_query: float32 [2, 1024, 1024], P(None, 'dp', 'mp')
- grad_w_key: float32 [2, 1024, 1024], P(None, 'dp', 'mp')
- grad_w_value: float32 [2, 1024, 1024], P(None, 'dp', 'mp')
- grad_w_out: float32 [2, 1024, 1024], P(None, 'mp', 'dp')
- grad_gain_ffn: float32 [2, 1024], P(None, 'dp')
- grad_w_gate: float32 [2, 1024, 4096], P(None, 'dp', 'mp')
- grad_w_up: float32 [2, 1024, 4096], P(None, 'dp', 'mp')
- grad_w_down: float32 [2, 4096, 1024], P(None, 'mp', 'dp')
The draws below stay inside these ranges and needn't reach their ends.
Inputs may be any that keep to these rules, and one draw needn't show every extreme that they name: `frame_mask`: 1 marks a frame that counts, 0 a padded frame.
All inputs are finite; a program needn't handle non-finite values. No bound on the sum of `frame_mask` on one device may be relied on, other than what follows from the above.
Results may differ from the reference program's by a relative error of at most 0.012.
Values may be sent and summed in bfloat16 or wider, within the bound.
No kernel may reach another device: no remote copies, remote signals or barrier semaphores. Data moves between devices by JAX's collectives and lax.ppermute only.
A program may use at most 192 MiB of HBM per device.

```python
import math
import jax
import jax.numpy as jnp
from jax import lax

D = 1024
HEADS = 16
HDIM = 64
FF = 4096
STEPS = 16
WSETS = 2
FRAMES = 1024


def touch_ends(values, own_key, smallest, high):
    extent = values.shape
    place = [jax.random.randint(jax.random.fold_in(own_key, axis), (), 0, extent[axis]) for axis in range(len(extent))]
    values = values.at[tuple(place)].set(smallest)
    longest = extent.index(max(extent))
    place[longest] = (place[longest] + 1) % extent[longest]
    return values.at[tuple(place)].set(high)


def steps_of(stream_key, shape, cuts, low, top_value):
    level = 1.0
    for dim, blocks in cuts:
        steps = jax.random.uniform(jax.random.fold_in(jax.random.fold_in(stream_key, 6), dim), (blocks,), jnp.float32, low / len(cuts), top_value / len(cuts))
        level = level * jnp.repeat(jnp.exp(steps), shape[dim] // blocks).reshape((-1,) + (1,) * (len(shape) - 1 - dim))
    return level


def scatter_about(own_key, dims, scale, limit, shards=(), kind=jnp.bfloat16):
    array = jax.random.normal(own_key, dims, jnp.float32) * scale
    if len(shards) > 0:
        array = steps_of(own_key, dims, shards, -0.22, 0.18) * array
    return jnp.clip(array, min=-limit, max=limit).astype(kind)


def setup_inputs(seed: int = 0) -> dict:
    keys = jax.random.split(jax.random.key(seed), 13)
    return {
        "layer_input": scatter_about(keys[0], (FRAMES, STEPS, D), 1.0, 6.0, ((0, 8),)),
        "frame_mask": touch_ends((jax.random.randint(keys[1], (FRAMES,), 0, 4) < 3).astype(jnp.int32), jax.random.fold_in(keys[1], 1), 0, 1),
        "gain_attn": jnp.clip(1.0 + 0.18 * jax.random.normal(keys[2], (WSETS, D), jnp.float32), 0.099609375, 1.8984375).astype(jnp.bfloat16),
        "w_query": scatter_about(keys[3], (WSETS, D, D), D ** -0.5, 0.1875, ((1, 8), (2, 4))),
        "w_key": scatter_about(keys[4], (WSETS, D, D), D ** -0.5, 0.1875, ((1, 8), (2, 4))),
        "w_value": scatter_about(keys[5], (WSETS, D, D), D ** -0.5, 0.1875, ((1, 8), (2, 4))),
        "w_out": scatter_about(keys[6], (WSETS, D, D), (D // 4) ** -0.5, 0.375, ((1, 4), (2, 8))),
        "gain_ffn": jnp.clip(1.0 + 0.18 * jax.random.normal(keys[7], (WSETS, D), jnp.float32), 0.099609375, 1.8984375).astype(jnp.bfloat16),
        "w_gate": scatter_about(keys[8], (WSETS, D, FF), D ** -0.5, 0.1875, ((1, 8), (2, 4))),
        "w_up": scatter_about(keys[9], (WSETS, D, FF), D ** -0.5, 0.1875, ((1, 8), (2, 4))),
        "w_down": scatter_about(keys[10], (WSETS, FF, D), FF ** -0.5, 0.09375, ((1, 4), (2, 8))),
        "cotangent": scatter_about(keys[11], (FRAMES, STEPS, D), 1.0, 6.0, ((0, 8),)),
    }


@jax.custom_vjp
def low(v):
    return lax.optimization_barrier(v.astype(jnp.bfloat16)).astype(jnp.float32)

@jax.custom_vjp
def low_back(v):
    return v

def low_keep(v):
    return (low(v), None)

def low_pass(kept, grad):
    return (grad,)

def back_keep(v):
    return (v, None)

def back_low(kept, grad):
    return (low(grad),)
low.defvjp(low_keep, low_pass)
low_back.defvjp(back_keep, back_low)
HIGH = lax.Precision.HIGHEST
EPS = 1e-05
NEG = -1e+30

def steps_gain(gain):
    return jnp.repeat(gain, STEPS // WSETS, axis=0)

def by_set(left, weight):
    frames = left.shape[0]
    split = left.reshape(frames, WSETS, STEPS // WSETS, left.shape[2])
    result = jnp.einsum('fcgk,cke->fcge', split, weight, precision=HIGH)
    return result.reshape(frames, STEPS, weight.shape[2])

def rms_norm(value, gain):
    scale = lax.rsqrt(lax.optimization_barrier(jnp.mean(value * value, axis=-1, keepdims=True)) + EPS)
    return value * scale * steps_gain(gain)

def layer(inputs, gain_attn, w_query, w_key, w_value, w_out, gain_ffn, w_gate, w_up, w_down):
    frames = inputs.shape[0]
    hidden_one = low(rms_norm(inputs, gain_attn))
    query = low(low_back(by_set(hidden_one, w_query))).reshape(frames, STEPS, HEADS, HDIM)
    key = low(low_back(by_set(hidden_one, w_key))).reshape(frames, STEPS, HEADS, HDIM)
    value = low(low_back(by_set(hidden_one, w_value))).reshape(frames, STEPS, HEADS, HDIM)
    scores = low_back(jnp.einsum('fshe,fthe->fhst', query, key, precision=HIGH) * HDIM ** (-0.5))
    causal = jnp.arange(STEPS)[:, None] >= jnp.arange(STEPS)[None, :]
    probs = low(jax.nn.softmax(jnp.where(causal, scores, NEG), axis=-1))
    mixed = jnp.einsum('fhst,fthe->fshe', probs, value, precision=HIGH).reshape(frames, STEPS, D)
    mixed = low(low_back(mixed))
    middle = inputs + low_back(by_set(mixed, w_out))
    hidden_two = low(rms_norm(middle, gain_ffn))
    gate = low_back(by_set(hidden_two, w_gate))
    up = low_back(by_set(hidden_two, w_up))
    inner = low(jax.nn.silu(gate) * up)
    return middle + low_back(by_set(inner, w_down))

def reference(layer_input, frame_mask, gain_attn, w_query, w_key, w_value, w_out, gain_ffn, w_gate, w_up, w_down, cotangent):
    params = tuple((p.astype(jnp.float32) for p in (gain_attn, w_query, w_key, w_value, w_out, gain_ffn, w_gate, w_up, w_down)))
    block = math.gcd(FRAMES, 256)
    count = FRAMES // block
    inputs = layer_input.astype(jnp.float32).reshape(count, block, STEPS, D)
    masked = cotangent.astype(jnp.float32) * frame_mask.astype(jnp.float32)[:, None, None]
    grads_in = masked.reshape(count, block, STEPS, D)
    zeros = tuple((jnp.zeros_like(p) for p in params))

    def one_block(totals, pair):
        block_in, block_grad = pair
        result, pull = jax.vjp(layer, block_in, *params)
        grads = pull(block_grad)
        summed = tuple((t + g for t, g in zip(totals, grads[1:])))
        return (summed, (result, grads[0]))
    totals, (results, grad_rows) = lax.scan(one_block, zeros, (inputs, grads_in))
    output = results.reshape(FRAMES, STEPS, D).astype(jnp.bfloat16)
    grad_input = grad_rows.reshape(FRAMES, STEPS, D).astype(jnp.bfloat16)
    return (output, grad_input, totals[0], totals[1], totals[2], totals[3], totals[4], totals[5], totals[6], totals[7], totals[8])
```

```python
import functools

import jax
import jax.numpy as jnp
from jax import lax
from jax.experimental import pallas as pl
from jax.experimental.pallas import tpu as pltpu
from jax.sharding import PartitionSpec as P

HDIM = 64
EPS = 1e-05
NEG = -1e30
BF = jnp.bfloat16
F32 = jnp.float32
NN = (((1,), (0,)), ((), ()))
NT = (((1,), (1,)), ((), ()))
TN = (((0,), (0,)), ((), ()))
MIB = 1024 * 1024
SUB = 128
PAIR = 2 * HDIM


def mm(left, right, dims=NN):
    return lax.dot_general(left, right, dims, preferred_element_type=F32)


def kernel_call(body, grid, ins, in_specs, outs, out_specs, flops, scratch=(), vmem=56):
    moved = sum(a.size * a.dtype.itemsize for a in ins) + sum(
        o.size * jnp.dtype(o.dtype).itemsize for o in outs
    )
    return pl.pallas_call(
        body,
        grid=grid,
        in_specs=in_specs,
        out_specs=out_specs,
        out_shape=outs,
        scratch_shapes=scratch,
        compiler_params=pltpu.CompilerParams(vmem_limit_bytes=vmem * MIB),
        cost_estimate=pl.CostEstimate(flops=flops, bytes_accessed=moved, transcendentals=0),
    )(*ins)


def whole(shape):
    return pl.BlockSpec(shape, lambda i: (0,) * len(shape))


def rows_of(rows, width):
    return pl.BlockSpec((rows, width), lambda i: (i, 0))


def out_of(shape, kind=BF):
    return jax.ShapeDtypeStruct(shape, kind)


def split_sets(block):
    frames, steps, width = block.shape
    parts = block.reshape(frames, 2, steps // 2, width)
    return [parts[:, c].reshape(frames * steps // 2, width) for c in range(2)]


def join_sets(first, second, frames):
    width = first.shape[1]
    both = [p.reshape(frames, 1, first.shape[0] // frames, width) for p in (first, second)]
    return jnp.concatenate(both, axis=1).reshape(frames, -1, width)


def prepare_body(x_ref, cot_ref, mask_ref, x0, x1, g0, g1):
    for ref, part in zip((x0, x1), split_sets(x_ref[...].astype(F32))):
        ref[...] = part.astype(BF)
    grad = cot_ref[...].astype(F32) * mask_ref[...]
    for ref, part in zip((g0, g1), split_sets(grad)):
        ref[...] = part.astype(BF)


def prepare(x, cot, mask):
    frames, steps, width = x.shape
    block = 16
    half = steps // 2
    cube = pl.BlockSpec((block, steps, width), lambda i: (i, 0, 0))
    flat = rows_of(block * half, width)
    tokens = out_of((frames * half, width))
    return kernel_call(
        prepare_body,
        (frames // block,),
        (x, cot, mask),
        [cube, cube, pl.BlockSpec((block, 1, 1), lambda i: (i, 0, 0))],
        [tokens] * 4,
        [flat] * 4,
        0,
    )


def norm(value):
    scale = lax.rsqrt(jnp.mean(value * value, axis=-1, keepdims=True) + EPS)
    return value * scale, scale


def lanes_low(shape):
    return lax.broadcasted_iota(jnp.int32, shape, 1) < HDIM


def stack_heads(pair):
    low = lanes_low(pair.shape)
    zero = jnp.zeros_like(pair)
    return jnp.concatenate([jnp.where(low, pair, zero), jnp.where(low, zero, pair)], axis=0)


def pick_heads(stacked):
    half = stacked.shape[0] // 2
    low = lanes_low((half, stacked.shape[1]))
    return jnp.where(low, stacked[:half], stacked[half:])


def visible(rows, keys, steps):
    row = lax.broadcasted_iota(jnp.int32, (rows, keys), 0) % SUB
    key = lax.broadcasted_iota(jnp.int32, (rows, keys), 1)
    same = row // steps == (key % SUB) // steps
    if keys == SUB:
        return same & (row >= key)
    return same & ((key < SUB) | (row >= key - SUB))


def softmax(query, keys, steps):
    raw = mm(query, keys, NT) * HDIM ** (-0.5)
    masked = jnp.where(visible(raw.shape[0], raw.shape[1], steps), raw, NEG)
    top = jnp.max(masked, axis=-1, keepdims=True)
    power = jnp.exp(masked - top)
    return power / jnp.sum(power, axis=-1, keepdims=True)


def attend_body(steps, heads_width, later, *refs):
    if later:
        x_ref, w_ref, gain_ref, before_ref, h_ref, qkv_ref, mixed_ref, part_ref = refs
    else:
        x_ref, w_ref, gain_ref, h_ref, qkv_ref, mixed_ref, part_ref = refs
    hw = heads_width
    normed, _ = norm(x_ref[...].astype(F32))
    hidden = (normed * gain_ref[...]).astype(BF)
    h_ref[...] = hidden
    qkv = mm(hidden, w_ref[:, : 3 * hw]).astype(BF)
    qkv_ref[...] = qkv
    for s in range(x_ref.shape[0] // SUB):
        rows = slice(s * SUB, (s + 1) * SUB)
        for j in range(hw // PAIR):
            q, k, v = (qkv[rows, t * hw + j * PAIR : t * hw + (j + 1) * PAIR] for t in range(3))
            if later:
                k_old, v_old = (
                    before_ref[rows, t * hw + j * PAIR : t * hw + (j + 1) * PAIR] for t in (1, 2)
                )
                k = jnp.concatenate([k_old, k], axis=0)
                v = jnp.concatenate([v_old, v], axis=0)
            probs = softmax(stack_heads(q), k, steps).astype(BF)
            mixed_ref[rows, j * PAIR : (j + 1) * PAIR] = pick_heads(mm(probs, v)).astype(BF)
    part_ref[...] = mm(mixed_ref[...], w_ref[:, 3 * hw :], NT).astype(BF)


def attend(x, w, gain, before, steps):
    tokens, width = x.shape
    hw = w.shape[1] // 4
    block = 256
    ins = [x, w, gain]
    specs = [rows_of(block, width), whole(w.shape), whole(gain.shape)]
    if before is not None:
        ins.append(before)
        specs.append(rows_of(block, 3 * hw))
    widths = (width, 3 * hw, hw, width)
    return kernel_call(
        functools.partial(attend_body, steps, hw, before is not None),
        (tokens // block,),
        ins,
        specs,
        [out_of((tokens, n)) for n in widths],
        [rows_of(block, n) for n in widths],
        2 * tokens * width * 4 * hw,
    )


def second_norm_body(x_ref, att_ref, gain_ref, h_ref):
    normed, _ = norm(x_ref[...].astype(F32) + att_ref[...].astype(F32))
    h_ref[...] = (normed * gain_ref[...]).astype(BF)


def second_norm(x, att, gain):
    tokens, width = x.shape
    block = 256
    flat = rows_of(block, width)
    return kernel_call(
        second_norm_body,
        (tokens // block,),
        (x, att, gain),
        [flat, flat, whole(gain.shape)],
        [out_of(x.shape)],
        [flat],
        0,
    )[0]


def hidden_body(h_ref, g_ref, wg_ref, wu_ref, wd_ref, inner_ref, dgate_ref, dup_ref):
    chunk = 256
    for s in range(h_ref.shape[0] // chunk):
        rows = slice(s * chunk, (s + 1) * chunk)
        gate = mm(h_ref[rows], wg_ref[...])
        up = mm(h_ref[rows], wu_ref[...])
        d_inner = mm(g_ref[rows], wd_ref[...])
        sigma = 1.0 / (1.0 + jnp.exp(-gate))
        active = gate * sigma
        inner_ref[rows] = (active * up).astype(BF)
        dup_ref[rows] = (d_inner * active).astype(BF)
        dgate_ref[rows] = (d_inner * up * sigma * (1.0 + gate * (1.0 - sigma))).astype(BF)


def hidden_units(h, g, w):
    tokens, width = h.shape
    units = w.shape[1] // 3
    block = 256
    steps = units // block
    cols = [
        pl.BlockSpec((width, block), lambda i, t=t: (0, t * steps + i)) for t in range(3)
    ]
    flat = pl.BlockSpec((tokens, block), lambda i: (0, i))
    return kernel_call(
        hidden_body,
        (steps,),
        (h, g, w, w, w),
        [whole(h.shape), whole(g.shape)] + cols,
        [out_of((tokens, units))] * 3,
        [flat] * 3,
        6 * tokens * width * units,
    )


def back_units_body(units, dgate_ref, dup_ref, inner_ref, w_ref, dh_ref, out_ref):
    grad = mm(dgate_ref[...], w_ref[:, :units], NT) + mm(dup_ref[...], w_ref[:, units : 2 * units], NT)
    dh_ref[...] = grad.astype(BF)
    out_ref[...] = mm(inner_ref[...], w_ref[:, 2 * units :], NT).astype(BF)


def back_units(d_gate, d_up, inner, w):
    tokens, units = inner.shape
    width = w.shape[0]
    block = 256
    flat = rows_of(block, units)
    wide = rows_of(block, width)
    return kernel_call(
        functools.partial(back_units_body, units),
        (tokens // block,),
        (d_gate, d_up, inner, w),
        [flat] * 3 + [whole(w.shape)],
        [out_of((tokens, width))] * 2,
        [wide] * 2,
        6 * tokens * width * units,
    )


def unit_grads_body(units, h_ref, g_ref, dgate_ref, dup_ref, inner_ref, w_ref):
    w_ref[:, :units] = mm(h_ref[...], dgate_ref[...], TN).astype(BF)
    w_ref[:, units : 2 * units] = mm(h_ref[...], dup_ref[...], TN).astype(BF)
    w_ref[:, 2 * units :] = mm(g_ref[...], inner_ref[...], TN).astype(BF)


def unit_grads(h, g, d_gate, d_up, inner):
    tokens, width = h.shape
    units = inner.shape[1]
    block = 256
    cols = pl.BlockSpec((tokens, block), lambda i: (0, i))
    return kernel_call(
        functools.partial(unit_grads_body, units),
        (width // block,),
        (h, g, d_gate, d_up, inner),
        [cols] * 2 + [whole((tokens, units))] * 3,
        [out_of((width, 3 * units))],
        [rows_of(block, 3 * units)],
        6 * tokens * width * units,
    )[0]


def norm_back(grad_hidden, value, gain):
    normed, scale = norm(value)
    scaled = grad_hidden * gain
    back = scale * (scaled - normed * jnp.mean(scaled * normed, axis=-1, keepdims=True))
    return back, jnp.sum(grad_hidden * normed, axis=0, keepdims=True)


def middle_body(x_ref, att_ref, g_ref, dh_ref, gain_ref, dm_ref, dgain_ref):
    value = x_ref[...].astype(F32) + att_ref[...].astype(F32)
    back, d_gain = norm_back(dh_ref[...].astype(F32), value, gain_ref[...])
    dm_ref[...] = (g_ref[...].astype(F32) + back).astype(BF)

    @pl.when(pl.program_id(0) == 0)
    def _():
        dgain_ref[...] = jnp.zeros_like(dgain_ref)

    dgain_ref[...] += d_gain


def middle_back(x, att, g, dh, gain):
    tokens, width = x.shape
    block = 256
    flat = rows_of(block, width)
    return kernel_call(
        middle_body,
        (tokens // block,),
        (x, att, g, dh, gain),
        [flat] * 4 + [whole(gain.shape)],
        [out_of(x.shape), out_of((1, width), F32)],
        [flat, whole((1, width))],
        0,
    )


def attend_back_body(steps, hw, dm0, dm1, w0, w1, qkv0, qkv1, dqkv0, dqkv1, dh0, dh1):
    scale = HDIM ** (-0.5)
    d_mixed = [mm(d[...], w[:, 3 * hw :]).astype(BF) for d, w in ((dm0, w0), (dm1, w1))]
    for s in range(dm0.shape[0] // SUB):
        rows = slice(s * SUB, (s + 1) * SUB)
        for j in range(hw // PAIR):
            cols = [slice(t * hw + j * PAIR, t * hw + (j + 1) * PAIR) for t in range(3)]
            q0, k0, v0 = (qkv0[rows, c] for c in cols)
            q1, k1, v1 = (qkv1[rows, c] for c in cols)
            keys = (k0, jnp.concatenate([k0, k1], axis=0))
            values = (v0, jnp.concatenate([v0, v1], axis=0))
            d_k, d_v = [], []
            for c, (q, out_ref) in enumerate(((q0, dqkv0), (q1, dqkv1))):
                q_two = stack_heads(q)
                d_two = stack_heads(d_mixed[c][rows, cols[0]])
                soft = softmax(q_two, keys[c], steps)
                d_probs = mm(d_two, values[c], NT)
                inside = jnp.sum(soft * d_probs, axis=-1, keepdims=True)
                d_scores = (soft * (d_probs - inside)).astype(BF)
                d_q = pick_heads(mm(d_scores, keys[c])) * scale
                out_ref[rows, cols[0]] = d_q.astype(BF)
                d_k.append(mm(d_scores, q_two, TN) * scale)
                d_v.append(mm(soft.astype(BF), d_two, TN))
            dqkv0[rows, cols[1]] = (d_k[0] + d_k[1][:SUB]).astype(BF)
            dqkv1[rows, cols[1]] = d_k[1][SUB:].astype(BF)
            dqkv0[rows, cols[2]] = (d_v[0] + d_v[1][:SUB]).astype(BF)
            dqkv1[rows, cols[2]] = d_v[1][SUB:].astype(BF)
    dh0[...] = mm(dqkv0[...], w0[:, : 3 * hw], NT).astype(BF)
    dh1[...] = mm(dqkv1[...], w1[:, : 3 * hw], NT).astype(BF)


def attend_back(dm, w, qkv, steps):
    tokens, width = dm[0].shape
    hw = w[0].shape[1] // 4
    block = 256
    return kernel_call(
        functools.partial(attend_back_body, steps, hw),
        (tokens // block,),
        (*dm, *w, *qkv),
        [rows_of(block, width)] * 2 + [whole(w[0].shape)] * 2 + [rows_of(block, 3 * hw)] * 2,
        [out_of((tokens, 3 * hw))] * 2 + [out_of((tokens, width))] * 2,
        [rows_of(block, 3 * hw)] * 2 + [rows_of(block, width)] * 2,
        4 * tokens * width * 4 * hw,
    )


def attend_grads_body(hw, h_ref, dqkv_ref, dm_ref, mixed_ref, w_ref):
    w_ref[:, : 3 * hw] = mm(h_ref[...], dqkv_ref[...], TN).astype(BF)
    w_ref[:, 3 * hw :] = mm(dm_ref[...], mixed_ref[...], TN).astype(BF)


def attend_grads(h, d_qkv, dm, mixed):
    tokens, width = h.shape
    hw = mixed.shape[1]
    block = 256
    cols = pl.BlockSpec((tokens, block), lambda i: (0, i))
    return kernel_call(
        functools.partial(attend_grads_body, hw),
        (width // block,),
        (h, d_qkv, dm, mixed),
        [cols, whole(d_qkv.shape), cols, whole(mixed.shape)],
        [out_of((width, 4 * hw))],
        [rows_of(block, 4 * hw)],
        2 * tokens * width * 4 * hw,
    )[0]


def output_body(x0, x1, a0, a1, m0, m1, out_ref):
    sums = [
        x[...].astype(F32) + a[...].astype(F32) + m[...].astype(F32)
        for x, a, m in ((x0, a0, m0), (x1, a1, m1))
    ]
    out_ref[...] = join_sets(*sums, out_ref.shape[0]).astype(BF)


def output_of(x, att, mlp, shape):
    frames, steps, width = shape
    block = 32
    flat = rows_of(block * steps // 2, width)
    return kernel_call(
        output_body,
        (frames // block,),
        (*x, *att, *mlp),
        [flat] * 6,
        [out_of(shape)],
        [pl.BlockSpec((block, steps, width), lambda i: (i, 0, 0))],
        0,
    )[0]


def input_body(x0, x1, dm0, dm1, dh0, dh1, gain_ref, out_ref, dgain_ref):
    sums, gains = [], []
    for c, (x, dm, dh) in enumerate(((x0, dm0, dh0), (x1, dm1, dh1))):
        back, d_gain = norm_back(dh[...].astype(F32), x[...].astype(F32), gain_ref[c : c + 1])
        sums.append(dm[...].astype(F32) + back)
        gains.append(d_gain)
    out_ref[...] = join_sets(*sums, out_ref.shape[0]).astype(BF)

    @pl.when(pl.program_id(0) == 0)
    def _():
        dgain_ref[...] = jnp.zeros_like(dgain_ref)

    dgain_ref[...] += jnp.concatenate(gains, axis=0)


def input_back(x, dm, dh, gain, shape):
    frames, steps, width = shape
    block = 32
    flat = rows_of(block * steps // 2, width)
    return kernel_call(
        input_body,
        (frames // block,),
        (*x, *dm, *dh, gain),
        [flat] * 6 + [whole(gain.shape)],
        [out_of(shape), out_of(gain.shape, F32)],
        [pl.BlockSpec((block, steps, width), lambda i: (i, 0, 0)), whole(gain.shape)],
        0,
    )


class Ring:
    def __init__(self, size):
        self.size = size
        half = size // 2
        order = [2 * q for q in range(half)] + [2 * (size - 1 - q) + 1 for q in range(half, size)]
        self.ahead = [(order[q], order[(q + 1) % size]) for q in range(size)]
        self.behind = [(b, a) for a, b in self.ahead]
        me = lax.axis_index("dp")
        self.me = me
        self.place = jnp.where(me % 2 == 0, me // 2, size - 1 - me // 2)

    def owner(self, offset):
        q = lax.rem(self.place + offset + self.size, self.size)
        return jnp.where(q < self.size // 2, 2 * q, 2 * (self.size - 1 - q) + 1)

    def gather(self, first, second):
        n = self.size
        if n > 16:
            return lax.all_gather(first, "dp"), lax.all_gather(second, "dp")
        put = lambda whole_, part, at: lax.dynamic_update_index_in_dim(whole_, part, at, 0)
        a, b = first, second
        all_a = put(jnp.zeros((n, *a.shape), a.dtype), a, self.me)
        all_b = put(jnp.zeros((n, *b.shape), b.dtype), b, self.me)
        for k in range(1, n):
            a = lax.ppermute(a, "dp", self.ahead)
            b = lax.ppermute(b, "dp", self.behind)
            all_a = put(all_a, a, self.owner(-k))
            all_b = put(all_b, b, self.owner(k))
        return all_a, all_b

    def scatter(self, first, second):
        n = self.size
        if n > 16:
            return tuple(
                lax.psum_scatter(g, "dp", scatter_dimension=0).astype(F32) for g in (first, second)
            )
        at = lambda g, offset: lax.dynamic_index_in_dim(g, self.owner(offset), 0, keepdims=False)
        a, b = at(first, -1), at(second, 1)
        for k in range(2, n + 1):
            a = lax.ppermute(a, "dp", self.ahead).astype(F32) + at(first, -k).astype(F32)
            b = lax.ppermute(b, "dp", self.behind).astype(F32) + at(second, k).astype(F32)
            if k < n:
                a, b = a.astype(BF), b.astype(BF)
        return a, b

    def doubling(self, value, join):
        step = 1
        while step < self.size:
            other = lax.ppermute(value, "dp", [(i, i ^ step) for i in range(self.size)])
            value = join(value, other, (self.me // step) % 2)
            step *= 2
        return value


def gather_small(ring, value):
    def join(mine, other, bit):
        return jnp.where(
            bit == 0, jnp.concatenate([mine, other], 0), jnp.concatenate([other, mine], 0)
        )

    return ring.doubling(value[None], join)


def sum_heads(part):
    size = lax.axis_size("mp")
    if size != 4:
        return lax.psum(part, "mp")
    near = [(i, i ^ 1) for i in range(size)]
    far = [(i, i ^ 2) for i in range(size)]
    bit = lax.axis_index("mp") % 2
    halves = part.reshape(2, part.shape[0] // 2, part.shape[1])
    mine = lax.dynamic_index_in_dim(halves, bit, 0, keepdims=False)
    other = lax.dynamic_index_in_dim(halves, 1 - bit, 0, keepdims=False)
    got = lax.ppermute(other, "mp", near)
    mine = (mine.astype(F32) + got.astype(F32)).astype(BF)
    got = lax.ppermute(mine, "mp", far)
    mine = (mine.astype(F32) + got.astype(F32)).astype(BF)
    got = lax.ppermute(mine, "mp", near)
    return jnp.where(
        bit == 0, jnp.concatenate([mine, got], 0), jnp.concatenate([got, mine], 0)
    )


def on_device(
    layer_input, frame_mask, gain_attn, w_query, w_key, w_value, w_out, gain_ffn, w_gate, w_up,
    w_down, cotangent,
):
    frames, steps, width = layer_input.shape
    sets = gain_attn.shape[0]
    ring = Ring(lax.axis_size("dp"))
    n = ring.size
    hw = w_query.shape[2]
    units = w_gate.shape[2]
    own = width // n
    each = steps // sets

    small = jnp.concatenate([gain_attn, gain_ffn], 0).astype(F32)
    gains = gather_small(ring, small).transpose(1, 0, 2).reshape(2 * sets, width)
    g_attn, g_ffn = gains[:sets], gains[sets:]
    attn_own = jnp.concatenate([w_query, w_key, w_value, w_out.transpose(0, 2, 1)], 2)
    ffn_own = jnp.concatenate([w_gate, w_up, w_down.transpose(0, 2, 1)], 2)
    w_attn = [w.reshape(width, 4 * hw) for w in ring.gather(attn_own[0], attn_own[1])]
    w_ffn = []
    for c in range(sets):
        pieces = ring.gather(ffn_own[c, : own // 2], ffn_own[c, own // 2 :])
        w_ffn.append(jnp.stack(pieces, 1).reshape(width, 3 * units))

    mask = frame_mask.astype(F32).reshape(frames, 1, 1)
    x0, x1, g0, g1 = prepare(layer_input, cotangent, mask)
    x, g = (x0, x1), (g0, g1)
    h1, qkv, mixed, att, h2, inner, d_gate, d_up, dm, mlp, w_grads, d_gain_ffn = ([] for _ in range(12))
    for c in range(sets):
        out = attend(x[c], w_attn[c], g_attn[c : c + 1], qkv[0] if c else None, each)
        h1.append(out[0])
        qkv.append(out[1])
        mixed.append(out[2])
        att.append(sum_heads(out[3]))
    for c in range(sets):
        h2.append(second_norm(x[c], att[c], g_ffn[c : c + 1]))
        one, two, three = hidden_units(h2[c], g[c], w_ffn[c])
        dh, partial = back_units(two, three, one, w_ffn[c])
        grads = unit_grads(h2[c], g[c], two, three, one)
        low, d_gain = middle_back(x[c], att[c], g[c], sum_heads(dh), g_ffn[c : c + 1])
        dm.append(low)
        d_gain_ffn.append(d_gain)
        mlp.append(sum_heads(partial))
        blocks = grads.reshape(n, 2, own // 2, 3 * units)
        w_grads.append(jnp.concatenate(ring.scatter(blocks[:, 0], blocks[:, 1]), 0))
    output = output_of(x, att, mlp, layer_input.shape)
    dqkv0, dqkv1, part0, part1 = attend_back(dm, w_attn, qkv, each)
    attn_grads = [
        attend_grads(h1[c], d, dm[c], mixed[c]).reshape(n, own, 4 * hw)
        for c, d in enumerate((dqkv0, dqkv1))
    ]
    dh1 = (sum_heads(part0), sum_heads(part1))
    grad_input, d_gain_attn = input_back(x, dm, dh1, g_attn, layer_input.shape)
    attn_own_grads = jnp.stack(ring.scatter(*attn_grads))
    ffn_own_grads = jnp.stack(w_grads)

    d_gains = jnp.concatenate([d_gain_attn, *d_gain_ffn], 0)
    d_gains = ring.doubling(d_gains, lambda mine, other, bit: mine + other)
    d_gains = lax.dynamic_slice_in_dim(d_gains, ring.me * own, own, 1)
    d_query, d_key, d_value, d_out = (attn_own_grads[..., t * hw : (t + 1) * hw] for t in range(4))
    dw_gate, dw_up, dw_down = (ffn_own_grads[..., t * units : (t + 1) * units] for t in range(3))
    return (
        output, grad_input, d_gains[:sets], d_query, d_key, d_value, d_out.transpose(0, 2, 1),
        d_gains[sets:], dw_gate, dw_up, dw_down.transpose(0, 2, 1),
    )


def solution(mesh):
    rows = P("dp", None, None)
    gain = P(None, "dp")
    into = P(None, "dp", "mp")
    back = P(None, "mp", "dp")
    weights = (gain, into, into, into, back, gain, into, into, back)
    return jax.shard_map(
        on_device,
        mesh=mesh,
        in_specs=(rows, P("dp"), *weights, rows),
        out_specs=(rows, rows, *weights),
        check_vma=False,
    )
```

```python
import functools

import jax
import jax.numpy as jnp
from jax import lax
from jax.experimental import pallas as pl
from jax.experimental.pallas import tpu as pltpu
from jax.sharding import PartitionSpec as P

HDIM = 64
EPS = 1e-05
NEG = -1e30
BF = jnp.bfloat16
F32 = jnp.float32
NN = (((1,), (0,)), ((), ()))
NT = (((1,), (1,)), ((), ()))
TN = (((0,), (0,)), ((), ()))
MIB = 1024 * 1024
SUB = 128
PAIR = 2 * HDIM
ROWS = 256
HBM = pl.BlockSpec(memory_space=pl.ANY)


def mm(left, right, dims=NN):
    return lax.dot_general(left, right, dims, preferred_element_type=F32)


def kernel_call(body, grid, ins, in_specs, outs, out_specs, flops, scratch=(), scalars=None, alias=None):
    moved = sum(a.size * a.dtype.itemsize for a in ins) + sum(
        o.size * jnp.dtype(o.dtype).itemsize for o in outs
    )
    spec = pltpu.PrefetchScalarGridSpec(
        num_scalar_prefetch=0 if scalars is None else 1,
        grid=grid,
        in_specs=in_specs,
        out_specs=out_specs,
        scratch_shapes=scratch,
    )
    args = ins if scalars is None else (scalars, *ins)
    return pl.pallas_call(
        body,
        grid_spec=spec,
        out_shape=outs,
        input_output_aliases=alias or {},
        compiler_params=pltpu.CompilerParams(vmem_limit_bytes=56 * MIB),
        cost_estimate=pl.CostEstimate(flops=flops, bytes_accessed=moved, transcendentals=0),
    )(*args)


def whole(shape):
    return pl.BlockSpec(shape, lambda *i: (0,) * len(shape))


def rows_of(rows, width, start=0):
    return pl.BlockSpec((rows, width), lambda i, *_: (i + start, 0))


def out_of(shape, kind=BF):
    return jax.ShapeDtypeStruct(shape, kind)


def prepare_body(_, x_ref, cot_ref, mask_ref, x0, x1, g0, g1):
    def split(block):
        frames, steps, width = block.shape
        parts = block.reshape(frames, 2, steps // 2, width)
        return [parts[:, c].reshape(frames * steps // 2, width) for c in range(2)]

    for ref, part in zip((x0, x1), split(x_ref[...].astype(F32))):
        ref[...] = part.astype(BF)
    grad = cot_ref[...].astype(F32) * mask_ref[...]
    for ref, part in zip((g0, g1), split(grad)):
        ref[...] = part.astype(BF)


def prepare(x, cot, mask, places, blocks):
    frames, steps, width = x.shape
    cut = width // blocks
    half = frames // 2
    cube = pl.BlockSpec((half, steps, cut), lambda i, t, p: ((i + p[blocks]) % 2, 0, p[t]))
    flat = pl.BlockSpec((half * steps // 2, cut), lambda i, t, p: (i, t))
    mask_spec = pl.BlockSpec((half, 1, 1), lambda i, t, p: ((i + p[blocks]) % 2, 0, 0))
    return kernel_call(
        prepare_body,
        (2, blocks),
        (x, cot, mask),
        [cube, cube, mask_spec],
        [out_of((frames * steps // 2, width))] * 4,
        [flat] * 4,
        0,
        scalars=places,
    )


def pack_attn_body(wq, wk, wv, wo, first, second):
    hw = wq.shape[2]
    for c, ref in enumerate((first, second)):
        for t, w in enumerate((wq, wk, wv)):
            ref[:, t * hw : (t + 1) * hw] = w[c]
        ref[:, 3 * hw :] = wo[c].T


def pack_attn(wq, wk, wv, wo):
    own, hw = wq.shape[1:]
    piece = (own, 4 * hw)
    return kernel_call(
        pack_attn_body,
        (1,),
        (wq, wk, wv, wo),
        [whole(w.shape) for w in (wq, wk, wv, wo)],
        [out_of(piece)] * 2,
        [whole(piece)] * 2,
        0,
    )


def pack_ffn_body(wg, wu, wd, after, first, second):
    units = wg.shape[2]
    half = wg.shape[1] // 2
    for k, ref in enumerate((first, second)):
        rows = slice(k * half, (k + 1) * half)
        ref[:, :units] = wg[0, rows]
        ref[:, units : 2 * units] = wu[0, rows]
    turned = wd[0].T
    first[:, 2 * units :] = turned[:half]
    second[:, 2 * units :] = turned[half:]


def pack_ffn(wg, wu, wd, c, after):
    own, units = wg.shape[1:]
    piece = (own // 2, 3 * units)
    into = pl.BlockSpec((1, own, units), lambda i: (c, 0, 0))
    back = pl.BlockSpec((1, units, own), lambda i: (c, 0, 0))
    return kernel_call(
        pack_ffn_body,
        (1,),
        (wg, wu, wd, after),
        [into, into, back, HBM],
        [out_of(piece)] * 2,
        [whole(piece)] * 2,
        0,
    )


def norm(value):
    scale = lax.rsqrt(jnp.mean(value * value, axis=-1, keepdims=True) + EPS)
    return value * scale, scale


def lanes_low(shape):
    return lax.broadcasted_iota(jnp.int32, shape, 1) < HDIM


def stack_heads(pair):
    low = lanes_low(pair.shape)
    zero = jnp.zeros_like(pair)
    return jnp.concatenate([jnp.where(low, pair, zero), jnp.where(low, zero, pair)], axis=0)


def pick_heads(stacked):
    half = stacked.shape[0] // 2
    low = lanes_low((half, stacked.shape[1]))
    return jnp.where(low, stacked[:half], stacked[half:])


def visible(rows, keys, steps):
    row = lax.broadcasted_iota(jnp.int32, (rows, keys), 0) % SUB
    key = lax.broadcasted_iota(jnp.int32, (rows, keys), 1)
    same = row // steps == (key % SUB) // steps
    if keys == SUB:
        return same & (row >= key)
    return same & ((key < SUB) | (row >= key - SUB))


def softmax(query, keys, steps):
    raw = mm(query, keys, NT) * HDIM ** (-0.5)
    masked = jnp.where(visible(raw.shape[0], raw.shape[1], steps), raw, NEG)
    top = jnp.max(masked, axis=-1, keepdims=True)
    power = jnp.exp(masked - top)
    return power / jnp.sum(power, axis=-1, keepdims=True)


class Pieces:
    def __init__(self, arrays, groups):
        self.arrays = arrays
        self.count = len(arrays)
        self.groups = groups
        self.shape = (sum(a.shape[0] for a in arrays), arrays[0].shape[1])
        self.scratch = [pltpu.VMEM(self.shape, BF), pltpu.SemaphoreType.DMA((groups, self.count))]

    def copies(self, refs, memory, sems, group):
        row = 0
        wide = self.shape[1] // self.groups
        for k, ref in enumerate(refs):
            cols = pl.ds(group * wide, wide)
            rows = pl.ds(row, ref.shape[0])
            yield pltpu.make_async_copy(ref.at[:, cols], memory.at[rows, cols], sems.at[group, k])
            row += ref.shape[0]

    def start(self, refs, memory, sems, order):
        @pl.when(pl.program_id(0) == 0)
        def _():
            for group in order:
                for copy in self.copies(refs, memory, sems, group):
                    copy.start()

    def wait(self, refs, memory, sems, group):
        @pl.when(pl.program_id(0) == 0)
        def _():
            for copy in self.copies(refs, memory, sems, group):
                copy.wait()


def attend_body(pieces, steps, hw, later, *refs):
    x_ref, gain_ref, *refs = refs
    if later:
        before_ref, *refs = refs
    w_refs, refs = refs[: pieces.count], refs[pieces.count :]
    h_ref, qkv_ref, mixed_ref, part_ref, w_ref, sems = refs
    pieces.start(w_refs, w_ref, sems, range(1))
    normed, _ = norm(x_ref[...].astype(F32))
    hidden = (normed * gain_ref[...]).astype(BF)
    h_ref[...] = hidden
    pieces.wait(w_refs, w_ref, sems, 0)
    qkv = mm(hidden, w_ref[:, : 3 * hw]).astype(BF)
    qkv_ref[...] = qkv
    for s in range(x_ref.shape[0] // SUB):
        rows = slice(s * SUB, (s + 1) * SUB)
        for j in range(hw // PAIR):
            q, k, v = (qkv[rows, t * hw + j * PAIR : t * hw + (j + 1) * PAIR] for t in range(3))
            if later:
                k_old, v_old = (
                    before_ref[rows, t * hw + j * PAIR : t * hw + (j + 1) * PAIR] for t in (1, 2)
                )
                k = jnp.concatenate([k_old, k], axis=0)
                v = jnp.concatenate([v_old, v], axis=0)
            probs = softmax(stack_heads(q), k, steps).astype(BF)
            mixed_ref[rows, j * PAIR : (j + 1) * PAIR] = pick_heads(mm(probs, v)).astype(BF)
    part_ref[...] = mm(mixed_ref[...], w_ref[:, 3 * hw :], NT).astype(BF)


def attend(x, gain, before, w, half, steps):
    tokens, width = x.shape[0] // 2, x.shape[1]
    pieces = Pieces(w, 1)
    hw = pieces.shape[1] // 4
    count = tokens // ROWS
    ins = [x, gain]
    specs = [rows_of(ROWS, width, half * count), whole(gain.shape)]
    if before is not None:
        ins.append(before)
        specs.append(rows_of(ROWS, 3 * hw))
    widths = (width, 3 * hw, hw, width)
    return kernel_call(
        functools.partial(attend_body, pieces, steps, hw, before is not None),
        (count,),
        [*ins, *w],
        [*specs, *[HBM] * pieces.count],
        [out_of((tokens, n)) for n in widths],
        [rows_of(ROWS, n) for n in widths],
        2 * tokens * width * 4 * hw,
        pieces.scratch,
    )


def units_body(pieces, units, *refs):
    x_ref, att_ref, g_ref, gain_ref, *refs = refs
    w_refs, refs = refs[: pieces.count], refs[pieces.count :]
    h_ref, inner_ref, dgate_ref, dup_ref, dh_ref, mlp_ref, w_ref, sems = refs
    pieces.start(w_refs, w_ref, sems, (2, 0, 1))
    normed, _ = norm(x_ref[...].astype(F32) + att_ref[...].astype(F32))
    hidden = (normed * gain_ref[...]).astype(BF)
    h_ref[...] = hidden
    for group in (2, 0, 1):
        pieces.wait(w_refs, w_ref, sems, group)
    cut = 256
    for u in range(units // cut):
        cols = [slice(t * units + u * cut, t * units + (u + 1) * cut) for t in range(3)]
        d_inner = mm(g_ref[...], w_ref[:, cols[2]])
        gate = mm(hidden, w_ref[:, cols[0]])
        up = mm(hidden, w_ref[:, cols[1]])
        sigma = 1.0 / (1.0 + jnp.exp(-gate))
        active = gate * sigma
        inner_ref[:, cols[0]] = (active * up).astype(BF)
        dup_ref[:, cols[0]] = (d_inner * active).astype(BF)
        dgate_ref[:, cols[0]] = (d_inner * up * sigma * (1.0 + gate * (1.0 - sigma))).astype(BF)
    grad = mm(dgate_ref[...], w_ref[:, :units], NT) + mm(dup_ref[...], w_ref[:, units : 2 * units], NT)
    dh_ref[...] = grad.astype(BF)
    mlp_ref[...] = mm(inner_ref[...], w_ref[:, 2 * units :], NT).astype(BF)


def hidden_units(x, att, g, gain, w, half):
    tokens, width = att.shape
    pieces = Pieces(w, 3)
    units = pieces.shape[1] // 3
    count = tokens // ROWS
    part = rows_of(ROWS, width, half * count)
    widths = (width, units, units, units, width, width)
    return kernel_call(
        functools.partial(units_body, pieces, units),
        (count,),
        (x, att, g, gain, *w),
        [part, rows_of(ROWS, width), part, whole(gain.shape), *[HBM] * pieces.count],
        [out_of((tokens, n)) for n in widths],
        [rows_of(ROWS, n) for n in widths],
        12 * tokens * width * units,
        pieces.scratch,
    )


def tn_pair(left, right):
    return mm(left[0][...], right[0][...], TN) + mm(left[1][...], right[1][...], TN)


def store_rows(refs, block, rows, cols, value):
    start = 0
    for ref in refs:
        low, high = max(start, block * rows), min(start + ref.shape[0], (block + 1) * rows)
        if low < high:
            ref[low - start : high - start, cols] = value[low - block * rows : high - block * rows]
        start += ref.shape[0]


def grads_body(columns, count, *refs):
    inputs = max(max(r) for _, r in columns) + 1
    outs = refs[inputs:]
    values = [
        tn_pair([refs[k] for k in left], [refs[k] for k in right]).astype(BF) for left, right in columns
    ]
    for block in range(count):

        @pl.when(pl.program_id(0) == block)
        def _():
            at = 0
            for value in values:
                store_rows(outs, block, ROWS, slice(at, at + value.shape[1]), value)
                at += value.shape[1]


def weight_grads(columns, heights):
    ins, specs, places = [], [], []
    for left, right in columns:
        at = []
        for array, start in left:
            ins.append(array)
            rows = array.shape[0] if start is None else array.shape[0] // 2
            specs.append(pl.BlockSpec((rows, ROWS), lambda i, s=start or 0: (s, i)))
            at.append(len(ins) - 1)
        places.append(tuple(at))
    pairs = []
    for (left, right), at in zip(columns, places):
        spot = []
        for array in right:
            ins.append(array)
            specs.append(whole(array.shape))
            spot.append(len(ins) - 1)
        pairs.append((at, tuple(spot)))
    total = sum(right[0].shape[1] for _, right in columns)
    tokens = sum(a.shape[0] for a in columns[0][1])
    width = sum(heights)
    return kernel_call(
        functools.partial(grads_body, pairs, width // ROWS),
        (width // ROWS,),
        ins,
        specs,
        [out_of((n, total)) for n in heights],
        [whole((n, total)) for n in heights],
        2 * tokens * width * total,
    )


def norm_back(grad_hidden, value, gain):
    normed, scale = norm(value)
    scaled = grad_hidden * gain
    back = scale * (scaled - normed * jnp.mean(scaled * normed, axis=-1, keepdims=True))
    return back, jnp.sum(grad_hidden * normed, axis=0, keepdims=True)


def add_up(ref, value):
    @pl.when(pl.program_id(0) == 0)
    def _():
        ref[...] = jnp.zeros_like(ref)

    ref[...] += value


def middle_body(x_ref, att_ref, g_ref, dh_ref, gain_ref, dm_ref, dgain_ref):
    value = x_ref[...].astype(F32) + att_ref[...].astype(F32)
    back, d_gain = norm_back(dh_ref[...].astype(F32), value, gain_ref[...])
    dm_ref[...] = (g_ref[...].astype(F32) + back).astype(BF)
    add_up(dgain_ref, d_gain)


def middle_back(x, att, g, dh, gain, half):
    tokens, width = att.shape
    count = tokens // ROWS
    part, flat = rows_of(ROWS, width, half * count), rows_of(ROWS, width)
    return kernel_call(
        middle_body,
        (count,),
        (x, att, g, dh, gain),
        [part, flat, part, flat, whole(gain.shape)],
        [out_of((tokens, width)), out_of((1, width), F32)],
        [flat, whole((1, width))],
        0,
    )


def attend_back_body(pieces, steps, hw, x0, x1, dm0, dm1, qkv0, qkv1, *refs):
    n = pieces[0].count
    sides = (refs[:n], refs[n : 2 * n])
    dqkv0, dqkv1, dh0, dh1, dgain, w0, sems0, w1, sems1 = refs[2 * n :]
    for p, s, w, sems in zip(pieces, sides, (w0, w1), (sems0, sems1)):
        p.start(s, w, sems, range(1))
    normed = [norm(x[...].astype(F32))[0] for x in (x0, x1)]
    for p, s, w, sems in zip(pieces, sides, (w0, w1), (sems0, sems1)):
        p.wait(s, w, sems, 0)
    scale = HDIM ** (-0.5)
    d_mixed = [mm(d[...], w[:, 3 * hw :]).astype(BF) for d, w in ((dm0, w0), (dm1, w1))]
    for s in range(dm0.shape[0] // SUB):
        rows = slice(s * SUB, (s + 1) * SUB)
        for j in range(hw // PAIR):
            cols = [slice(t * hw + j * PAIR, t * hw + (j + 1) * PAIR) for t in range(3)]
            q0, k0, v0 = (qkv0[rows, c] for c in cols)
            q1, k1, v1 = (qkv1[rows, c] for c in cols)
            keys = (k0, jnp.concatenate([k0, k1], axis=0))
            values = (v0, jnp.concatenate([v0, v1], axis=0))
            d_k, d_v = [], []
            for c, (q, out_ref) in enumerate(((q0, dqkv0), (q1, dqkv1))):
                q_two = stack_heads(q)
                d_two = stack_heads(d_mixed[c][rows, cols[0]])
                soft = softmax(q_two, keys[c], steps)
                d_probs = mm(d_two, values[c], NT)
                inside = jnp.sum(soft * d_probs, axis=-1, keepdims=True)
                d_scores = (soft * (d_probs - inside)).astype(BF)
                d_q = pick_heads(mm(d_scores, keys[c])) * scale
                out_ref[rows, cols[0]] = d_q.astype(BF)
                d_k.append(mm(d_scores, q_two, TN) * scale)
                d_v.append(mm(soft.astype(BF), d_two, TN))
            dqkv0[rows, cols[1]] = (d_k[0] + d_k[1][:SUB]).astype(BF)
            dqkv1[rows, cols[1]] = d_k[1][SUB:].astype(BF)
            dqkv0[rows, cols[2]] = (d_v[0] + d_v[1][:SUB]).astype(BF)
            dqkv1[rows, cols[2]] = d_v[1][SUB:].astype(BF)
    gains = []
    for c, (d, w, out_ref) in enumerate(((dqkv0, w0, dh0), (dqkv1, w1, dh1))):
        grad = mm(d[...], w[:, : 3 * hw], NT)
        out_ref[...] = grad.astype(BF)
        gains.append(jnp.sum(grad * normed[c], axis=0, keepdims=True))
    add_up(dgain, jnp.concatenate(gains, axis=0))


def attend_back(x, dm, qkv, w, half, steps):
    tokens, width = dm[0].shape
    count = tokens // ROWS
    pieces = [Pieces(side, 1) for side in w]
    hw = pieces[0].shape[1] // 4
    part, flat, thin = rows_of(ROWS, width, half * count), rows_of(ROWS, width), rows_of(ROWS, 3 * hw)
    return kernel_call(
        functools.partial(attend_back_body, pieces, steps, hw),
        (count,),
        (*x, *dm, *qkv, *w[0], *w[1]),
        [part] * 2 + [flat] * 2 + [thin] * 2 + [HBM] * (2 * pieces[0].count),
        [out_of((tokens, 3 * hw))] * 2 + [out_of((tokens, width))] * 2 + [out_of((2, width), F32)],
        [thin] * 2 + [flat] * 2 + [whole((2, width))],
        4 * tokens * width * 4 * hw,
        pieces[0].scratch + pieces[1].scratch,
    )


def store_frames(out_ref, sums, places, blocks):
    frames, _, width = out_ref.shape
    cut = width // blocks
    both = [p.reshape(frames, 1, p.shape[0] // frames, width) for p in sums]
    joined = jnp.concatenate(both, axis=1).reshape(frames, -1, width).astype(BF)
    if blocks == 1:
        out_ref[...] = joined
        return
    for t in range(blocks):
        at = pl.multiple_of(places[t] * cut, cut)
        out_ref[:, :, pl.ds(at, cut)] = joined[:, :, t * cut : (t + 1) * cut]


def output_body(blocks, places, x0, x1, a0, a1, m0, m1, *refs):
    sums = [
        x[...].astype(F32) + a[...].astype(F32) + m[...].astype(F32)
        for x, a, m in ((x0, a0, m0), (x1, a1, m1))
    ]
    store_frames(refs[-1], sums, places, blocks)


def input_body(blocks, places, x0, x1, dm0, dm1, dh0, dh1, gain_ref, *refs):
    sums = []
    for c, (x, dm, dh) in enumerate(((x0, dm0, dh0), (x1, dm1, dh1))):
        back, _ = norm_back(dh[...].astype(F32), x[...].astype(F32), gain_ref[c : c + 1])
        sums.append(dm[...].astype(F32) + back)
    store_frames(refs[-1], sums, places, blocks)


def join_frames(body, x, sides, extra, before, half, places, blocks, shape):
    frames, steps, width = shape
    block = 16
    count = frames // 2 // block
    rows = block * steps // 2
    ins = [*x, *sides, *extra]
    specs = [rows_of(rows, width, half * count)] * 2 + [rows_of(rows, width)] * len(sides)
    specs += [whole(e.shape) for e in extra]
    alias = {}
    if before is not None:
        ins.append(before)
        specs.append(HBM)
        alias = {len(ins): 0}
    cube = pl.BlockSpec((block, steps, width), lambda i, p: (i + (half + p[blocks]) % 2 * count, 0, 0))
    return kernel_call(
        functools.partial(body, blocks),
        (count,),
        ins,
        specs,
        [out_of(shape)],
        [cube],
        0,
        scalars=places,
        alias=alias,
    )[0]


def finish_ffn_body(units, *refs):
    ins, (gate, up, down) = refs[:8], refs[8:]
    for c in range(2):
        for k in range(2):
            got, own = ins[4 * c + 2 * k : 4 * c + 2 * k + 2]
            half = got.shape[0]
            total = got[...].astype(F32) + own[...].astype(F32)
            rows = slice(k * half, (k + 1) * half)
            gate[c, rows] = total[:, :units]
            up[c, rows] = total[:, units : 2 * units]
        both = [
            (ins[4 * c + 2 * k][:, 2 * units :].astype(F32) + ins[4 * c + 2 * k + 1][:, 2 * units :].astype(F32))
            for k in range(2)
        ]
        down[c] = jnp.concatenate(both, axis=0).T


def finish_ffn(parts):
    half, total = parts[0].shape
    units = total // 3
    into, back = (2, 2 * half, units), (2, units, 2 * half)
    shapes = (into, into, back)
    return kernel_call(
        functools.partial(finish_ffn_body, units),
        (1,),
        parts,
        [whole(p.shape) for p in parts],
        [out_of(s, F32) for s in shapes],
        [whole(s) for s in shapes],
        0,
    )


def finish_attn_body(hw, *refs):
    ins, outs = refs[:4], refs[4:]
    for c in range(2):
        total = ins[2 * c][...].astype(F32) + ins[2 * c + 1][...].astype(F32)
        for t in range(3):
            outs[t][c] = total[:, t * hw : (t + 1) * hw]
        outs[3][c] = total[:, 3 * hw :].T


def finish_attn(parts):
    own, total = parts[0].shape
    hw = total // 4
    into, back = (2, own, hw), (2, hw, own)
    shapes = (into, into, into, back)
    return kernel_call(
        functools.partial(finish_attn_body, hw),
        (1,),
        parts,
        [whole(p.shape) for p in parts],
        [out_of(s, F32) for s in shapes],
        [whole(s) for s in shapes],
        0,
    )


class Ring:
    def __init__(self, size):
        self.size = size
        self.rings = size <= 16
        half = size // 2
        order = [2 * q for q in range(half)] + [2 * (size - 1 - q) + 1 for q in range(half, size)]
        self.ahead = [(order[q], order[(q + 1) % size]) for q in range(size)]
        self.behind = [(b, a) for a, b in self.ahead]
        self.me = lax.axis_index("dp")
        place = jnp.where(self.me % 2 == 0, self.me // 2, size - 1 - self.me // 2)
        q = lax.rem(place + jnp.arange(size, dtype=jnp.int32), size)
        self.order = jnp.where(q < half, 2 * q, 2 * (size - 1 - q) + 1).astype(jnp.int32)

    def gather(self, first, second):
        n = self.size
        if not self.rings:
            return [lax.all_gather(first, "dp")], [lax.all_gather(second, "dp")]
        a, b = [first], [second]
        for _ in range(1, n):
            a.append(lax.ppermute(a[-1], "dp", self.ahead))
            b.append(lax.ppermute(b[-1], "dp", self.behind))
        return [a[-t % n] for t in range(n)], b

    def scatter(self, first, second):
        n = self.size
        a, b = first[n - 1], second[1]
        for k in range(2, n + 1):
            a = lax.ppermute(a, "dp", self.ahead)
            b = lax.ppermute(b, "dp", self.behind)
            if k < n:
                a = (a.astype(F32) + first[n - k].astype(F32)).astype(BF)
                b = (b.astype(F32) + second[k].astype(F32)).astype(BF)
        return [a, first[0]], [b, second[0]]

    def gather_small(self, value):
        step = 1
        value = value[None]
        while step < self.size:
            other = lax.ppermute(value, "dp", [(i, i ^ step) for i in range(self.size)])
            bit = (self.me // step) % 2
            value = jnp.where(
                bit == 0,
                jnp.concatenate([value, other], 0),
                jnp.concatenate([other, value], 0),
            )
            step *= 2
        return value


def sum_heads(mine, other):
    size = lax.axis_size("mp")
    near = [(i, i ^ 1) for i in range(size)]
    far = [(i, i ^ 2) for i in range(size)]
    got = lax.ppermute(other, "mp", near)
    mine = (mine.astype(F32) + got.astype(F32)).astype(BF)
    got = lax.ppermute(mine, "mp", far)
    mine = (mine.astype(F32) + got.astype(F32)).astype(BF)
    return mine, lax.ppermute(mine, "mp", near)


def on_device(
    layer_input, frame_mask, gain_attn, w_query, w_key, w_value, w_out, gain_ffn, w_gate, w_up,
    w_down, cotangent,
):
    frames, steps, width = layer_input.shape
    sets = gain_attn.shape[0]
    ring = Ring(lax.axis_size("dp"))
    n = ring.size
    own = width // n
    each = steps // sets
    blocks = n if ring.rings else 1
    order = ring.order if ring.rings else jnp.zeros((1,), jnp.int32)
    places = jnp.concatenate([order, (lax.axis_index("mp") % 2).astype(jnp.int32)[None]])

    first, second = pack_attn(w_query, w_key, w_value, w_out)
    w_attn = ring.gather(first, second)
    after = w_attn[1][-2] if ring.rings else first
    w_ffn = []
    for c in range(sets):
        first, second = pack_ffn(w_gate, w_up, w_down, c, after)
        a, b = ring.gather(first, second)
        after = b[-2] if ring.rings else first
        if ring.rings:
            w_ffn.append([piece for pair in zip(a, b) for piece in pair])
        else:
            w_ffn.append([jnp.concatenate([a[0], b[0]], 1).reshape(width, -1)])
    if not ring.rings:
        w_attn = [[w[0].reshape(width, -1)] for w in w_attn]

    small = jnp.concatenate([gain_attn, gain_ffn], 0).astype(F32)
    gains = ring.gather_small(small)
    if ring.rings:
        gains = jnp.take(gains, order, axis=0)
    gains = gains.transpose(1, 0, 2).reshape(2 * sets, width)
    g_attn, g_ffn = gains[:sets], gains[sets:]

    mask = frame_mask.astype(F32).reshape(frames, 1, 1)
    x0, x1, g0, g1 = prepare(layer_input, cotangent, mask, places, blocks)
    x, g = (x0, x1), (g0, g1)
    h1, qkv, mixed, att, h2, inner, d_gate, d_up, dm, mlp = ([[None] * 2 for _ in range(sets)] for _ in range(10))
    for c in range(sets):
        part = [None, None]
        for h in (1, 0):
            before = qkv[0][h] if c else None
            h1[c][h], qkv[c][h], mixed[c][h], part[h] = attend(
                x[c], g_attn[c : c + 1], before, w_attn[c], h, each
            )
        att[c] = sum_heads(*part)
    scattered, d_gain_ffn = [], []
    for c in range(sets):
        dh, out = [None] * 2, [None] * 2
        for h in (1, 0):
            h2[c][h], inner[c][h], d_gate[c][h], d_up[c][h], dh[h], out[h] = hidden_units(
                x[c], att[c][h], g[c], g_ffn[c : c + 1], w_ffn[c], h
            )
        heights = [own // 2] * (2 * n) if ring.rings else [width]
        halves = [(a, None) for a in h2[c]]
        pieces = weight_grads(
            [
                (halves, d_gate[c]),
                (halves, d_up[c]),
                ([(g[c], 0), (g[c], 1)], inner[c]),
            ],
            heights,
        )
        dh = sum_heads(*dh)
        mlp[c] = sum_heads(*out)
        total = 0.0
        for h in range(2):
            dm[c][h], d_gain = middle_back(x[c], att[c][h], g[c], dh[h], g_ffn[c : c + 1], h)
            total = total + d_gain
        d_gain_ffn.append(total)
        if ring.rings:
            sides = ring.scatter(pieces[0::2], pieces[1::2])
            scattered += sides[0] + sides[1]
        else:
            whole_ = lax.psum_scatter(pieces[0], "dp", scatter_dimension=0, tiled=True)
            for part in jnp.split(whole_, 2, 0):
                scattered += [part, jnp.zeros_like(part)]
    d_gate_w, d_up_w, d_down_w = finish_ffn(scattered)
    output = None
    for h in range(2):
        sides = [att[0][h], att[1][h], mlp[0][h], mlp[1][h]]
        output = join_frames(output_body, x, sides, [], output, h, places, blocks, layer_input.shape)

    d_qkv, part = [[None] * 2 for _ in range(sets)], [[None] * 2 for _ in range(sets)]
    d_gain_attn = 0.0
    for h in (1, 0):
        d_qkv[0][h], d_qkv[1][h], part[0][h], part[1][h], d_gain = attend_back(
            x, [d[h] for d in dm], [q[h] for q in qkv], w_attn, h, each
        )
        d_gain_attn = d_gain_attn + d_gain
    sides = []
    for c in range(sets):
        sides.append(
            weight_grads(
                [
                    ([(a, None) for a in h1[c]], d_qkv[c]),
                    ([(a, None) for a in dm[c]], mixed[c]),
                ],
                [own] * n if ring.rings else [width],
            )
        )
    dh1 = [sum_heads(*p) for p in part]
    grad_input = None
    for h in range(2):
        last = [dm[0][h], dm[1][h], dh1[0][h], dh1[1][h]]
        grad_input = join_frames(input_body, x, last, [g_attn], grad_input, h, places, blocks, layer_input.shape)
    if ring.rings:
        first, second = ring.scatter(*sides)
        scattered = first + second
    else:
        scattered = []
        for side in sides:
            part = lax.psum_scatter(side[0], "dp", scatter_dimension=0, tiled=True)
            scattered += [part, jnp.zeros_like(part)]
    d_query, d_key, d_value, d_out = finish_attn(scattered)

    shared = lax.axis_size("mp")
    d_gains = jnp.concatenate([d_gain_attn, *[d / shared for d in d_gain_ffn]], 0)
    d_gains = d_gains.reshape(2 * sets, blocks, width // blocks)
    if ring.rings:
        spots = jnp.argsort(order)
        d_gains = jnp.take(d_gains, spots, axis=1)
    d_gains = lax.psum(d_gains.reshape(2 * sets, width), ("dp", "mp"))
    d_gains = lax.dynamic_slice_in_dim(d_gains, ring.me * own, own, 1)
    return (
        output, grad_input, d_gains[:sets], d_query, d_key, d_value, d_out,
        d_gains[sets:], d_gate_w, d_up_w, d_down_w,
    )


def solution(mesh):
    rows = P("dp", None, None)
    gain = P(None, "dp")
    into = P(None, "dp", "mp")
    back = P(None, "mp", "dp")
    weights = (gain, into, into, into, back, gain, into, into, back)
    return jax.shard_map(
        on_device,
        mesh=mesh,
        in_specs=(rows, P("dp"), *weights, rows),
        out_specs=(rows, rows, *weights),
        check_vma=False,
    )
```

```python
import functools

import jax
import jax.numpy as jnp
from jax import lax
from jax.experimental import pallas as pl
from jax.experimental.pallas import tpu as pltpu
from jax.sharding import PartitionSpec as P

HDIM = 64
EPS = 1e-05
NEG = -1e30
BF = jnp.bfloat16
F32 = jnp.float32
NN = (((1,), (0,)), ((), ()))
NT = (((1,), (1,)), ((), ()))
TN = (((0,), (0,)), ((), ()))
MIB = 1024 * 1024
SUB = 128
PAIR = 2 * HDIM
ROWS = 256
HBM = pl.BlockSpec(memory_space=pl.ANY)


def mm(left, right, dims=NN):
    return lax.dot_general(left, right, dims, preferred_element_type=F32)


def kernel_call(body, grid, ins, in_specs, outs, out_specs, flops, scratch=(), scalars=None, alias=None):
    moved = sum(a.size * a.dtype.itemsize for a in ins) + sum(
        o.size * jnp.dtype(o.dtype).itemsize for o in outs
    )
    spec = pltpu.PrefetchScalarGridSpec(
        num_scalar_prefetch=0 if scalars is None else 1,
        grid=grid,
        in_specs=in_specs,
        out_specs=out_specs,
        scratch_shapes=scratch,
    )
    args = ins if scalars is None else (scalars, *ins)
    return pl.pallas_call(
        body,
        grid_spec=spec,
        out_shape=outs,
        input_output_aliases=alias or {},
        compiler_params=pltpu.CompilerParams(vmem_limit_bytes=56 * MIB),
        cost_estimate=pl.CostEstimate(flops=1, bytes_accessed=1, transcendentals=0),
    )(*args)


def whole(shape):
    return pl.BlockSpec(shape, lambda *i: (0,) * len(shape))


def rows_of(rows, width, start=0):
    return pl.BlockSpec((rows, width), lambda i, *_: (i + start, 0))


def out_of(shape, kind=BF):
    return jax.ShapeDtypeStruct(shape, kind)


class Halves:
    def __init__(self, tokens):
        self.count = tokens // 2 // ROWS
        self.grid = (2 * self.count,)

    def block(self, i, places):
        half = (1 - i // self.count + places[places.shape[0] - 1]) % 2
        return half * self.count + i % self.count

    def both(self, width):
        return pl.BlockSpec((ROWS, width), lambda i, p: (self.block(i, p), 0))

    def pair(self, width):
        return [
            pl.BlockSpec((ROWS, width), lambda i, p: (jnp.maximum(i - self.count, 0), 0)),
            pl.BlockSpec((ROWS, width), lambda i, p: (jnp.minimum(i, self.count - 1), 0)),
        ]

    def pick(self, pair):
        return jnp.where(pl.program_id(0) < self.count, pair[1][...], pair[0][...])

    def put(self, pair, value):
        for k in range(2):

            @pl.when((pl.program_id(0) < self.count) == (k == 1))
            def _():
                pair[k][...] = value


def split_sets(value, sets):
    frames, steps, width = value.shape
    parts = value.reshape(frames, sets, steps // sets, width)
    return [parts[:, c].reshape(-1, width) for c in range(sets)]


def pack_attn_body(wq, wk, wv, wo, first, second):
    hw = wq.shape[2]
    for c, ref in enumerate((first, second)):
        for t, w in enumerate((wq, wk, wv)):
            ref[:, t * hw : (t + 1) * hw] = w[c]
        ref[:, 3 * hw :] = wo[c].T


def pack_attn(wq, wk, wv, wo):
    own, hw = wq.shape[1:]
    piece = (own, 4 * hw)
    return kernel_call(
        pack_attn_body,
        (1,),
        (wq, wk, wv, wo),
        [whole(w.shape) for w in (wq, wk, wv, wo)],
        [out_of(piece)] * 2,
        [whole(piece)] * 2,
        0,
    )


def pack_ffn_body(wg, wu, wd, first, second):
    units = wg.shape[2]
    half = wg.shape[1] // 2
    for k, ref in enumerate((first, second)):
        rows = slice(k * half, (k + 1) * half)
        ref[:, :units] = wg[0, rows]
        ref[:, units : 2 * units] = wu[0, rows]
    turned = wd[0].T
    first[:, 2 * units :] = turned[:half]
    second[:, 2 * units :] = turned[half:]


def pack_ffn(wg, wu, wd, c):
    own, units = wg.shape[1:]
    piece = (own // 2, 3 * units)
    into = pl.BlockSpec((1, own, units), lambda i: (c, 0, 0))
    back = pl.BlockSpec((1, units, own), lambda i: (c, 0, 0))
    return kernel_call(
        pack_ffn_body,
        (1,),
        (wg, wu, wd),
        [into, into, back],
        [out_of(piece)] * 2,
        [whole(piece)] * 2,
        0,
    )


def norm(value):
    scale = lax.rsqrt(jnp.mean(value * value, axis=-1, keepdims=True) + EPS)
    return value * scale, scale


def lanes_low(shape):
    return lax.broadcasted_iota(jnp.int32, shape, 1) < HDIM


def stack_heads(pair):
    low = lanes_low(pair.shape)
    zero = jnp.zeros_like(pair)
    return jnp.concatenate([jnp.where(low, pair, zero), jnp.where(low, zero, pair)], axis=0)


def pick_heads(stacked):
    half = stacked.shape[0] // 2
    low = lanes_low((half, stacked.shape[1]))
    return jnp.where(low, stacked[:half], stacked[half:])


def visible(rows, keys, steps):
    row = lax.broadcasted_iota(jnp.int32, (rows, keys), 0) % SUB
    key = lax.broadcasted_iota(jnp.int32, (rows, keys), 1)
    same = row // steps == (key % SUB) // steps
    if keys == SUB:
        return same & (row >= key)
    return same & ((key < SUB) | (row >= key - SUB))


def softmax(query, keys, steps):
    raw = mm(query, keys, NT) * HDIM ** (-0.5)
    masked = jnp.where(visible(raw.shape[0], raw.shape[1], steps), raw, NEG)
    top = jnp.max(masked, axis=-1, keepdims=True)
    power = jnp.exp(masked - top)
    return power / jnp.sum(power, axis=-1, keepdims=True)


class Pieces:
    def __init__(self, arrays, groups):
        self.arrays = arrays
        self.count = len(arrays)
        self.groups = groups
        self.shape = (sum(a.shape[0] for a in arrays), arrays[0].shape[1])
        self.scratch = [pltpu.VMEM(self.shape, BF), pltpu.SemaphoreType.DMA((groups, self.count))]

    def copies(self, refs, places, memory, sems, group):
        wide = self.shape[1] // self.groups
        cols = pl.ds(group * wide, wide)
        for k, ref in enumerate(refs):
            if self.count == 1:
                start = 0
            else:
                parts = self.count // (places.shape[0] - 1)
                start = (places[k // parts] * parts + k % parts) * ref.shape[0]
                start = pl.multiple_of(start, ref.shape[0])
            rows = pl.ds(start, ref.shape[0])
            yield pltpu.make_async_copy(ref.at[:, cols], memory.at[rows, cols], sems.at[group, k])

    def start(self, refs, places, memory, sems, order):
        @pl.when(pl.program_id(0) == 0)
        def _():
            for group in order:
                for copy in self.copies(refs, places, memory, sems, group):
                    copy.start()

    def wait(self, refs, places, memory, sems, group):
        @pl.when(pl.program_id(0) == 0)
        def _():
            for copy in self.copies(refs, places, memory, sems, group):
                copy.wait()


def attend_body(pieces, halves, steps, hw, later, places, *refs):
    x_ref, gain_ref, *refs = refs
    if later:
        before_ref, *refs = refs
    w_refs, refs = refs[: pieces.count], refs[pieces.count :]
    h_ref, qkv_ref, mixed_ref, mine_ref, other_ref, w_ref, sems = refs
    pieces.start(w_refs, places, w_ref, sems, range(1))
    normed, _ = norm(x_ref[...].astype(F32))
    hidden = (normed * gain_ref[...]).astype(BF)
    h_ref[...] = hidden
    pieces.wait(w_refs, places, w_ref, sems, 0)
    qkv = mm(hidden, w_ref[:, : 3 * hw]).astype(BF)
    qkv_ref[...] = qkv
    for s in range(x_ref.shape[0] // SUB):
        rows = slice(s * SUB, (s + 1) * SUB)
        for j in range(hw // PAIR):
            q, k, v = (qkv[rows, t * hw + j * PAIR : t * hw + (j + 1) * PAIR] for t in range(3))
            if later:
                k_old, v_old = (
                    before_ref[rows, t * hw + j * PAIR : t * hw + (j + 1) * PAIR] for t in (1, 2)
                )
                k = jnp.concatenate([k_old, k], axis=0)
                v = jnp.concatenate([v_old, v], axis=0)
            probs = softmax(stack_heads(q), k, steps).astype(BF)
            mixed_ref[rows, j * PAIR : (j + 1) * PAIR] = pick_heads(mm(probs, v)).astype(BF)
    halves.put((mine_ref, other_ref), mm(mixed_ref[...], w_ref[:, 3 * hw :], NT).astype(BF))


def attend(places, x, gain, before, w, steps):
    tokens, width = x.shape
    pieces, halves = Pieces(w, 1), Halves(tokens)
    hw = pieces.shape[1] // 4
    ins = [x, gain]
    specs = [halves.both(width), whole(gain.shape)]
    if before is not None:
        ins.append(before)
        specs.append(halves.both(3 * hw))
    widths = (width, 3 * hw, hw)
    *out, mine, other = kernel_call(
        functools.partial(attend_body, pieces, halves, steps, hw, before is not None),
        halves.grid,
        [*ins, *w],
        [*specs, *[HBM] * pieces.count],
        [out_of((tokens, n)) for n in widths] + [out_of((tokens // 2, width))] * 2,
        [halves.both(n) for n in widths] + halves.pair(width),
        2 * tokens * width * 4 * hw,
        pieces.scratch,
        places,
    )
    return *out, (mine, other)


def units_body(pieces, halves, units, places, *refs):
    x_ref, att0, att1, g_ref, gain_ref, *refs = refs
    w_refs, refs = refs[: pieces.count], refs[pieces.count :]
    h_ref, inner_ref, dgate_ref, dup_ref, dh0, dh1, mlp0, mlp1, w_ref, sems = refs
    pieces.start(w_refs, places, w_ref, sems, (2, 0, 1))
    normed, _ = norm(x_ref[...].astype(F32) + halves.pick((att0, att1)).astype(F32))
    hidden = (normed * gain_ref[...]).astype(BF)
    h_ref[...] = hidden
    cut = 256
    cols = [
        [slice(t * units + u * cut, t * units + (u + 1) * cut) for t in range(3)] for u in range(units // cut)
    ]
    pieces.wait(w_refs, places, w_ref, sems, 2)
    d_inners = [mm(g_ref[...], w_ref[:, c[2]]) for c in cols]
    pieces.wait(w_refs, places, w_ref, sems, 0)
    pieces.wait(w_refs, places, w_ref, sems, 1)
    for c, d_inner in zip(cols, d_inners):
        gate = mm(hidden, w_ref[:, c[0]])
        up = mm(hidden, w_ref[:, c[1]])
        sigma = 1.0 / (1.0 + jnp.exp(-gate))
        active = gate * sigma
        inner_ref[:, c[0]] = (active * up).astype(BF)
        dup_ref[:, c[0]] = (d_inner * active).astype(BF)
        dgate_ref[:, c[0]] = (d_inner * up * sigma * (1.0 + gate * (1.0 - sigma))).astype(BF)
    grad = mm(dgate_ref[...], w_ref[:, :units], NT) + mm(dup_ref[...], w_ref[:, units : 2 * units], NT)
    halves.put((dh0, dh1), grad.astype(BF))
    halves.put((mlp0, mlp1), mm(inner_ref[...], w_ref[:, 2 * units :], NT).astype(BF))


def hidden_units(places, x, att, g, gain, w):
    tokens, width = x.shape
    pieces, halves = Pieces(w, 3), Halves(tokens)
    units = pieces.shape[1] // 3
    part = halves.both(width)
    widths = (width, units, units, units)
    *out, dh0, dh1, mlp0, mlp1 = kernel_call(
        functools.partial(units_body, pieces, halves, units),
        halves.grid,
        (x, *att, g, gain, *w),
        [part, *halves.pair(width), part, whole(gain.shape), *[HBM] * pieces.count],
        [out_of((tokens, n)) for n in widths] + [out_of((tokens // 2, width))] * 4,
        [halves.both(n) for n in widths] + halves.pair(width) * 2,
        12 * tokens * width * units,
        pieces.scratch,
        places,
    )
    return *out, (dh0, dh1), (mlp0, mlp1)


def grads_body(columns, parts, steps, places, *refs):
    inputs = max(right for _, right in columns) + 1
    ins, outs = refs[:inputs], refs[inputs:]
    values = []
    for slots, k in columns:
        rows = [ins[s][...] for s in slots]
        rows = jnp.concatenate(rows, axis=1) if len(rows) > 1 else rows[0]
        values.append(mm(rows, ins[k][...], TN).astype(BF))
    if parts == 0:
        at = 0
        for value in values:
            outs[0][:, at : at + value.shape[1]] = value
            at += value.shape[1]
        return
    *outs, buffer, sems = outs
    height = outs[0].shape[0]
    per = buffer.shape[1] // height

    def copies(block):
        for k in range(per):
            rows = buffer.at[block % 2, pl.ds(k * height, height)]
            yield pltpu.make_async_copy(rows, outs[block * per + k], sems.at[block % 2, k])

    for block in range(steps):

        @pl.when(pl.program_id(0) == block)
        def _():
            if block >= 2:
                for copy in copies(block - 2):
                    copy.wait()
            at = 0
            for value in values:
                buffer[block % 2, :, at : at + value.shape[1]] = value
                at += value.shape[1]
            for copy in copies(block):
                copy.start()
            if block == steps - 1:
                for last in range(max(0, steps - 2), steps):
                    for copy in copies(last):
                        copy.wait()


def weight_grads(places, columns, parts):
    count = places.shape[0] - 1
    tokens, width = columns[0][0].shape
    own = width // count
    steps = width // ROWS
    slots = ROWS // own if parts else 1
    ins, specs, marks = [], [], []
    for left, _ in columns:
        mark = []
        for k in range(slots):
            place = (lambda i, p, k=k: (0, p[i * slots + k])) if parts else (lambda i, p: (0, i))
            ins.append(left)
            specs.append(pl.BlockSpec((tokens, ROWS // slots), place))
            mark.append(len(ins) - 1)
        marks.append(tuple(mark))
    pairs = []
    for (_, right), mark in zip(columns, marks):
        ins.append(right)
        specs.append(whole(right.shape))
        pairs.append((mark, len(ins) - 1))
    total = sum(right.shape[1] for _, right in columns)
    if parts:
        outs = [out_of((own // parts, total))] * (parts * count)
        out_specs = [HBM] * len(outs)
        scratch = [pltpu.VMEM((2, ROWS, total), BF), pltpu.SemaphoreType.DMA((2, slots * parts))]
    else:
        outs, out_specs, scratch = [out_of((width, total))], [rows_of(ROWS, total)], []
    return kernel_call(
        functools.partial(grads_body, pairs, parts, steps),
        (steps,),
        ins,
        specs,
        outs,
        out_specs,
        2 * tokens * width * total,
        scratch,
        places,
    )


def norm_back(grad_hidden, value, gain):
    normed, scale = norm(value)
    scaled = grad_hidden * gain
    back = scale * (scaled - normed * jnp.mean(scaled * normed, axis=-1, keepdims=True))
    return back, jnp.sum(grad_hidden * normed, axis=0, keepdims=True)


def add_up(ref, value):
    @pl.when(pl.program_id(0) == 0)
    def _():
        ref[...] = jnp.zeros_like(ref)

    ref[...] += value


def middle_body(halves, _, x_ref, att0, att1, g_ref, dh0, dh1, gain_ref, dm_ref, dgain_ref):
    value = x_ref[...].astype(F32) + halves.pick((att0, att1)).astype(F32)
    back, d_gain = norm_back(halves.pick((dh0, dh1)).astype(F32), value, gain_ref[...])
    dm_ref[...] = (g_ref[...].astype(F32) + back).astype(BF)
    add_up(dgain_ref, d_gain)


def middle_back(places, x, att, g, dh, gain):
    tokens, width = x.shape
    halves = Halves(tokens)
    part, pair = halves.both(width), halves.pair(width)
    return kernel_call(
        functools.partial(middle_body, halves),
        halves.grid,
        (x, *att, g, *dh, gain),
        [part, *pair, part, *pair, whole(gain.shape)],
        [out_of((tokens, width)), out_of((1, width), F32)],
        [part, whole((1, width))],
        0,
        (),
        places,
    )


def attend_back_body(pieces, steps, hw, places, x0, x1, dm0, dm1, qkv0, qkv1, *refs):
    n = pieces[0].count
    sides = (refs[:n], refs[n : 2 * n])
    dqkv0, dqkv1, mine, other, dgain, w0, sems0, w1, sems1 = refs[-9:]
    for p, s, w, sems in zip(pieces, sides, (w0, w1), (sems0, sems1)):
        p.start(s, places, w, sems, range(1))
    normed = [norm(x[...].astype(F32))[0] for x in (x0, x1)]
    for p, s, w, sems in zip(pieces, sides, (w0, w1), (sems0, sems1)):
        p.wait(s, places, w, sems, 0)
    scale = HDIM ** (-0.5)
    d_mixed = [mm(d[...], w[:, 3 * hw :]).astype(BF) for d, w in ((dm0, w0), (dm1, w1))]
    for s in range(dm0.shape[0] // SUB):
        rows = slice(s * SUB, (s + 1) * SUB)
        for j in range(hw // PAIR):
            cols = [slice(t * hw + j * PAIR, t * hw + (j + 1) * PAIR) for t in range(3)]
            q0, k0, v0 = (qkv0[rows, c] for c in cols)
            q1, k1, v1 = (qkv1[rows, c] for c in cols)
            keys = (k0, jnp.concatenate([k0, k1], axis=0))
            values = (v0, jnp.concatenate([v0, v1], axis=0))
            d_k, d_v = [], []
            for c, (q, out_ref) in enumerate(((q0, dqkv0), (q1, dqkv1))):
                q_two = stack_heads(q)
                d_two = stack_heads(d_mixed[c][rows, cols[0]])
                soft = softmax(q_two, keys[c], steps)
                d_probs = mm(d_two, values[c], NT)
                inside = jnp.sum(soft * d_probs, axis=-1, keepdims=True)
                d_scores = (soft * (d_probs - inside)).astype(BF)
                d_q = pick_heads(mm(d_scores, keys[c])) * scale
                out_ref[rows, cols[0]] = d_q.astype(BF)
                d_k.append(mm(d_scores, q_two, TN) * scale)
                d_v.append(mm(soft.astype(BF), d_two, TN))
            dqkv0[rows, cols[1]] = (d_k[0] + d_k[1][:SUB]).astype(BF)
            dqkv1[rows, cols[1]] = d_k[1][SUB:].astype(BF)
            dqkv0[rows, cols[2]] = (d_v[0] + d_v[1][:SUB]).astype(BF)
            dqkv1[rows, cols[2]] = d_v[1][SUB:].astype(BF)
    gains = []
    for c, (d, w) in enumerate(((dqkv0, w0), (dqkv1, w1))):
        grad = mm(d[...], w[:, : 3 * hw], NT)
        gains.append(jnp.sum(grad * normed[c], axis=0, keepdims=True))
        for k, ref in enumerate((other, mine)):

            @pl.when(pl.program_id(0) == k)
            def _():
                ref[c * ROWS : (c + 1) * ROWS] = grad.astype(BF)

    add_up(dgain, jnp.concatenate(gains, axis=0))


def attend_back(places, x, dm, qkv, w, part, before, steps):
    tokens, width = dm[0].shape
    halves = Halves(tokens)
    pieces = [Pieces(side, 1) for side in w]
    hw = pieces[0].shape[1] // 4
    spot = lambda i, p: (halves.block(i * halves.count, p) + part, 0)
    flat, thin = pl.BlockSpec((ROWS, width), spot), pl.BlockSpec((ROWS, 3 * hw), spot)
    ins = [*x, *dm, *qkv, *w[0], *w[1], *(before or ())]
    specs = [flat] * 4 + [thin] * 2 + [HBM] * (len(ins) - 6)
    alias = {len(ins) - 1: 0, len(ins): 1} if before else {}
    d0, d1, mine, other, d_gain = kernel_call(
        functools.partial(attend_back_body, pieces, steps, hw),
        (2,),
        ins,
        specs,
        [out_of((tokens, 3 * hw))] * 2 + [out_of((2 * ROWS, width))] * 2 + [out_of((2, width), F32)],
        [thin] * 2 + [whole((2 * ROWS, width))] * 2 + [whole((2, width))],
        8 * ROWS * width * 4 * hw,
        pieces[0].scratch + pieces[1].scratch,
        places,
        alias,
    )
    return (d0, d1), (mine, other), d_gain


def store_frames(out_ref, sums):
    frames, _, width = out_ref.shape
    both = [p.reshape(frames, 1, p.shape[0] // frames, width) for p in sums]
    out_ref[...] = jnp.concatenate(both, axis=1).reshape(frames, -1, width).astype(BF)


def output_body(halves, _, x0, x1, *refs):
    *refs, out_ref = refs
    pairs = [halves.pick(refs[k : k + 2]).astype(F32) for k in range(0, 8, 2)]
    sums = [x[...].astype(F32) + pairs[2 * c] + pairs[2 * c + 1] for c, x in enumerate((x0, x1))]
    store_frames(out_ref, sums)


def output_of(places, x, att, mlp, shape):
    frames, steps, width = shape
    halves = Halves(x[0].shape[0])
    sides = [a for c in range(2) for pair in (att[c], mlp[c]) for a in pair]
    cube = pl.BlockSpec((2 * ROWS // steps, steps, width), lambda i, p: (halves.block(i, p), 0, 0))
    return kernel_call(
        functools.partial(output_body, halves),
        halves.grid,
        [*x, *sides],
        [halves.both(width)] * 2 + halves.pair(width) * 4,
        [out_of(shape)],
        [cube],
        0,
        (),
        places,
    )[0]


def input_body(_, x0, x1, dm0, dm1, mine, other, gain_ref, *refs):
    first = pl.program_id(0) == 0
    sums = []
    for c, (x, dm) in enumerate(((x0, dm0), (x1, dm1))):
        rows = slice(c * ROWS, (c + 1) * ROWS)
        dh = jnp.where(first, other[rows], mine[rows]).astype(F32)
        back, _ = norm_back(dh, x[...].astype(F32), gain_ref[c : c + 1])
        sums.append(dm[...].astype(F32) + back)
    store_frames(refs[-1], sums)


def input_back(places, x, dm, dh, gain, part, before, shape):
    frames, steps, width = shape
    halves = Halves(x[0].shape[0])
    block = lambda i, p: halves.block(i * halves.count, p) + part
    flat = pl.BlockSpec((ROWS, width), lambda i, p: (block(i, p), 0))
    cube = pl.BlockSpec((2 * ROWS // steps, steps, width), lambda i, p: (block(i, p), 0, 0))
    ins = [*x, *dm, *dh, gain]
    specs = [flat] * 4 + [whole(d.shape) for d in dh] + [whole(gain.shape)]
    alias = {}
    if before is not None:
        ins.append(before)
        specs.append(HBM)
        alias = {len(ins): 0}
    return kernel_call(input_body, (2,), ins, specs, [out_of(shape)], [cube], 0, (), places, alias)[0]


def add_terms(refs):
    total = refs[0][...].astype(F32)
    for ref in refs[1:]:
        total = total + ref[...].astype(F32)
    return total


def finish_body(layout, turned, *refs):
    count = sum(len(terms) for side in layout for terms in side)
    ins, outs = list(refs[:count]), refs[count:]
    wide = ins[0].shape[1] // len(outs)
    for c, side in enumerate(layout):
        sums = []
        for terms in side:
            sums.append(add_terms([ins.pop(0) for _ in terms]))
        total = jnp.concatenate(sums, axis=0) if len(sums) > 1 else sums[0]
        for t, ref in enumerate(outs):
            part = total[:, t * wide : (t + 1) * wide]
            ref[c] = part.T if t == turned else part


def finish(sides, kinds):
    arrays = [a for side in sides for terms in side for a in terms]
    own = sum(terms[0].shape[0] for terms in sides[0])
    wide = arrays[0].shape[1] // kinds
    shapes = [(len(sides), own, wide)] * (kinds - 1) + [(len(sides), wide, own)]
    layout = [[[0] * len(terms) for terms in side] for side in sides]
    return kernel_call(
        functools.partial(finish_body, layout, kinds - 1),
        (1,),
        arrays,
        [whole(a.shape) for a in arrays],
        [out_of(s, F32) for s in shapes],
        [whole(s) for s in shapes],
        0,
    )


class Ring:
    def __init__(self, size):
        self.size = size
        self.rings = size <= 16
        half = size // 2
        order = [2 * q for q in range(half)] + [2 * (size - 1 - q) + 1 for q in range(half, size)]
        self.ahead = [(order[q], order[(q + 1) % size]) for q in range(size)]
        self.behind = [(b, a) for a, b in self.ahead]
        self.me = lax.axis_index("dp")
        place = jnp.where(self.me % 2 == 0, self.me // 2, size - 1 - self.me // 2)
        q = lax.rem(place + jnp.arange(size, dtype=jnp.int32), size)
        self.order = jnp.where(q < half, 2 * q, 2 * (size - 1 - q) + 1).astype(jnp.int32)


class Rounds:
    def __init__(self):
        self.done = ()

    def now(self, value):
        return lax.optimization_barrier((value, *self.done))[0] if self.done else value

    def close(self, *arrays):
        self.done = arrays


class Gather:
    def __init__(self, rounds, ring, first, second):
        self.rounds, self.ring, self.a, self.b = rounds, ring, [first], [second]

    def step(self):
        self.a.append(lax.ppermute(self.rounds.now(self.a[-1]), "dp", self.ring.ahead))
        self.b.append(lax.ppermute(self.rounds.now(self.b[-1]), "dp", self.ring.behind))
        return self.a[-1], self.b[-1]

    def slots(self):
        return [self.a[-t % self.ring.size] for t in range(self.ring.size)], self.b


class Scatter:
    def __init__(self, rounds, ring, first, second):
        self.rounds, self.ring, self.first, self.second = rounds, ring, first, second
        self.a, self.b = first[-1], second[1]
        self.k = 1

    def step(self):
        n = self.ring.size
        self.k += 1
        if self.k > 2:
            self.a = (self.a.astype(F32) + self.first[n - self.k + 1].astype(F32)).astype(BF)
            self.b = (self.b.astype(F32) + self.second[self.k - 1].astype(F32)).astype(BF)
        self.a = lax.ppermute(self.rounds.now(self.a), "dp", self.ring.ahead)
        self.b = lax.ppermute(self.rounds.now(self.b), "dp", self.ring.behind)
        return self.a, self.b

    def sums(self):
        return [self.a, self.first[0]], [self.b, self.second[0]]


class HeadSum:
    def __init__(self, rounds, pair):
        size = lax.axis_size("mp")
        self.rounds, self.pair = rounds, pair
        self.near_moves = [(i, i ^ 1) for i in range(size)]
        self.far_moves = [(i, i ^ 2) for i in range(size)]

    def add(self, one, two):
        return (one.astype(F32) + two.astype(F32)).astype(BF)

    def near(self):
        got = lax.ppermute(self.rounds.now(self.pair[1]), "mp", self.near_moves)
        self.mine = self.add(self.pair[0], got)
        return self.mine

    def far(self):
        self.got = lax.ppermute(self.rounds.now(self.mine), "mp", self.far_moves)
        return self.got

    def last(self):
        self.mine = self.add(self.mine, self.rounds.now(self.got))
        self.sum = (self.mine, lax.ppermute(self.mine, "mp", self.near_moves))
        return self.sum[1]


def exchange_steps(axes):
    for axis in axes:
        size, step = lax.axis_size(axis), 1
        while step < size:
            yield axis, [(i, i ^ step) for i in range(size)], step
            step *= 2


def on_device(
    layer_input, frame_mask, gain_attn, w_query, w_key, w_value, w_out, gain_ffn, w_gate, w_up,
    w_down, cotangent,
):
    sets, width = gain_attn.shape[0], layer_input.shape[2]
    shape = layer_input.shape
    each = shape[1] // sets
    ring = Ring(lax.axis_size("dp"))
    rings, n = ring.rings, ring.size
    own = width // n
    places = jnp.concatenate([ring.order, (lax.axis_index("mp") % 2).astype(jnp.int32)[None]])
    gather = lambda value: lax.all_gather(value, "dp", tiled=True)
    scatter = lambda value: [[lax.psum_scatter(value, "dp", scatter_dimension=0, tiled=True)]]
    rounds = Rounds()
    now, close = rounds.now, rounds.close

    first, second = pack_attn(w_query, w_key, w_value, w_out)
    small = jnp.concatenate([gain_attn, gain_ffn], 0).astype(F32)[None]
    steps = list(exchange_steps(("dp",)))
    pack, x, g = [], [], []

    def gain_step(value):
        axis, moves, step = steps.pop(0)
        other = lax.ppermute(now(value), axis, moves)
        bit = (ring.me // step) % 2
        both = [jnp.concatenate(pair, 0) for pair in ((value, other), (other, value))]
        return jnp.where(bit == 0, *both)

    masks = frame_mask.astype(BF)[:, None, None]
    chores = [
        lambda: pack.append(pack_ffn(now(w_gate), w_up, w_down, 0)),
        lambda: pack.append(pack_ffn(now(w_gate), w_up, w_down, 1)),
        lambda: x.append(split_sets(now(layer_input), sets)[0]),
        lambda: x.append(split_sets(now(layer_input), sets)[1]),
        lambda: g.append(split_sets(now(cotangent) * masks, sets)[0]),
        lambda: g.append(split_sets(now(cotangent) * masks, sets)[1]),
        lambda: None,
    ]
    chores.pop(0)()
    attn = Gather(rounds, ring, first, second)
    rows = [Gather(rounds, ring, *pack[0])]
    for chore in chores:
        moved = (*attn.step(), *rows[0].step()) if rings else ()
        chore()
        if steps:
            small = gain_step(small)
        held = [v[-1] if not isinstance(v[-1], (list, tuple)) else v[-1][0] for v in (pack, x, g) if v]
        close(small, *held, *moved)
    while steps:
        small = gain_step(small)
    if rings:
        close(*attn.step(), *rows[0].step())
        rows.append(Gather(rounds, ring, *pack[1]))
        move = rows[1].step
    else:
        move = lambda: ()
    gains = small.transpose(1, 0, 2).reshape(2 * sets, width)
    g_attn, g_ffn = [[gains[k * sets + c][None] for c in range(sets)] for k in range(2)]
    w_attn = list(attn.slots()) if rings else [[gather(first)], [gather(second)]]
    w_ffn = [None if rings else [gather(jnp.concatenate(p, 0))] for p in pack]

    def take(c):
        if rings:
            a, b = rows[c].slots()
            w_ffn[c] = [piece for pair in zip(a, b) for piece in pair]

    take(0)
    h1, qkv, mixed, heads = [None] * 2, [None] * 2, [None] * 2, [None] * 2
    moved = move()
    h1[0], qkv[0], mixed[0], part = attend(now(places), x[0], g_attn[0], None, w_attn[0], each)
    heads[0] = HeadSum(rounds, part)
    close(*moved, part[0])
    close(heads[0].near())
    moved = move()
    heads[0].far()
    h1[1], qkv[1], mixed[1], part = attend(now(places), x[1], g_attn[1], qkv[0], w_attn[1], each)
    heads[1] = HeadSum(rounds, part)
    close(*moved, part[0])
    moved = move()
    close(*moved, heads[1].near())
    moved = move()
    heads[1].far()
    close(*moved, heads[0].got)
    close(heads[0].last())

    def grads_of(c, out):
        columns = [(out[0], out[2]), (out[0], out[3]), (g[c], out[1])]
        return weight_grads(now(places), columns, 2 if rings else 0)

    dh, mlp, grads, dm, d_gain_ffn = ([None] * 2 for _ in range(5))
    moved = move()
    out = hidden_units(now(places), x[0], heads[0].sum, g[0], g_ffn[0], w_ffn[0])
    dh[0], mlp[0] = HeadSum(rounds, out[4]), HeadSum(rounds, out[5])
    close(*moved, out[0], heads[1].got)
    moved = move()
    close(dh[0].near(), heads[1].last())
    att = [head.sum for head in heads]
    dh[0].far()
    grads[0] = grads_of(0, out)
    close(*moved, grads[0][0])
    close(*move(), mlp[0].near())
    take(1)
    if rings:
        sums = [Scatter(rounds, ring, grads[0][0::2], grads[0][1::2])]
        move = lambda: sum((s.step() for s in sums if s.k < n), ())
    moved = move()
    out = hidden_units(now(places), x[1], att[1], g[1], g_ffn[1], w_ffn[1])
    dh[1], mlp[1] = HeadSum(rounds, out[4]), HeadSum(rounds, out[5])
    close(*moved, out[0], dh[0].got)
    moved = move()
    close(dh[1].near(), dh[0].last())
    dh[1].far()
    grads[1] = grads_of(1, out)
    close(*moved, grads[1][0], mlp[1].near())
    if rings:
        sums.append(Scatter(rounds, ring, grads[1][0::2], grads[1][1::2]))
    moved = move()
    dm[0], d_gain_ffn[0] = middle_back(now(places), x[0], att[0], g[0], dh[0].sum, g_ffn[0])
    close(*moved, dm[0], dh[1].got)
    mlp[0].far()
    moved = move()
    close(dh[1].last())
    dm[1], d_gain_ffn[1] = middle_back(now(places), x[1], att[1], g[1], dh[1].sum, g_ffn[1])
    close(*moved, dm[1])

    moved = move()
    d_qkv, part, d_gain0 = attend_back(now(places), x, dm, qkv, w_attn, 0, None, each)
    back = [HeadSum(rounds, part)]
    close(*moved, part[0], mlp[0].got)
    close(back[0].near(), mlp[0].last())
    moved = move()
    back[0].far()
    d_qkv, part, d_gain1 = attend_back(now(places), x, dm, qkv, w_attn, 1, d_qkv, each)
    back.append(HeadSum(rounds, part))
    close(*moved, part[0], back[0].got)
    close(back[1].near())
    moved = move()
    back[1].far()
    sides = [
        weight_grads(now(places), [(h1[c], d_qkv[c]), (dm[c], mixed[c])], 1 if rings else 0)
        for c in range(sets)
    ]
    close(*moved, *[side[0] for side in sides], back[0].last())
    if rings:
        sums.append(Scatter(rounds, ring, *sides))
    shared = lax.axis_size("mp")
    d_gains = jnp.concatenate([d_gain0 + d_gain1, *[d / shared for d in d_gain_ffn]], 0)
    steps = list(exchange_steps(("dp", "mp")))

    def sum_step(value):
        axis, moves, _ = steps.pop(0)
        return value + lax.ppermute(now(value), axis, moves)

    gain = gains[:sets]
    moved = move()
    d_gains = sum_step(d_gains)
    mlp[1].far()
    grad_input = input_back(now(places), x, dm, back[0].sum, gain, 0, None, shape)
    close(*moved, grad_input, d_gains, back[1].got)
    moved = move()
    d_gains = sum_step(d_gains)
    close(*moved, back[1].last(), d_gains)
    moved = move()
    d_gains = sum_step(d_gains)
    grad_input = input_back(now(places), x, dm, back[1].sum, gain, 1, grad_input, shape)
    close(*moved, grad_input, d_gains, mlp[1].got)
    moved = move()
    d_gains = sum_step(d_gains)
    close(*moved, mlp[1].last(), d_gains)
    moved = move()
    output = output_of(now(places), x, att, [m.sum for m in mlp], shape)
    d_gains = sum_step(d_gains)
    close(*moved, output, d_gains)
    moved = move()
    if rings:
        ffn_sums = [list(s.sums()) for s in sums[:2]]
    else:
        ffn_sums = [scatter(g_[0]) for g_ in grads]
    d_gate_w, d_up_w, d_down_w = finish([[[now(t) for t in run] for run in side] for side in ffn_sums], 3)
    close(*moved, d_gate_w)
    moved = move()
    while steps:
        d_gains = sum_step(d_gains)
    attn_sums = [[run] for run in sums[2].sums()] if rings else [scatter(side[0]) for side in sides]
    d_query, d_key, d_value, d_out = finish(attn_sums, 4)
    d_gains = lax.dynamic_slice_in_dim(d_gains, ring.me * own, own, 1)
    return (
        output, grad_input, d_gains[:sets], d_query, d_key, d_value, d_out,
        d_gains[sets:], d_gate_w, d_up_w, d_down_w,
    )


def solution(mesh):
    rows = P("dp", None, None)
    gain = P(None, "dp")
    into = P(None, "dp", "mp")
    back = P(None, "mp", "dp")
    weights = (gain, into, into, into, back, gain, into, into, back)
    return jax.shard_map(
        on_device,
        mesh=mesh,
        in_specs=(rows, P("dp"), *weights, rows),
        out_specs=(rows, rows, *weights),
        check_vma=False,
    )
```

```python
import functools

import jax
import jax.numpy as jnp
from jax import lax
from jax.experimental import pallas as pl
from jax.experimental.pallas import tpu as pltpu
from jax.sharding import PartitionSpec as P

HDIM = 64
EPS = 1e-05
NEG = -1e30
BF = jnp.bfloat16
F32 = jnp.float32
NN = (((1,), (0,)), ((), ()))
NT = (((1,), (1,)), ((), ()))
TN = (((0,), (0,)), ((), ()))
MIB = 1024 * 1024
SUB = 128
PAIR = 2 * HDIM
ROWS = 256
HBM = pl.BlockSpec(memory_space=pl.ANY)


def mm(left, right, dims=NN):
    return lax.dot_general(left, right, dims, preferred_element_type=F32)


def kernel_call(body, grid, ins, in_specs, outs, out_specs, flops, scratch=(), scalars=None, alias=None):
    moved = sum(a.size * a.dtype.itemsize for a in ins) + sum(
        o.size * jnp.dtype(o.dtype).itemsize for o in outs
    )
    spec = pltpu.PrefetchScalarGridSpec(
        num_scalar_prefetch=0 if scalars is None else 1,
        grid=grid,
        in_specs=in_specs,
        out_specs=out_specs,
        scratch_shapes=scratch,
    )
    args = ins if scalars is None else (scalars, *ins)
    return pl.pallas_call(
        body,
        grid_spec=spec,
        out_shape=outs,
        input_output_aliases=alias or {},
        compiler_params=pltpu.CompilerParams(vmem_limit_bytes=56 * MIB),
        cost_estimate=pl.CostEstimate(flops=1, bytes_accessed=1, transcendentals=0),
    )(*args)


def whole(shape):
    return pl.BlockSpec(shape, lambda *i: (0,) * len(shape))


def rows_of(rows, width, start=0):
    return pl.BlockSpec((rows, width), lambda i, *_: (i + start, 0))


def out_of(shape, kind=BF):
    return jax.ShapeDtypeStruct(shape, kind)


class Halves:
    def __init__(self, tokens):
        self.count = tokens // 2 // ROWS
        self.grid = (2 * self.count,)

    def block(self, i, places):
        half = (1 - i // self.count + places[places.shape[0] - 1]) % 2
        return half * self.count + i % self.count

    def both(self, width):
        return pl.BlockSpec((ROWS, width), lambda i, p: (self.block(i, p), 0))

    def pair(self, width):
        return [
            pl.BlockSpec((ROWS, width), lambda i, p: (jnp.maximum(i - self.count, 0), 0)),
            pl.BlockSpec((ROWS, width), lambda i, p: (jnp.minimum(i, self.count - 1), 0)),
        ]

    def pick(self, pair):
        return jnp.where(pl.program_id(0) < self.count, pair[1][...], pair[0][...])

    def put(self, pair, value):
        pair[0][...] = value

        @pl.when(pl.program_id(0) < self.count)
        def _():
            pair[1][...] = pair[0][...]


def split_sets(value, sets):
    frames, steps, width = value.shape
    parts = value.reshape(frames, sets, steps // sets, width)
    return [parts[:, c].reshape(-1, width) for c in range(sets)]


def pack_attn_body(wq, wk, wv, wo, out):
    own, hw = wq.shape[1:]
    for c in range(2):
        rows = slice(c * own, (c + 1) * own)
        for t, w in enumerate((wq, wk, wv)):
            out[rows, t * hw : (t + 1) * hw] = w[c]
        out[rows, 3 * hw :] = wo[c].T


def pack_attn(wq, wk, wv, wo):
    sets, own, hw = wq.shape
    piece = (sets * own, 4 * hw)
    return kernel_call(
        pack_attn_body,
        (1,),
        (wq, wk, wv, wo),
        [whole(w.shape) for w in (wq, wk, wv, wo)],
        [out_of(piece)],
        [whole(piece)],
        0,
    )[0]


def pack_ffn_body(wg, wu, wd, out):
    units = wg.shape[2]
    out[:, :units] = wg[0]
    out[:, units : 2 * units] = wu[0]
    out[:, 2 * units :] = wd[0].T


def pack_ffn(wg, wu, wd, c):
    own, units = wg.shape[1:]
    piece = (own, 3 * units)
    into = pl.BlockSpec((1, own, units), lambda i: (c, 0, 0))
    back = pl.BlockSpec((1, units, own), lambda i: (c, 0, 0))
    return kernel_call(
        pack_ffn_body,
        (1,),
        (wg, wu, wd),
        [into, into, back],
        [out_of(piece)],
        [whole(piece)],
        0,
    )[0]


def norm(value):
    scale = lax.rsqrt(jnp.mean(value * value, axis=-1, keepdims=True) + EPS)
    return value * scale, scale


def lanes_low(shape):
    return lax.broadcasted_iota(jnp.int32, shape, 1) < HDIM


def stack_heads(pair):
    low = lanes_low(pair.shape)
    zero = jnp.zeros_like(pair)
    return jnp.concatenate([jnp.where(low, pair, zero), jnp.where(low, zero, pair)], axis=0)


def pick_heads(stacked):
    half = stacked.shape[0] // 2
    low = lanes_low((half, stacked.shape[1]))
    return jnp.where(low, stacked[:half], stacked[half:])


def visible(rows, keys, steps):
    row = lax.broadcasted_iota(jnp.int32, (rows, keys), 0) % SUB
    key = lax.broadcasted_iota(jnp.int32, (rows, keys), 1)
    same = row // steps == (key % SUB) // steps
    if keys == SUB:
        return same & (row >= key)
    return same & ((key < SUB) | (row >= key - SUB))


def softmax(query, keys, steps):
    raw = mm(query, keys, NT) * HDIM ** (-0.5)
    masked = jnp.where(visible(raw.shape[0], raw.shape[1], steps), raw, NEG)
    top = jnp.max(masked, axis=-1, keepdims=True)
    power = jnp.exp(masked - top)
    return power / jnp.sum(power, axis=-1, keepdims=True)


class Pieces:
    def __init__(self, entries, own, groups):
        self.entries = entries
        self.own = own
        self.groups = groups
        self.arrays = []
        for array, *_ in entries:
            if not any(array is a for a in self.arrays):
                self.arrays.append(array)
        self.count = len(self.arrays)
        self.shape = (sum(e[4] for e in entries), entries[0][0].shape[1])
        self.scratch = [pltpu.VMEM(self.shape, BF), pltpu.SemaphoreType.DMA((groups, len(entries)))]

    def copies(self, refs, places, memory, sems, group):
        wide = self.shape[1] // self.groups
        cols = pl.ds(group * wide, wide)
        for k, (array, slot, row, first, rows) in enumerate(self.entries):
            ref = [r for r, a in zip(refs, self.arrays) if a is array][0]
            start = row if slot is None else pl.multiple_of(places[slot] * self.own + row, rows)
            source = ref.at[pl.ds(first, rows), cols]
            yield pltpu.make_async_copy(source, memory.at[pl.ds(start, rows), cols], sems.at[group, k])

    def start(self, refs, places, memory, sems, order):
        @pl.when(pl.program_id(0) == 0)
        def _():
            for group in order:
                for copy in self.copies(refs, places, memory, sems, group):
                    copy.start()

    def wait(self, refs, places, memory, sems, group):
        @pl.when(pl.program_id(0) == 0)
        def _():
            for copy in self.copies(refs, places, memory, sems, group):
                copy.wait()


def attend_body(pieces, halves, steps, hw, later, places, *refs):
    x_ref, gain_ref, *refs = refs
    if later:
        before_ref, *refs = refs
    w_refs, refs = refs[: pieces.count], refs[pieces.count :]
    h_ref, qkv_ref, mixed_ref, mine_ref, other_ref, w_ref, sems = refs
    pieces.start(w_refs, places, w_ref, sems, range(1))
    normed, _ = norm(x_ref[...].astype(F32))
    hidden = (normed * gain_ref[...]).astype(BF)
    h_ref[...] = hidden
    pieces.wait(w_refs, places, w_ref, sems, 0)
    qkv = mm(hidden, w_ref[:, : 3 * hw]).astype(BF)
    qkv_ref[...] = qkv
    for s in range(x_ref.shape[0] // SUB):
        rows = slice(s * SUB, (s + 1) * SUB)
        for j in range(hw // PAIR):
            q, k, v = (qkv[rows, t * hw + j * PAIR : t * hw + (j + 1) * PAIR] for t in range(3))
            if later:
                k_old, v_old = (
                    before_ref[rows, t * hw + j * PAIR : t * hw + (j + 1) * PAIR] for t in (1, 2)
                )
                k = jnp.concatenate([k_old, k], axis=0)
                v = jnp.concatenate([v_old, v], axis=0)
            probs = softmax(stack_heads(q), k, steps).astype(BF)
            mixed_ref[rows, j * PAIR : (j + 1) * PAIR] = pick_heads(mm(probs, v)).astype(BF)
    halves.put((mine_ref, other_ref), mm(mixed_ref[...], w_ref[:, 3 * hw :], NT).astype(BF))


def attend(places, x, gain, before, w, steps):
    tokens, width = x.shape
    pieces, halves = Pieces(*w, 1), Halves(tokens)
    hw = pieces.shape[1] // 4
    ins = [x, gain]
    specs = [halves.both(width), whole(gain.shape)]
    if before is not None:
        ins.append(before)
        specs.append(halves.both(3 * hw))
    widths = (width, 3 * hw, hw)
    *out, mine, other = kernel_call(
        functools.partial(attend_body, pieces, halves, steps, hw, before is not None),
        halves.grid,
        [*ins, *pieces.arrays],
        [*specs, *[HBM] * pieces.count],
        [out_of((tokens, n)) for n in widths] + [out_of((tokens // 2, width))] * 2,
        [halves.both(n) for n in widths] + halves.pair(width),
        2 * tokens * width * 4 * hw,
        pieces.scratch,
        places,
    )
    return *out, (mine, other)


def units_body(pieces, halves, units, places, *refs):
    x_ref, att0, att1, g_ref, gain_ref, *refs = refs
    w_refs, refs = refs[: pieces.count], refs[pieces.count :]
    h_ref, inner_ref, dgate_ref, dup_ref, dh0, dh1, mlp0, mlp1, w_ref, sems = refs
    pieces.start(w_refs, places, w_ref, sems, (2, 0, 1))
    normed, _ = norm(x_ref[...].astype(F32) + halves.pick((att0, att1)).astype(F32))
    hidden = (normed * gain_ref[...]).astype(BF)
    h_ref[...] = hidden
    cut = 256
    cols = [
        [slice(t * units + u * cut, t * units + (u + 1) * cut) for t in range(3)] for u in range(units // cut)
    ]
    pieces.wait(w_refs, places, w_ref, sems, 2)
    d_inners = [mm(g_ref[...], w_ref[:, c[2]]) for c in cols]
    pieces.wait(w_refs, places, w_ref, sems, 0)
    pieces.wait(w_refs, places, w_ref, sems, 1)
    for c, d_inner in zip(cols, d_inners):
        gate = mm(hidden, w_ref[:, c[0]])
        up = mm(hidden, w_ref[:, c[1]])
        sigma = 1.0 / (1.0 + jnp.exp(-gate))
        active = gate * sigma
        inner_ref[:, c[0]] = (active * up).astype(BF)
        dup_ref[:, c[0]] = (d_inner * active).astype(BF)
        dgate_ref[:, c[0]] = (d_inner * up * sigma * (1.0 + gate * (1.0 - sigma))).astype(BF)
    grad = mm(dgate_ref[...], w_ref[:, :units], NT) + mm(dup_ref[...], w_ref[:, units : 2 * units], NT)
    halves.put((dh0, dh1), grad.astype(BF))
    halves.put((mlp0, mlp1), mm(inner_ref[...], w_ref[:, 2 * units :], NT).astype(BF))


def hidden_units(places, x, att, g, gain, w):
    tokens, width = x.shape
    pieces, halves = Pieces(*w, 3), Halves(tokens)
    units = pieces.shape[1] // 3
    part = halves.both(width)
    widths = (width, units, units, units)
    *out, dh0, dh1, mlp0, mlp1 = kernel_call(
        functools.partial(units_body, pieces, halves, units),
        halves.grid,
        (x, *att, g, gain, *pieces.arrays),
        [part, *halves.pair(width), part, whole(gain.shape), *[HBM] * pieces.count],
        [out_of((tokens, n)) for n in widths] + [out_of((tokens // 2, width))] * 4,
        [halves.both(n) for n in widths] + halves.pair(width) * 2,
        12 * tokens * width * units,
        pieces.scratch,
        places,
    )
    return *out, (dh0, dh1), (mlp0, mlp1)


def grads_body(runs, cut, steps, places, *refs):
    inputs = max(right for columns in runs for _, right in columns) + 1
    ins, outs = refs[:inputs], refs[inputs:]
    values = []
    for columns in runs:
        values.append([])
        for slots, k in columns:
            rows = [ins[s][...] for s in slots]
            rows = jnp.concatenate(rows, axis=1) if len(rows) > 1 else rows[0]
            values[-1].append(mm(rows, ins[k][...], TN).astype(BF))
    if not cut:
        at = 0
        for value in values[0]:
            outs[0][:, at : at + value.shape[1]] = value
            at += value.shape[1]
        return
    *outs, buffer, sems = outs
    height = outs[0].shape[0]
    own = height // len(runs)
    slots = ROWS // own

    def copies(block):
        at = 0
        for k in range(slots):
            t = block * slots + k
            for ref in outs[t : t + 1] if t < cut else outs[t : t + 2] if t == cut else outs[t + 1 : t + 2]:
                rows = buffer.at[block % 2, pl.ds(at, ref.shape[0])]
                yield pltpu.make_async_copy(rows, ref, sems.at[block % 2, at // (height // 2)])
                at += ref.shape[0]

    for block in range(steps):

        @pl.when(pl.program_id(0) == block)
        def _():
            if block >= 2:
                for copy in copies(block - 2):
                    copy.wait()
            for k in range(slots):
                for r, columns in enumerate(values):
                    at = 0
                    first = (k * len(runs) + r) * own
                    for value in columns:
                        cols = slice(at, at + value.shape[1])
                        buffer[block % 2, first : first + own, cols] = value[k * own : (k + 1) * own]
                        at += value.shape[1]
            for copy in copies(block):
                copy.start()
            if block == steps - 1:
                for last in range(max(0, steps - 2), steps):
                    for copy in copies(last):
                        copy.wait()


def weight_grads(places, runs, cut):
    count = places.shape[0] - 1
    tokens, width = runs[0][0][0].shape
    own = width // count
    steps = width // ROWS
    slots = ROWS // own if cut else 1
    ins, specs, marks = [], [], []
    for columns in runs:
        for left, _ in columns:
            mark = []
            for k in range(slots):
                place = (lambda i, p, k=k: (0, p[i * slots + k])) if cut else (lambda i, p: (0, i))
                ins.append(left)
                specs.append(pl.BlockSpec((tokens, ROWS // slots), place))
                mark.append(len(ins) - 1)
            marks.append(tuple(mark))
    pairs = []
    for columns in runs:
        pairs.append([])
        for _, right in columns:
            ins.append(right)
            specs.append(whole(right.shape))
            pairs[-1].append((marks.pop(0), len(ins) - 1))
    total = sum(right.shape[1] for _, right in runs[0])
    if cut:
        height = own * len(runs)
        heights = [height] * cut + [height // 2] * 2 + [height] * (count - cut - 1)
        outs = [out_of((h, total)) for h in heights]
        out_specs = [HBM] * len(outs)
        scratch = [
            pltpu.VMEM((2, slots * height, total), BF),
            pltpu.SemaphoreType.DMA((2, 2 * slots)),
        ]
    else:
        outs, out_specs, scratch = [out_of((width, total))], [rows_of(ROWS, total)], []
    return kernel_call(
        functools.partial(grads_body, pairs, cut, steps),
        (steps,),
        ins,
        specs,
        outs,
        out_specs,
        2 * tokens * width * total,
        scratch,
        places,
    )


def norm_back(grad_hidden, value, gain):
    normed, scale = norm(value)
    scaled = grad_hidden * gain
    back = scale * (scaled - normed * jnp.mean(scaled * normed, axis=-1, keepdims=True))
    return back, jnp.sum(grad_hidden * normed, axis=0, keepdims=True)


def add_up(ref, value):
    @pl.when(pl.program_id(0) == 0)
    def _():
        ref[...] = jnp.zeros_like(ref)

    ref[...] += value


def middle_body(halves, _, x_ref, att0, att1, g_ref, dh0, dh1, gain_ref, dm_ref, dgain_ref):
    value = x_ref[...].astype(F32) + halves.pick((att0, att1)).astype(F32)
    back, d_gain = norm_back(halves.pick((dh0, dh1)).astype(F32), value, gain_ref[...])
    dm_ref[...] = (g_ref[...].astype(F32) + back).astype(BF)
    add_up(dgain_ref, d_gain)


def middle_back(places, x, att, g, dh, gain):
    tokens, width = x.shape
    halves = Halves(tokens)
    part, pair = halves.both(width), halves.pair(width)
    return kernel_call(
        functools.partial(middle_body, halves),
        halves.grid,
        (x, *att, g, *dh, gain),
        [part, *pair, part, *pair, whole(gain.shape)],
        [out_of((tokens, width)), out_of((1, width), F32)],
        [part, whole((1, width))],
        0,
        (),
        places,
    )


def attend_back_body(pieces, shared, steps, hw, places, x0, x1, dm0, dm1, qkv0, qkv1, *refs):
    sides = [
        [r for a in p.arrays for r, b in zip(refs, shared.arrays) if a is b] for p in pieces
    ]
    dqkv0, dqkv1, mine, other, dgain, w0, sems0, w1, sems1 = refs[-9:]
    for p, s, w, sems in zip(pieces, sides, (w0, w1), (sems0, sems1)):
        p.start(s, places, w, sems, range(1))
    normed = [norm(x[...].astype(F32))[0] for x in (x0, x1)]
    for p, s, w, sems in zip(pieces, sides, (w0, w1), (sems0, sems1)):
        p.wait(s, places, w, sems, 0)
    scale = HDIM ** (-0.5)
    d_mixed = [mm(d[...], w[:, 3 * hw :]).astype(BF) for d, w in ((dm0, w0), (dm1, w1))]
    for s in range(dm0.shape[0] // SUB):
        rows = slice(s * SUB, (s + 1) * SUB)
        for j in range(hw // PAIR):
            cols = [slice(t * hw + j * PAIR, t * hw + (j + 1) * PAIR) for t in range(3)]
            q0, k0, v0 = (qkv0[rows, c] for c in cols)
            q1, k1, v1 = (qkv1[rows, c] for c in cols)
            keys = (k0, jnp.concatenate([k0, k1], axis=0))
            values = (v0, jnp.concatenate([v0, v1], axis=0))
            d_k, d_v = [], []
            for c, (q, out_ref) in enumerate(((q0, dqkv0), (q1, dqkv1))):
                q_two = stack_heads(q)
                d_two = stack_heads(d_mixed[c][rows, cols[0]])
                soft = softmax(q_two, keys[c], steps)
                d_probs = mm(d_two, values[c], NT)
                inside = jnp.sum(soft * d_probs, axis=-1, keepdims=True)
                d_scores = (soft * (d_probs - inside)).astype(BF)
                d_q = pick_heads(mm(d_scores, keys[c])) * scale
                out_ref[rows, cols[0]] = d_q.astype(BF)
                d_k.append(mm(d_scores, q_two, TN) * scale)
                d_v.append(mm(soft.astype(BF), d_two, TN))
            dqkv0[rows, cols[1]] = (d_k[0] + d_k[1][:SUB]).astype(BF)
            dqkv1[rows, cols[1]] = d_k[1][SUB:].astype(BF)
            dqkv0[rows, cols[2]] = (d_v[0] + d_v[1][:SUB]).astype(BF)
            dqkv1[rows, cols[2]] = d_v[1][SUB:].astype(BF)
    gains = []
    for c, (d, w) in enumerate(((dqkv0, w0), (dqkv1, w1))):
        grad = mm(d[...], w[:, : 3 * hw], NT)
        gains.append(jnp.sum(grad * normed[c], axis=0, keepdims=True))
        mine[c * ROWS : (c + 1) * ROWS] = grad.astype(BF)

    @pl.when(pl.program_id(0) == 0)
    def _():
        other[...] = mine[...]

    add_up(dgain, jnp.concatenate(gains, axis=0))


def attend_back(places, x, dm, qkv, w, part, before, steps):
    tokens, width = dm[0].shape
    halves = Halves(tokens)
    pieces = [Pieces(*side, 1) for side in w]
    shared = Pieces(w[0][0] + w[1][0], w[0][1], 1)
    hw = pieces[0].shape[1] // 4
    spot = lambda i, p: (halves.block(i * halves.count, p) + part, 0)
    flat, thin = pl.BlockSpec((ROWS, width), spot), pl.BlockSpec((ROWS, 3 * hw), spot)
    ins = [*x, *dm, *qkv, *shared.arrays, *(before or ())]
    specs = [flat] * 4 + [thin] * 2 + [HBM] * (len(ins) - 6)
    alias = {len(ins) - 1: 0, len(ins): 1} if before else {}
    d0, d1, mine, other, d_gain = kernel_call(
        functools.partial(attend_back_body, pieces, shared, steps, hw),
        (2,),
        ins,
        specs,
        [out_of((tokens, 3 * hw))] * 2 + [out_of((2 * ROWS, width))] * 2 + [out_of((2, width), F32)],
        [thin] * 2 + [whole((2 * ROWS, width))] * 2 + [whole((2, width))],
        8 * ROWS * width * 4 * hw,
        pieces[0].scratch + pieces[1].scratch,
        places,
        alias,
    )
    return (d0, d1), (mine, other), d_gain


def store_frames(out_ref, sums):
    frames, _, width = out_ref.shape
    both = [p.reshape(frames, 1, p.shape[0] // frames, width) for p in sums]
    out_ref[...] = jnp.concatenate(both, axis=1).reshape(frames, -1, width).astype(BF)


def output_body(halves, _, x0, x1, *refs):
    *refs, out_ref = refs
    pairs = [halves.pick(refs[k : k + 2]).astype(F32) for k in range(0, 8, 2)]
    sums = [x[...].astype(F32) + pairs[2 * c] + pairs[2 * c + 1] for c, x in enumerate((x0, x1))]
    store_frames(out_ref, sums)


def output_of(places, x, att, mlp, shape):
    frames, steps, width = shape
    halves = Halves(x[0].shape[0])
    sides = [a for c in range(2) for pair in (att[c], mlp[c]) for a in pair]
    cube = pl.BlockSpec((2 * ROWS // steps, steps, width), lambda i, p: (halves.block(i, p), 0, 0))
    return kernel_call(
        functools.partial(output_body, halves),
        halves.grid,
        [*x, *sides],
        [halves.both(width)] * 2 + halves.pair(width) * 4,
        [out_of(shape)],
        [cube],
        0,
        (),
        places,
    )[0]


def input_body(_, x0, x1, dm0, dm1, mine, other, gain_ref, *refs):
    first = pl.program_id(0) == 0
    sums = []
    for c, (x, dm) in enumerate(((x0, dm0), (x1, dm1))):
        rows = slice(c * ROWS, (c + 1) * ROWS)
        dh = jnp.where(first, other[rows], mine[rows]).astype(F32)
        back, _ = norm_back(dh, x[...].astype(F32), gain_ref[c : c + 1])
        sums.append(dm[...].astype(F32) + back)
    store_frames(refs[-1], sums)


def input_back(places, x, dm, dh, gain, part, before, shape):
    frames, steps, width = shape
    halves = Halves(x[0].shape[0])
    block = lambda i, p: halves.block(i * halves.count, p) + part
    flat = pl.BlockSpec((ROWS, width), lambda i, p: (block(i, p), 0))
    cube = pl.BlockSpec((2 * ROWS // steps, steps, width), lambda i, p: (block(i, p), 0, 0))
    ins = [*x, *dm, *dh, gain]
    specs = [flat] * 4 + [whole(d.shape) for d in dh] + [whole(gain.shape)]
    alias = {}
    if before is not None:
        ins.append(before)
        specs.append(HBM)
        alias = {len(ins): 0}
    return kernel_call(input_body, (2,), ins, specs, [out_of(shape)], [cube], 0, (), places, alias)[0]


def finish_body(layout, turned, *refs):
    count = 1 + max(k for terms, _ in layout for k in terms)
    ins, outs = refs[:count], refs[count:]
    own, wide = outs[0].shape[1:]
    for c, (terms, first) in enumerate(layout):
        rows = slice(first, first + own)
        for t, ref in enumerate(outs):
            cols = slice(t * wide, (t + 1) * wide)
            total = ins[terms[0]][rows, cols].astype(F32)
            for k in terms[1:]:
                total = total + ins[k][rows, cols].astype(F32)
            ref[c] = total.T if t == turned else total


def finish(sides, kinds, own):
    arrays, layout = [], []
    for terms, first in sides:
        spots = []
        for term in terms:
            found = [k for k, a in enumerate(arrays) if a is term]
            if not found:
                arrays.append(term)
            spots.append(found[0] if found else len(arrays) - 1)
        layout.append((spots, first))
    wide = arrays[0].shape[1] // kinds
    shapes = [(len(sides), own, wide)] * (kinds - 1) + [(len(sides), wide, own)]
    return kernel_call(
        functools.partial(finish_body, layout, kinds - 1),
        (1,),
        arrays,
        [whole(a.shape) for a in arrays],
        [out_of(s, F32) for s in shapes],
        [whole(s) for s in shapes],
        0,
    )


class Ring:
    def __init__(self, size):
        self.size = size
        self.rings = size <= 16
        half = size // 2
        order = [2 * q for q in range(half)] + [2 * (size - 1 - q) + 1 for q in range(half, size)]
        self.ahead = [(order[q], order[(q + 1) % size]) for q in range(size)]
        self.behind = [(b, a) for a, b in self.ahead]
        self.me = lax.axis_index("dp")
        place = jnp.where(self.me % 2 == 0, self.me // 2, size - 1 - self.me // 2)
        q = lax.rem(place + jnp.arange(size, dtype=jnp.int32), size)
        self.order = jnp.where(q < half, 2 * q, 2 * (size - 1 - q) + 1).astype(jnp.int32)


class Rounds:
    def __init__(self):
        self.done = ()

    def now(self, value):
        return lax.optimization_barrier((value, *self.done))[0] if self.done else value

    def close(self, *arrays):
        self.done = arrays


class Gather:
    def __init__(self, rounds, ring, shard):
        self.rounds, self.ring = rounds, ring
        self.a, self.b = [shard], [shard]

    def step(self):
        a, b = self.a[-1], self.b[-1]
        if len(self.a) == self.ring.size // 2:
            half = a.shape[0] // 2
            a, b = a[:half], b[half:]
        self.a.append(lax.ppermute(self.rounds.now(a), "dp", self.ring.ahead))
        self.b.append(lax.ppermute(self.rounds.now(b), "dp", self.ring.behind))
        return self.a[-1], self.b[-1]

    def entries(self, part=0, parts=1):
        n = self.ring.size
        own = self.a[0].shape[0] // parts
        found = []
        for t in range(n):
            if t != n // 2:
                found.append((self.b[t] if t < n // 2 else self.a[n - t], t, 0, part * own, own))
            elif parts == 1:
                found.append((self.a[t], t, 0, 0, own // 2))
                found.append((self.b[t], t, own // 2, 0, own // 2))
            else:
                found.append(((self.a[t], self.b[t])[part], t, 0, 0, own))
        return found, own


class Scatter:
    def __init__(self, rounds, ring, blocks):
        self.rounds, self.ring = rounds, ring
        far = ring.size // 2
        self.a, self.b = blocks[far], blocks[far + 1]
        self.blocks = [*blocks[:far], None, *blocks[far + 2 :]]
        self.k = far

    def step(self):
        n = self.ring.size
        if self.k < n // 2:
            one, two = self.blocks[self.k].astype(F32), self.blocks[n - self.k].astype(F32)
            a, b = self.a.astype(F32), self.b.astype(F32)
            if self.k == n // 2 - 1:
                half = a.shape[0]
                a = jnp.pad(a, ((0, half), (0, 0)))
                b = jnp.pad(b, ((half, 0), (0, 0)))
            self.a, self.b = (one + a).astype(BF), (two + b).astype(BF)
        self.k -= 1
        self.a = lax.ppermute(self.rounds.now(self.a), "dp", self.ring.ahead)
        self.b = lax.ppermute(self.rounds.now(self.b), "dp", self.ring.behind)
        return self.a, self.b

    def terms(self):
        return [self.blocks[0], self.a, self.b]


class HeadSum:
    def __init__(self, rounds, pair):
        size = lax.axis_size("mp")
        self.rounds, self.pair = rounds, pair
        self.near_moves = [(i, i ^ 1) for i in range(size)]
        self.far_moves = [(i, i ^ 2) for i in range(size)]

    def add(self, one, two):
        return (one.astype(F32) + two.astype(F32)).astype(BF)

    def near(self):
        got = lax.ppermute(self.rounds.now(self.pair[1]), "mp", self.near_moves)
        self.mine = self.add(self.pair[0], got)
        return self.mine

    def far(self):
        self.got = lax.ppermute(self.rounds.now(self.mine), "mp", self.far_moves)
        return self.got

    def last(self):
        self.mine = self.add(self.mine, self.rounds.now(self.got))
        self.sum = (self.mine, lax.ppermute(self.mine, "mp", self.near_moves))
        return self.sum[1]


def exchange_steps(axes):
    for axis in axes:
        size, step = lax.axis_size(axis), 1
        while step < size:
            yield axis, [(i, i ^ step) for i in range(size)], step
            step *= 2


def on_device(
    layer_input, frame_mask, gain_attn, w_query, w_key, w_value, w_out, gain_ffn, w_gate, w_up,
    w_down, cotangent,
):
    sets, width = gain_attn.shape[0], layer_input.shape[2]
    shape = layer_input.shape
    each = shape[1] // sets
    ring = Ring(lax.axis_size("dp"))
    rings, n = ring.rings, ring.size
    far = n // 2 if rings else 0
    own = width // n
    places = jnp.concatenate([ring.order, (lax.axis_index("mp") % 2).astype(jnp.int32)[None]])
    gather = lambda value: lax.all_gather(value, "dp", tiled=True)
    scatter = lambda value: lax.psum_scatter(value, "dp", scatter_dimension=0, tiled=True)
    rounds = Rounds()
    now, close = rounds.now, rounds.close

    attn_own = pack_attn(w_query, w_key, w_value, w_out)
    small = jnp.concatenate([gain_attn, gain_ffn], 0).astype(F32)[None]
    steps = list(exchange_steps(("dp",)))
    ffn_own, x, g = [], [], []

    def gain_step(value):
        axis, moves, step = steps.pop(0)
        other = lax.ppermute(now(value), axis, moves)
        bit = (ring.me // step) % 2
        both = [jnp.concatenate(pair, 0) for pair in ((value, other), (other, value))]
        return jnp.where(bit == 0, *both)

    masks = frame_mask.astype(BF)[:, None, None]
    chores = [
        lambda: ffn_own.append(pack_ffn(now(w_gate), w_up, w_down, 0)),
        lambda: x.append(split_sets(now(layer_input), sets)[0]),
        lambda: ffn_own.append(pack_ffn(now(w_gate), w_up, w_down, 1)),
        lambda: x.append(split_sets(now(layer_input), sets)[1]),
        lambda: g.append(split_sets(now(cotangent) * masks, sets)[0]),
        lambda: g.append(split_sets(now(cotangent) * masks, sets)[1]),
    ]
    attn = Gather(rounds, ring, attn_own)
    for _ in range(max(far, 3)):
        moved = attn.step() if rings else ()
        for chore in chores[:2]:
            chore()
        del chores[:2]
        if steps:
            small = gain_step(small)
        close(small, *moved, *[v[-1] for v in (ffn_own, x, g) if v])
    while steps:
        small = gain_step(small)
    gains = small.transpose(1, 0, 2).reshape(2 * sets, width)
    g_attn, g_ffn = [[gains[k * sets + c][None] for c in range(sets)] for k in range(2)]
    if rings:
        rows = [Gather(rounds, ring, shard) for shard in ffn_own]
        w_attn = [attn.entries(c, sets) for c in range(sets)]
    else:
        both = gather(attn_own).reshape(n, sets, own, -1)
        w_attn = [([(both[:, c].reshape(width, -1), None, 0, 0, width)], width) for c in range(sets)]

    def move(c):
        return rows[c].step() if rings else ()

    def weights(c):
        if rings:
            return rows[c].entries()
        return [(gather(ffn_own[c]), None, 0, 0, width)], width

    h1, qkv, mixed, heads = [None] * 2, [None] * 2, [None] * 2, [None] * 2
    moved = move(0)
    h1[0], qkv[0], mixed[0], part = attend(now(places), x[0], g_attn[0], None, w_attn[0], each)
    heads[0] = HeadSum(rounds, part)
    close(*moved, part[0])
    close(heads[0].near())
    moved = move(0)
    got = heads[0].far()
    h1[1], qkv[1], mixed[1], part = attend(now(places), x[1], g_attn[1], qkv[0], w_attn[1], each)
    heads[1] = HeadSum(rounds, part)
    close(*moved, part[0], got)
    close(*move(0), heads[1].near(), heads[0].last())
    close(*move(0), *move(1), heads[1].far())

    def grads_of(c, out):
        columns = [(out[0], out[2]), (out[0], out[3]), (g[c], out[1])]
        return weight_grads(now(places), [columns], far)

    dh, mlp, grads, dm, d_gain_ffn = ([None] * 2 for _ in range(5))
    moved = move(1)
    out = hidden_units(now(places), x[0], heads[0].sum, g[0], g_ffn[0], weights(0))
    dh[0], mlp[0] = HeadSum(rounds, out[4]), HeadSum(rounds, out[5])
    close(*moved, out[0], heads[1].last())
    att = [head.sum for head in heads]
    close(dh[0].near())
    moved = move(1)
    got = dh[0].far()
    grads[0] = grads_of(0, out)
    close(*moved, grads[0][0], got, mlp[0].near())
    close(*move(1), dh[0].last())

    sums = [Scatter(rounds, ring, grads[0])] if rings else []
    add = lambda k: sums[k].step() if rings else ()
    moved = add(0)
    got = mlp[0].far()
    out = hidden_units(now(places), x[1], att[1], g[1], g_ffn[1], weights(1))
    dh[1], mlp[1] = HeadSum(rounds, out[4]), HeadSum(rounds, out[5])
    close(*moved, out[0], got)
    close(dh[1].near(), mlp[0].last())
    moved = add(0)
    got = dh[1].far()
    grads[1] = grads_of(1, out)
    order = now(places)
    dm[0], d_gain_ffn[0] = middle_back(order, x[0], att[0], g[0], dh[0].sum, g_ffn[0])
    close(*moved, grads[1][0], dm[0], got)
    close(dh[1].last(), mlp[1].near())
    if rings:
        sums.append(Scatter(rounds, ring, grads[1]))

    moved = (*add(0), *add(1))
    got = mlp[1].far()
    dm[1], d_gain_ffn[1] = middle_back(now(places), x[1], att[1], g[1], dh[1].sum, g_ffn[1])
    d_qkv, part, d_gain0 = attend_back(now(places), x, dm, qkv, w_attn, 0, None, each)
    back = [HeadSum(rounds, part)]
    close(*moved, part[0], got)
    close(back[0].near(), mlp[1].last())
    moved = add(0)
    got = back[0].far()
    d_qkv, part, d_gain1 = attend_back(now(places), x, dm, qkv, w_attn, 1, d_qkv, each)
    back.append(HeadSum(rounds, part))
    close(*moved, part[0], got)
    close(back[1].near(), back[0].last())
    gain = gains[:sets]
    moved = add(1)
    got = back[1].far()
    runs = [[(h1[c], d_qkv[c]), (dm[c], mixed[c])] for c in range(sets)]
    if rings:
        blocks = weight_grads(now(places), runs, far)
    else:
        blocks = [weight_grads(now(places), [run], far)[0] for run in runs]
    grad_input = input_back(now(places), x, dm, back[0].sum, gain, 0, None, shape)
    close(*moved, blocks[0], grad_input, got)
    if rings:
        sums.append(Scatter(rounds, ring, blocks))

    shared = lax.axis_size("mp")
    d_gains = jnp.concatenate([d_gain0 + d_gain1, *[d / shared for d in d_gain_ffn]], 0)
    steps = list(exchange_steps(("dp", "mp")))

    def sum_step(value):
        axis, moves, _ = steps.pop(0)
        return value + lax.ppermute(now(value), axis, moves)

    moved = (*add(2), *add(1))
    d_gains = sum_step(d_gains)
    output = output_of(now(places), x, att, [m.sum for m in mlp], shape)
    close(*moved, back[1].last(), d_gains, output)
    moved = (*add(2), *add(1))
    d_gains = sum_step(d_gains)
    grad_input = input_back(now(places), x, dm, back[1].sum, gain, 1, grad_input, shape)
    close(*moved, grad_input, d_gains)
    moved = add(2)
    d_gains = sum_step(d_gains)
    if rings:
        ffn_sums = [([now(t) for t in s.terms()], 0) for s in sums[:2]]
    else:
        ffn_sums = [([scatter(b[0])], 0) for b in grads]
    d_gate_w, d_up_w, d_down_w = finish(ffn_sums, 3, own)
    close(*moved, d_gate_w, d_gains)
    moved = add(2)
    while steps:
        d_gains = sum_step(d_gains)
    if rings:
        terms = sums[2].terms()
        attn_sums = [(terms, c * own) for c in range(sets)]
    else:
        attn_sums = [([scatter(b)], 0) for b in blocks]
    d_query, d_key, d_value, d_out = finish(attn_sums, 4, own)
    d_gains = lax.dynamic_slice_in_dim(d_gains, ring.me * own, own, 1)
    return (
        output, grad_input, d_gains[:sets], d_query, d_key, d_value, d_out,
        d_gains[sets:], d_gate_w, d_up_w, d_down_w,
    )


def solution(mesh):
    rows = P("dp", None, None)
    gain = P(None, "dp")
    into = P(None, "dp", "mp")
    back = P(None, "mp", "dp")
    weights = (gain, into, into, into, back, gain, into, into, back)
    return jax.shard_map(
        on_device,
        mesh=mesh,
        in_specs=(rows, P("dp"), *weights, rows),
        out_specs=(rows, rows, *weights),
        check_vma=False,
    )
```

```python
import functools

import jax
import jax.numpy as jnp
from jax import lax
from jax.experimental import pallas as pl
from jax.experimental.pallas import tpu as pltpu
from jax.sharding import PartitionSpec as P

HDIM = 64
EPS = 1e-05
NEG = -1e30
BF = jnp.bfloat16
F32 = jnp.float32
NN = (((1,), (0,)), ((), ()))
NT = (((1,), (1,)), ((), ()))
TN = (((0,), (0,)), ((), ()))
MIB = 1024 * 1024
SUB = 128
PAIR = 2 * HDIM
ROWS = 256
HBM = pl.BlockSpec(memory_space=pl.ANY)


def mm(left, right, dims=NN):
    return lax.dot_general(left, right, dims, preferred_element_type=F32)


def kernel_call(body, grid, ins, in_specs, outs, out_specs, flops, scratch=(), scalars=None, alias=None):
    moved = sum(a.size * a.dtype.itemsize for a in ins) + sum(
        o.size * jnp.dtype(o.dtype).itemsize for o in outs
    )
    spec = pltpu.PrefetchScalarGridSpec(
        num_scalar_prefetch=0 if scalars is None else 1,
        grid=grid,
        in_specs=in_specs,
        out_specs=out_specs,
        scratch_shapes=scratch,
    )
    args = ins if scalars is None else (scalars, *ins)
    return pl.pallas_call(
        body,
        grid_spec=spec,
        out_shape=outs,
        input_output_aliases=alias or {},
        compiler_params=pltpu.CompilerParams(vmem_limit_bytes=56 * MIB),
        cost_estimate=pl.CostEstimate(flops=1, bytes_accessed=1, transcendentals=0),
    )(*args)


def whole(shape):
    return pl.BlockSpec(shape, lambda *i: (0,) * len(shape))


def rows_of(rows, width, start=0):
    return pl.BlockSpec((rows, width), lambda i, *_: (i + start, 0))


def out_of(shape, kind=BF):
    return jax.ShapeDtypeStruct(shape, kind)


class Halves:
    def __init__(self, tokens):
        self.count = tokens // 2 // ROWS
        self.grid = (2 * self.count,)

    def block(self, i, places):
        half = (1 - i // self.count + places[places.shape[0] - 1]) % 2
        return half * self.count + i % self.count

    def both(self, width):
        return pl.BlockSpec((ROWS, width), lambda i, p: (self.block(i, p), 0))

    def pair(self, width):
        return [
            pl.BlockSpec((ROWS, width), lambda i, p: (jnp.maximum(i - self.count, 0), 0)),
            pl.BlockSpec((ROWS, width), lambda i, p: (jnp.minimum(i, self.count - 1), 0)),
        ]

    def pick(self, pair):
        return jnp.where(pl.program_id(0) < self.count, pair[1][...], pair[0][...])

    def put(self, pair, value):
        pair[0][...] = value

        @pl.when(pl.program_id(0) < self.count)
        def _():
            pair[1][...] = pair[0][...]


def split_sets(value, sets):
    frames, steps, width = value.shape
    parts = value.reshape(frames, sets, steps // sets, width)
    return [parts[:, c].reshape(-1, width) for c in range(sets)]


def pack_attn_body(wq, wk, wv, wo, out):
    own, hw = wq.shape[1:]
    for c in range(2):
        rows = slice(c * own, (c + 1) * own)
        for t, w in enumerate((wq, wk, wv)):
            out[rows, t * hw : (t + 1) * hw] = w[c]
        out[rows, 3 * hw :] = wo[c].T


def pack_attn(wq, wk, wv, wo):
    sets, own, hw = wq.shape
    piece = (sets * own, 4 * hw)
    return kernel_call(
        pack_attn_body,
        (1,),
        (wq, wk, wv, wo),
        [whole(w.shape) for w in (wq, wk, wv, wo)],
        [out_of(piece)],
        [whole(piece)],
        0,
    )[0]


def pack_ffn_body(wg, wu, wd, out):
    units = wg.shape[2]
    out[:, :units] = wg[0]
    out[:, units : 2 * units] = wu[0]
    out[:, 2 * units :] = wd[0].T


def pack_ffn(wg, wu, wd, c):
    own, units = wg.shape[1:]
    piece = (own, 3 * units)
    into = pl.BlockSpec((1, own, units), lambda i: (c, 0, 0))
    back = pl.BlockSpec((1, units, own), lambda i: (c, 0, 0))
    return kernel_call(
        pack_ffn_body,
        (1,),
        (wg, wu, wd),
        [into, into, back],
        [out_of(piece)],
        [whole(piece)],
        0,
    )[0]


def norm(value):
    scale = lax.rsqrt(jnp.mean(value * value, axis=-1, keepdims=True) + EPS)
    return value * scale, scale


def lanes_low(shape):
    return lax.broadcasted_iota(jnp.int32, shape, 1) < HDIM


def stack_heads(pair):
    low = lanes_low(pair.shape)
    zero = jnp.zeros_like(pair)
    return jnp.concatenate([jnp.where(low, pair, zero), jnp.where(low, zero, pair)], axis=0)


def pick_heads(stacked):
    half = stacked.shape[0] // 2
    low = lanes_low((half, stacked.shape[1]))
    return jnp.where(low, stacked[:half], stacked[half:])


def visible(rows, keys, steps):
    row = lax.broadcasted_iota(jnp.int32, (rows, keys), 0) % SUB
    key = lax.broadcasted_iota(jnp.int32, (rows, keys), 1)
    same = row // steps == (key % SUB) // steps
    if keys == SUB:
        return same & (row >= key)
    return same & ((key < SUB) | (row >= key - SUB))


def softmax(query, keys, steps):
    raw = mm(query, keys, NT) * HDIM ** (-0.5)
    masked = jnp.where(visible(raw.shape[0], raw.shape[1], steps), raw, NEG)
    top = jnp.max(masked, axis=-1, keepdims=True)
    power = jnp.exp(masked - top)
    return power / jnp.sum(power, axis=-1, keepdims=True)


class Pieces:
    def __init__(self, entries, own, groups):
        self.entries = entries
        self.own = own
        self.groups = groups
        self.arrays = []
        for array, *_ in entries:
            if not any(array is a for a in self.arrays):
                self.arrays.append(array)
        self.count = len(self.arrays)
        self.shape = (sum(e[4] for e in entries), entries[0][0].shape[1])
        self.scratch = [pltpu.VMEM(self.shape, BF), pltpu.SemaphoreType.DMA((groups, len(entries)))]

    def copies(self, refs, places, memory, sems, group):
        wide = self.shape[1] // self.groups
        cols = pl.ds(group * wide, wide)
        for k, (array, slot, row, first, rows) in enumerate(self.entries):
            ref = [r for r, a in zip(refs, self.arrays) if a is array][0]
            start = row if slot is None else pl.multiple_of(places[slot] * self.own + row, rows)
            source = ref.at[pl.ds(first, rows), cols]
            yield pltpu.make_async_copy(source, memory.at[pl.ds(start, rows), cols], sems.at[group, k])

    def start(self, refs, places, memory, sems, order):
        @pl.when(pl.program_id(0) == 0)
        def _():
            for group in order:
                for copy in self.copies(refs, places, memory, sems, group):
                    copy.start()

    def wait(self, refs, places, memory, sems, group):
        @pl.when(pl.program_id(0) == 0)
        def _():
            for copy in self.copies(refs, places, memory, sems, group):
                copy.wait()


def attend_body(pieces, halves, steps, hw, later, places, *refs):
    x_ref, gain_ref, *refs = refs
    if later:
        before_ref, *refs = refs
    w_refs, refs = refs[: pieces.count], refs[pieces.count :]
    h_ref, qkv_ref, mixed_ref, mine_ref, other_ref, w_ref, sems = refs
    pieces.start(w_refs, places, w_ref, sems, range(1))
    normed, _ = norm(x_ref[...].astype(F32))
    hidden = (normed * gain_ref[...]).astype(BF)
    h_ref[...] = hidden
    pieces.wait(w_refs, places, w_ref, sems, 0)
    qkv = mm(hidden, w_ref[:, : 3 * hw]).astype(BF)
    qkv_ref[...] = qkv
    for s in range(x_ref.shape[0] // SUB):
        rows = slice(s * SUB, (s + 1) * SUB)
        for j in range(hw // PAIR):
            q, k, v = (qkv[rows, t * hw + j * PAIR : t * hw + (j + 1) * PAIR] for t in range(3))
            if later:
                k_old, v_old = (
                    before_ref[rows, t * hw + j * PAIR : t * hw + (j + 1) * PAIR] for t in (1, 2)
                )
                k = jnp.concatenate([k_old, k], axis=0)
                v = jnp.concatenate([v_old, v], axis=0)
            probs = softmax(stack_heads(q), k, steps).astype(BF)
            mixed_ref[rows, j * PAIR : (j + 1) * PAIR] = pick_heads(mm(probs, v)).astype(BF)
    halves.put((mine_ref, other_ref), mm(mixed_ref[...], w_ref[:, 3 * hw :], NT).astype(BF))


def attend(places, x, gain, before, w, steps):
    tokens, width = x.shape
    pieces, halves = Pieces(*w, 1), Halves(tokens)
    hw = pieces.shape[1] // 4
    ins = [x, gain]
    specs = [halves.both(width), whole(gain.shape)]
    if before is not None:
        ins.append(before)
        specs.append(halves.both(3 * hw))
    widths = (width, 3 * hw, hw)
    *out, mine, other = kernel_call(
        functools.partial(attend_body, pieces, halves, steps, hw, before is not None),
        halves.grid,
        [*ins, *pieces.arrays],
        [*specs, *[HBM] * pieces.count],
        [out_of((tokens, n)) for n in widths] + [out_of((tokens // 2, width))] * 2,
        [halves.both(n) for n in widths] + halves.pair(width),
        2 * tokens * width * 4 * hw,
        pieces.scratch,
        places,
    )
    return *out, (mine, other)


def units_body(pieces, halves, units, places, *refs):
    x_ref, att0, att1, g_ref, gain_ref, *refs = refs
    w_refs, refs = refs[: pieces.count], refs[pieces.count :]
    h_ref, inner_ref, dgate_ref, dup_ref, dh0, dh1, mlp0, mlp1, w_ref, sems = refs
    pieces.start(w_refs, places, w_ref, sems, (2, 0, 1))
    normed, _ = norm(x_ref[...].astype(F32) + halves.pick((att0, att1)).astype(F32))
    hidden = (normed * gain_ref[...]).astype(BF)
    h_ref[...] = hidden
    cut = 256
    cols = [
        [slice(t * units + u * cut, t * units + (u + 1) * cut) for t in range(3)] for u in range(units // cut)
    ]
    pieces.wait(w_refs, places, w_ref, sems, 2)
    d_inners = [mm(g_ref[...], w_ref[:, c[2]]) for c in cols]
    pieces.wait(w_refs, places, w_ref, sems, 0)
    pieces.wait(w_refs, places, w_ref, sems, 1)
    for c, d_inner in zip(cols, d_inners):
        gate = mm(hidden, w_ref[:, c[0]])
        up = mm(hidden, w_ref[:, c[1]])
        sigma = 1.0 / (1.0 + jnp.exp(-gate))
        active = gate * sigma
        inner_ref[:, c[0]] = (active * up).astype(BF)
        dup_ref[:, c[0]] = (d_inner * active).astype(BF)
        dgate_ref[:, c[0]] = (d_inner * up * sigma * (1.0 + gate * (1.0 - sigma))).astype(BF)
    grad = mm(dgate_ref[...], w_ref[:, :units], NT) + mm(dup_ref[...], w_ref[:, units : 2 * units], NT)
    halves.put((dh0, dh1), grad.astype(BF))
    halves.put((mlp0, mlp1), mm(inner_ref[...], w_ref[:, 2 * units :], NT).astype(BF))


def hidden_units(places, x, att, g, gain, w):
    tokens, width = x.shape
    pieces, halves = Pieces(*w, 3), Halves(tokens)
    units = pieces.shape[1] // 3
    part = halves.both(width)
    widths = (width, units, units, units)
    *out, dh0, dh1, mlp0, mlp1 = kernel_call(
        functools.partial(units_body, pieces, halves, units),
        halves.grid,
        (x, *att, g, gain, *pieces.arrays),
        [part, *halves.pair(width), part, whole(gain.shape), *[HBM] * pieces.count],
        [out_of((tokens, n)) for n in widths] + [out_of((tokens // 2, width))] * 4,
        [halves.both(n) for n in widths] + halves.pair(width) * 2,
        12 * tokens * width * units,
        pieces.scratch,
        places,
    )
    return *out, (dh0, dh1), (mlp0, mlp1)


def grads_body(runs, cut, steps, places, *refs):
    inputs = max(right for columns in runs for _, right in columns) + 1
    ins, outs = refs[:inputs], refs[inputs:]
    values = []
    for columns in runs:
        values.append([])
        for slots, k in columns:
            rows = [ins[s][...] for s in slots]
            rows = jnp.concatenate(rows, axis=1) if len(rows) > 1 else rows[0]
            values[-1].append(mm(rows, ins[k][...], TN).astype(BF))
    if not cut:
        at = 0
        for value in values[0]:
            outs[0][:, at : at + value.shape[1]] = value
            at += value.shape[1]
        return
    *outs, buffer, sems = outs
    height = outs[0].shape[0]
    own = height // len(runs)
    slots = ROWS // own

    def copies(block):
        at = 0
        for k in range(slots):
            t = block * slots + k
            for ref in outs[t : t + 1] if t < cut else outs[t : t + 2] if t == cut else outs[t + 1 : t + 2]:
                rows = buffer.at[block % 2, pl.ds(at, ref.shape[0])]
                yield pltpu.make_async_copy(rows, ref, sems.at[block % 2, at // (height // 2)])
                at += ref.shape[0]

    for block in range(steps):

        @pl.when(pl.program_id(0) == block)
        def _():
            if block >= 2:
                for copy in copies(block - 2):
                    copy.wait()
            for k in range(slots):
                for r, columns in enumerate(values):
                    at = 0
                    first = (k * len(runs) + r) * own
                    for value in columns:
                        cols = slice(at, at + value.shape[1])
                        buffer[block % 2, first : first + own, cols] = value[k * own : (k + 1) * own]
                        at += value.shape[1]
            for copy in copies(block):
                copy.start()
            if block == steps - 1:
                for last in range(max(0, steps - 2), steps):
                    for copy in copies(last):
                        copy.wait()


def weight_grads(places, runs, cut):
    count = places.shape[0] - 1
    tokens, width = runs[0][0][0].shape
    own = width // count
    steps = width // ROWS
    slots = ROWS // own if cut else 1
    ins, specs, marks = [], [], []
    for columns in runs:
        for left, _ in columns:
            mark = []
            for k in range(slots):
                place = (lambda i, p, k=k: (0, p[i * slots + k])) if cut else (lambda i, p: (0, i))
                ins.append(left)
                specs.append(pl.BlockSpec((tokens, ROWS // slots), place))
                mark.append(len(ins) - 1)
            marks.append(tuple(mark))
    pairs = []
    for columns in runs:
        pairs.append([])
        for _, right in columns:
            ins.append(right)
            specs.append(whole(right.shape))
            pairs[-1].append((marks.pop(0), len(ins) - 1))
    total = sum(right.shape[1] for _, right in runs[0])
    if cut:
        height = own * len(runs)
        heights = [height] * cut + [height // 2] * 2 + [height] * (count - cut - 1)
        outs = [out_of((h, total)) for h in heights]
        out_specs = [HBM] * len(outs)
        scratch = [
            pltpu.VMEM((2, slots * height, total), BF),
            pltpu.SemaphoreType.DMA((2, 2 * slots)),
        ]
    else:
        outs, out_specs, scratch = [out_of((width, total))], [rows_of(ROWS, total)], []
    return kernel_call(
        functools.partial(grads_body, pairs, cut, steps),
        (steps,),
        ins,
        specs,
        outs,
        out_specs,
        2 * tokens * width * total,
        scratch,
        places,
    )


def norm_back(grad_hidden, value, gain):
    normed, scale = norm(value)
    scaled = grad_hidden * gain
    back = scale * (scaled - normed * jnp.mean(scaled * normed, axis=-1, keepdims=True))
    return back, jnp.sum(grad_hidden * normed, axis=0, keepdims=True)


def add_up(ref, value):
    @pl.when(pl.program_id(0) == 0)
    def _():
        ref[...] = jnp.zeros_like(ref)

    ref[...] += value


def middle_body(halves, _, x_ref, att0, att1, g_ref, dh0, dh1, gain_ref, dm_ref, dgain_ref):
    value = x_ref[...].astype(F32) + halves.pick((att0, att1)).astype(F32)
    back, d_gain = norm_back(halves.pick((dh0, dh1)).astype(F32), value, gain_ref[...])
    dm_ref[...] = (g_ref[...].astype(F32) + back).astype(BF)
    add_up(dgain_ref, d_gain)


def middle_back(places, x, att, g, dh, gain):
    tokens, width = x.shape
    halves = Halves(tokens)
    part, pair = halves.both(width), halves.pair(width)
    return kernel_call(
        functools.partial(middle_body, halves),
        halves.grid,
        (x, *att, g, *dh, gain),
        [part, *pair, part, *pair, whole(gain.shape)],
        [out_of((tokens, width)), out_of((1, width), F32)],
        [part, whole((1, width))],
        0,
        (),
        places,
    )


def attend_back_body(pieces, shared, steps, hw, places, x0, x1, dm0, dm1, qkv0, qkv1, *refs):
    sides = [
        [r for a in p.arrays for r, b in zip(refs, shared.arrays) if a is b] for p in pieces
    ]
    dqkv0, dqkv1, mine, other, dgain, w0, sems0, w1, sems1 = refs[-9:]
    for p, s, w, sems in zip(pieces, sides, (w0, w1), (sems0, sems1)):
        p.start(s, places, w, sems, range(1))
    normed = [norm(x[...].astype(F32))[0] for x in (x0, x1)]
    for p, s, w, sems in zip(pieces, sides, (w0, w1), (sems0, sems1)):
        p.wait(s, places, w, sems, 0)
    scale = HDIM ** (-0.5)
    d_mixed = [mm(d[...], w[:, 3 * hw :]).astype(BF) for d, w in ((dm0, w0), (dm1, w1))]
    for s in range(dm0.shape[0] // SUB):
        rows = slice(s * SUB, (s + 1) * SUB)
        for j in range(hw // PAIR):
            cols = [slice(t * hw + j * PAIR, t * hw + (j + 1) * PAIR) for t in range(3)]
            q0, k0, v0 = (qkv0[rows, c] for c in cols)
            q1, k1, v1 = (qkv1[rows, c] for c in cols)
            keys = (k0, jnp.concatenate([k0, k1], axis=0))
            values = (v0, jnp.concatenate([v0, v1], axis=0))
            d_k, d_v = [], []
            for c, (q, out_ref) in enumerate(((q0, dqkv0), (q1, dqkv1))):
                q_two = stack_heads(q)
                d_two = stack_heads(d_mixed[c][rows, cols[0]])
                soft = softmax(q_two, keys[c], steps)
                d_probs = mm(d_two, values[c], NT)
                inside = jnp.sum(soft * d_probs, axis=-1, keepdims=True)
                d_scores = (soft * (d_probs - inside)).astype(BF)
                d_q = pick_heads(mm(d_scores, keys[c])) * scale
                out_ref[rows, cols[0]] = d_q.astype(BF)
                d_k.append(mm(d_scores, q_two, TN) * scale)
                d_v.append(mm(soft.astype(BF), d_two, TN))
            dqkv0[rows, cols[1]] = (d_k[0] + d_k[1][:SUB]).astype(BF)
            dqkv1[rows, cols[1]] = d_k[1][SUB:].astype(BF)
            dqkv0[rows, cols[2]] = (d_v[0] + d_v[1][:SUB]).astype(BF)
            dqkv1[rows, cols[2]] = d_v[1][SUB:].astype(BF)
    gains = []
    for c, (d, w) in enumerate(((dqkv0, w0), (dqkv1, w1))):
        grad = mm(d[...], w[:, : 3 * hw], NT)
        gains.append(jnp.sum(grad * normed[c], axis=0, keepdims=True))
        mine[c * ROWS : (c + 1) * ROWS] = grad.astype(BF)

    @pl.when(pl.program_id(0) == 0)
    def _():
        other[...] = mine[...]

    add_up(dgain, jnp.concatenate(gains, axis=0))


def attend_back(places, x, dm, qkv, w, part, before, steps):
    tokens, width = dm[0].shape
    halves = Halves(tokens)
    pieces = [Pieces(*side, 1) for side in w]
    shared = Pieces(w[0][0] + w[1][0], w[0][1], 1)
    hw = pieces[0].shape[1] // 4
    spot = lambda i, p: (halves.block(i * halves.count, p) + part, 0)
    flat, thin = pl.BlockSpec((ROWS, width), spot), pl.BlockSpec((ROWS, 3 * hw), spot)
    ins = [*x, *dm, *qkv, *shared.arrays, *(before or ())]
    specs = [flat] * 4 + [thin] * 2 + [HBM] * (len(ins) - 6)
    alias = {len(ins) - 1: 0, len(ins): 1} if before else {}
    d0, d1, mine, other, d_gain = kernel_call(
        functools.partial(attend_back_body, pieces, shared, steps, hw),
        (2,),
        ins,
        specs,
        [out_of((tokens, 3 * hw))] * 2 + [out_of((2 * ROWS, width))] * 2 + [out_of((2, width), F32)],
        [thin] * 2 + [whole((2 * ROWS, width))] * 2 + [whole((2, width))],
        8 * ROWS * width * 4 * hw,
        pieces[0].scratch + pieces[1].scratch,
        places,
        alias,
    )
    return (d0, d1), (mine, other), d_gain


def store_frames(out_ref, sums):
    frames, _, width = out_ref.shape
    both = [p.reshape(frames, 1, p.shape[0] // frames, width) for p in sums]
    out_ref[...] = jnp.concatenate(both, axis=1).reshape(frames, -1, width).astype(BF)


def output_body(halves, _, x0, x1, *refs):
    *refs, out_ref = refs
    pairs = [halves.pick(refs[k : k + 2]).astype(F32) for k in range(0, 8, 2)]
    sums = [x[...].astype(F32) + pairs[2 * c] + pairs[2 * c + 1] for c, x in enumerate((x0, x1))]
    store_frames(out_ref, sums)


def output_of(places, x, att, mlp, shape):
    frames, steps, width = shape
    halves = Halves(x[0].shape[0])
    sides = [a for c in range(2) for pair in (att[c], mlp[c]) for a in pair]
    cube = pl.BlockSpec((2 * ROWS // steps, steps, width), lambda i, p: (halves.block(i, p), 0, 0))
    return kernel_call(
        functools.partial(output_body, halves),
        halves.grid,
        [*x, *sides],
        [halves.both(width)] * 2 + halves.pair(width) * 4,
        [out_of(shape)],
        [cube],
        0,
        (),
        places,
    )[0]


def input_body(_, x0, x1, dm0, dm1, mine, other, gain_ref, *refs):
    first = pl.program_id(0) == 0
    sums = []
    for c, (x, dm) in enumerate(((x0, dm0), (x1, dm1))):
        rows = slice(c * ROWS, (c + 1) * ROWS)
        dh = jnp.where(first, other[rows], mine[rows]).astype(F32)
        back, _ = norm_back(dh, x[...].astype(F32), gain_ref[c : c + 1])
        sums.append(dm[...].astype(F32) + back)
    store_frames(refs[-1], sums)


def input_back(places, x, dm, dh, gain, part, before, shape):
    frames, steps, width = shape
    halves = Halves(x[0].shape[0])
    block = lambda i, p: halves.block(i * halves.count, p) + part
    flat = pl.BlockSpec((ROWS, width), lambda i, p: (block(i, p), 0))
    cube = pl.BlockSpec((2 * ROWS // steps, steps, width), lambda i, p: (block(i, p), 0, 0))
    ins = [*x, *dm, *dh, gain]
    specs = [flat] * 4 + [whole(d.shape) for d in dh] + [whole(gain.shape)]
    alias = {}
    if before is not None:
        ins.append(before)
        specs.append(HBM)
        alias = {len(ins): 0}
    return kernel_call(input_body, (2,), ins, specs, [out_of(shape)], [cube], 0, (), places, alias)[0]


def finish_body(layout, turned, *refs):
    count = 1 + max(k for terms, _ in layout for k in terms)
    ins, outs = refs[:count], refs[count:]
    own, wide = outs[0].shape[1:]
    for c, (terms, first) in enumerate(layout):
        rows = slice(first, first + own)
        for t, ref in enumerate(outs):
            cols = slice(t * wide, (t + 1) * wide)
            total = ins[terms[0]][rows, cols].astype(F32)
            for k in terms[1:]:
                total = total + ins[k][rows, cols].astype(F32)
            ref[c] = total.T if t == turned else total


def finish(sides, kinds, own):
    arrays, layout = [], []
    for terms, first in sides:
        spots = []
        for term in terms:
            found = [k for k, a in enumerate(arrays) if a is term]
            if not found:
                arrays.append(term)
            spots.append(found[0] if found else len(arrays) - 1)
        layout.append((spots, first))
    wide = arrays[0].shape[1] // kinds
    shapes = [(len(sides), own, wide)] * (kinds - 1) + [(len(sides), wide, own)]
    return kernel_call(
        functools.partial(finish_body, layout, kinds - 1),
        (1,),
        arrays,
        [whole(a.shape) for a in arrays],
        [out_of(s, F32) for s in shapes],
        [whole(s) for s in shapes],
        0,
    )


class Ring:
    def __init__(self, size):
        self.size = size
        self.rings = size <= 16
        half = size // 2
        order = [2 * q for q in range(half)] + [2 * (size - 1 - q) + 1 for q in range(half, size)]
        self.ahead = [(order[q], order[(q + 1) % size]) for q in range(size)]
        self.behind = [(b, a) for a, b in self.ahead]
        self.me = lax.axis_index("dp")
        place = jnp.where(self.me % 2 == 0, self.me // 2, size - 1 - self.me // 2)
        q = lax.rem(place + jnp.arange(size, dtype=jnp.int32), size)
        self.order = jnp.where(q < half, 2 * q, 2 * (size - 1 - q) + 1).astype(jnp.int32)


class Rounds:
    def __init__(self):
        self.done = ()

    def now(self, value):
        return lax.optimization_barrier((value, *self.done))[0] if self.done else value

    def close(self, *arrays):
        self.done = arrays


class Gather:
    def __init__(self, rounds, ring, shard):
        self.rounds, self.ring = rounds, ring
        self.a, self.b = [shard], [shard]

    def step(self):
        a, b = self.a[-1], self.b[-1]
        if len(self.a) == self.ring.size // 2:
            half = a.shape[0] // 2
            a, b = a[:half], b[half:]
        self.a.append(lax.ppermute(self.rounds.now(a), "dp", self.ring.ahead))
        self.b.append(lax.ppermute(self.rounds.now(b), "dp", self.ring.behind))
        return self.a[-1], self.b[-1]

    def entries(self, part=0, parts=1):
        n = self.ring.size
        own = self.a[0].shape[0] // parts
        found = []
        for t in range(n):
            if t != n // 2:
                found.append((self.b[t] if t < n // 2 else self.a[n - t], t, 0, part * own, own))
            elif parts == 1:
                found.append((self.a[t], t, 0, 0, own // 2))
                found.append((self.b[t], t, own // 2, 0, own // 2))
            else:
                found.append(((self.a[t], self.b[t])[part], t, 0, 0, own))
        return found, own


class Scatter:
    def __init__(self, rounds, ring, blocks):
        self.rounds, self.ring = rounds, ring
        far = ring.size // 2
        self.a, self.b = blocks[far], blocks[far + 1]
        self.blocks = [*blocks[:far], None, *blocks[far + 2 :]]
        self.k = far

    def step(self):
        n = self.ring.size
        if self.k < n // 2:
            one, two = self.blocks[self.k].astype(F32), self.blocks[n - self.k].astype(F32)
            a, b = self.a.astype(F32), self.b.astype(F32)
            if self.k == n // 2 - 1:
                half = a.shape[0]
                a = jnp.pad(a, ((0, half), (0, 0)))
                b = jnp.pad(b, ((half, 0), (0, 0)))
            self.a, self.b = (one + a).astype(BF), (two + b).astype(BF)
        self.k -= 1
        self.a = lax.ppermute(self.rounds.now(self.a), "dp", self.ring.ahead)
        self.b = lax.ppermute(self.rounds.now(self.b), "dp", self.ring.behind)
        return self.a, self.b

    def terms(self):
        return [self.blocks[0], self.a, self.b]


class HeadSum:
    def __init__(self, rounds, pair):
        size = lax.axis_size("mp")
        self.rounds, self.pair, self.got = rounds, pair, []
        self.near_moves = [(i, i ^ 1) for i in range(size)]
        self.far_moves = [(i, i ^ 2) for i in range(size)]

    def add(self, one, two):
        return (one.astype(F32) + two.astype(F32)).astype(BF)

    def near(self):
        got = lax.ppermute(self.rounds.now(self.pair[1]), "mp", self.near_moves)
        self.mine = self.add(self.pair[0], got)
        return self.mine

    def far(self, parts=1):
        rows = self.mine.shape[0] // parts
        start = len(self.got) * rows
        self.got.append(lax.ppermute(self.rounds.now(self.mine[start : start + rows]), "mp", self.far_moves))
        return self.got[-1]

    def last(self):
        got = [self.rounds.now(got) for got in self.got]
        self.mine = self.add(self.mine, jnp.concatenate(got, 0))
        self.sum = (self.mine, lax.ppermute(self.mine, "mp", self.near_moves))
        return self.sum[1]


def exchange_steps(axes):
    for axis in axes:
        size, step = lax.axis_size(axis), 1
        while step < size:
            yield axis, [(i, i ^ step) for i in range(size)], step
            step *= 2


def on_device(
    layer_input, frame_mask, gain_attn, w_query, w_key, w_value, w_out, gain_ffn, w_gate, w_up,
    w_down, cotangent,
):
    sets, width = gain_attn.shape[0], layer_input.shape[2]
    shape = layer_input.shape
    each = shape[1] // sets
    ring = Ring(lax.axis_size("dp"))
    rings, n = ring.rings, ring.size
    far = n // 2 if rings else 0
    own = width // n
    places = jnp.concatenate([ring.order, (lax.axis_index("mp") % 2).astype(jnp.int32)[None]])
    gather = lambda value: lax.all_gather(value, "dp", tiled=True)
    scatter = lambda value: lax.psum_scatter(value, "dp", scatter_dimension=0, tiled=True)
    rounds = Rounds()
    now, close = rounds.now, rounds.close

    attn_own = pack_attn(w_query, w_key, w_value, w_out)
    small = jnp.concatenate([gain_attn, gain_ffn], 0).astype(F32)[None]
    steps = list(exchange_steps(("dp",)))
    ffn_own, x, g = [], [], []

    def gain_step(value):
        axis, moves, step = steps.pop(0)
        other = lax.ppermute(now(value), axis, moves)
        bit = (ring.me // step) % 2
        both = [jnp.concatenate(pair, 0) for pair in ((value, other), (other, value))]
        return jnp.where(bit == 0, *both)

    masks = frame_mask.astype(BF)[:, None, None]
    chores = [
        lambda: ffn_own.append(pack_ffn(now(w_gate), w_up, w_down, 0)),
        lambda: x.append(split_sets(now(layer_input), sets)[0]),
        lambda: ffn_own.append(pack_ffn(now(w_gate), w_up, w_down, 1)),
        lambda: x.append(split_sets(now(layer_input), sets)[1]),
        lambda: g.append(split_sets(now(cotangent) * masks, sets)[0]),
        lambda: g.append(split_sets(now(cotangent) * masks, sets)[1]),
    ]
    attn = Gather(rounds, ring, attn_own)
    for k in range(max(far, 3)):
        moved = attn.step() if rings else ()
        if rings and k == far - 1:
            rows = [Gather(rounds, ring, shard) for shard in ffn_own]
            moved += rows[0].step()
        for chore in chores[:2]:
            chore()
        del chores[:2]
        if steps:
            small = gain_step(small)
        close(small, *moved, *[v[-1] for v in (ffn_own, x, g) if v])
    while steps:
        small = gain_step(small)
    gains = small.transpose(1, 0, 2).reshape(2 * sets, width)
    g_attn, g_ffn = [[gains[k * sets + c][None] for c in range(sets)] for k in range(2)]
    if rings:
        w_attn = [attn.entries(c, sets) for c in range(sets)]
    else:
        both = gather(attn_own).reshape(n, sets, own, -1)
        w_attn = [([(both[:, c].reshape(width, -1), None, 0, 0, width)], width) for c in range(sets)]

    def move(c):
        return rows[c].step() if rings else ()

    def weights(c):
        if rings:
            return rows[c].entries()
        return [(gather(ffn_own[c]), None, 0, 0, width)], width

    h1, qkv, mixed, heads = [None] * 2, [None] * 2, [None] * 2, [None] * 2
    moved = move(0)
    h1[0], qkv[0], mixed[0], part = attend(now(places), x[0], g_attn[0], None, w_attn[0], each)
    heads[0] = HeadSum(rounds, part)
    close(*moved, part[0])
    close(heads[0].near())
    moved = move(0)
    got = heads[0].far()
    h1[1], qkv[1], mixed[1], part = attend(now(places), x[1], g_attn[1], qkv[0], w_attn[1], each)
    heads[1] = HeadSum(rounds, part)
    close(*moved, part[0], got)
    close(*move(0), heads[1].near(), heads[0].last())

    def grads_of(c, out):
        columns = [(out[0], out[2]), (out[0], out[3]), (g[c], out[1])]
        return weight_grads(now(places), [columns], far)

    dh, mlp, grads, dm, d_gain_ffn = ([None] * 2 for _ in range(5))
    moved = move(1)
    got = heads[1].far()
    out = hidden_units(now(places), x[0], heads[0].sum, g[0], g_ffn[0], weights(0))
    dh[0], mlp[0] = HeadSum(rounds, out[4]), HeadSum(rounds, out[5])
    close(*moved, out[0], got)
    moved = move(1)
    grads[0] = grads_of(0, out)
    close(*moved, grads[0][0], dh[0].near(), mlp[0].near(), heads[1].last())
    att = [head.sum for head in heads]
    sums = [Scatter(rounds, ring, grads[0])] if rings else []
    add = lambda k: sums[k].step() if rings else ()
    close(*move(1), mlp[0].far(2))
    close(*move(1), *add(0), mlp[0].far(2))

    moved = add(0)
    got = dh[0].far()
    out = hidden_units(now(places), x[1], att[1], g[1], g_ffn[1], weights(1))
    dh[1], mlp[1] = HeadSum(rounds, out[4]), HeadSum(rounds, out[5])
    close(*moved, out[0], got)
    close(dh[1].near(), dh[0].last(), mlp[0].last())
    moved = add(0)
    got = dh[1].far()
    grads[1] = grads_of(1, out)
    dm[0], d_gain_ffn[0] = middle_back(now(places), x[0], att[0], g[0], dh[0].sum, g_ffn[0])
    close(*moved, grads[1][0], dm[0], got)
    if rings:
        sums.append(Scatter(rounds, ring, grads[1]))

    moved = (*add(0), *add(1))
    dh[1].last()
    dm[1], d_gain_ffn[1] = middle_back(now(places), x[1], att[1], g[1], dh[1].sum, g_ffn[1])
    d_qkv, part, d_gain0 = attend_back(now(places), x, dm, qkv, w_attn, 0, None, each)
    back = [HeadSum(rounds, part)]
    close(*moved, part[0])
    close(back[0].near(), mlp[1].near())
    moved = add(1)
    got = back[0].far()
    d_qkv, part, d_gain1 = attend_back(now(places), x, dm, qkv, w_attn, 1, d_qkv, each)
    back.append(HeadSum(rounds, part))
    close(*moved, part[0], got)

    shared = lax.axis_size("mp")
    d_gains = jnp.concatenate([d_gain0 + d_gain1, *[d / shared for d in d_gain_ffn]], 0)
    steps = list(exchange_steps(("mp", "dp")))

    def sum_step(value):
        axis, moves, _ = steps.pop(0)
        return value + lax.ppermute(now(value), axis, moves)

    d_gains = sum_step(d_gains)
    close(back[1].near(), back[0].last(), d_gains)
    gain = gains[:sets]
    moved = add(1)
    got = back[1].far()
    d_gains = sum_step(d_gains)
    runs = [[(h1[c], d_qkv[c]), (dm[c], mixed[c])] for c in range(sets)]
    if rings:
        blocks = weight_grads(now(places), runs, far)
        sums.append(Scatter(rounds, ring, blocks))
    else:
        blocks = [weight_grads(now(places), [run], far)[0] for run in runs]
    grad_input = input_back(now(places), x, dm, back[0].sum, gain, 0, None, shape)
    close(*moved, blocks[0], grad_input, got, d_gains)
    close(*add(2), *add(1), mlp[1].far())
    moved = add(2)
    d_gains = sum_step(d_gains)
    if rings:
        ffn_sums = [([now(t) for t in s.terms()], 0) for s in sums[:2]]
    else:
        ffn_sums = [([scatter(b[0])], 0) for b in grads]
    d_gate_w, d_up_w, d_down_w = finish(ffn_sums, 3, own)
    close(*moved, d_gains, d_gate_w, back[1].last(), mlp[1].last())
    moved = add(2)
    d_gains = sum_step(d_gains)
    output = output_of(now(places), x, att, [m.sum for m in mlp], shape)
    close(*moved, output, d_gains)
    moved = add(2)
    grad_input = input_back(now(places), x, dm, back[1].sum, gain, 1, grad_input, shape)
    while steps:
        d_gains = sum_step(d_gains)
    close(*moved, grad_input, d_gains)
    if rings:
        terms = [now(t) for t in sums[2].terms()]
        attn_sums = [(terms, c * own) for c in range(sets)]
    else:
        attn_sums = [([scatter(b)], 0) for b in blocks]
    d_query, d_key, d_value, d_out = finish(attn_sums, 4, own)
    d_gains = lax.dynamic_slice_in_dim(d_gains, ring.me * own, own, 1)
    return (
        output, grad_input, d_gains[:sets], d_query, d_key, d_value, d_out,
        d_gains[sets:], d_gate_w, d_up_w, d_down_w,
    )


def solution(mesh):
    rows = P("dp", None, None)
    gain = P(None, "dp")
    into = P(None, "dp", "mp")
    back = P(None, "mp", "dp")
    weights = (gain, into, into, into, back, gain, into, into, back)
    return jax.shard_map(
        on_device,
        mesh=mesh,
        in_specs=(rows, P("dp"), *weights, rows),
        out_specs=(rows, rows, *weights),
        check_vma=False,
    )
```

```python
import functools

import jax
import jax.numpy as jnp
from jax import lax
from jax.experimental import pallas as pl
from jax.experimental.pallas import tpu as pltpu
from jax.sharding import PartitionSpec as P

HDIM = 64
EPS = 1e-05
NEG = -1e30
BF = jnp.bfloat16
F32 = jnp.float32
NN = (((1,), (0,)), ((), ()))
NT = (((1,), (1,)), ((), ()))
TN = (((0,), (0,)), ((), ()))
MIB = 1024 * 1024
SUB = 128
PAIR = 2 * HDIM
ROWS = 256
HBM = pl.BlockSpec(memory_space=pl.ANY)


def mm(left, right, dims=NN):
    return lax.dot_general(left, right, dims, preferred_element_type=F32)


def kernel_call(body, grid, ins, in_specs, outs, out_specs, flops, scratch=(), scalars=None, alias=None):
    moved = sum(a.size * a.dtype.itemsize for a in ins) + sum(
        o.size * jnp.dtype(o.dtype).itemsize for o in outs
    )
    spec = pltpu.PrefetchScalarGridSpec(
        num_scalar_prefetch=0 if scalars is None else 1,
        grid=grid,
        in_specs=in_specs,
        out_specs=out_specs,
        scratch_shapes=scratch,
    )
    args = ins if scalars is None else (scalars, *ins)
    return pl.pallas_call(
        body,
        grid_spec=spec,
        out_shape=outs,
        input_output_aliases=alias or {},
        compiler_params=pltpu.CompilerParams(vmem_limit_bytes=56 * MIB),
        cost_estimate=pl.CostEstimate(flops=1, bytes_accessed=1, transcendentals=0),
    )(*args)


def whole(shape):
    return pl.BlockSpec(shape, lambda *i: (0,) * len(shape))


def rows_of(rows, width, start=0):
    return pl.BlockSpec((rows, width), lambda i, *_: (i + start, 0))


def out_of(shape, kind=BF):
    return jax.ShapeDtypeStruct(shape, kind)


class Halves:
    def __init__(self, tokens):
        self.count = tokens // 2 // ROWS
        self.grid = (2 * self.count,)

    def block(self, i, places):
        half = (1 - i // self.count + places[places.shape[0] - 1]) % 2
        return half * self.count + i % self.count

    def both(self, width):
        return pl.BlockSpec((ROWS, width), lambda i, p: (self.block(i, p), 0))

    def pair(self, width):
        return [
            pl.BlockSpec((ROWS, width), lambda i, p: (jnp.maximum(i - self.count, 0), 0)),
            pl.BlockSpec((ROWS, width), lambda i, p: (jnp.minimum(i, self.count - 1), 0)),
        ]

    def pick(self, pair):
        return jnp.where(pl.program_id(0) < self.count, pair[1][...], pair[0][...])

    def one(self, width, half):
        shift = 0 if half else self.count
        return pl.BlockSpec((ROWS, width), lambda i, p: (self.block(i + shift, p), 0))

    def put(self, pair, value):
        pair[0][...] = value

        @pl.when(pl.program_id(0) < self.count)
        def _():
            pair[1][...] = pair[0][...]


def split_sets(value, sets):
    frames, steps, width = value.shape
    parts = value.reshape(frames, sets, steps // sets, width)
    return [parts[:, c].reshape(-1, width) for c in range(sets)]


def pack_attn_body(wq, wk, wv, wo, out):
    own, hw = wq.shape[1:]
    for c in range(2):
        rows = slice(c * own, (c + 1) * own)
        for t, w in enumerate((wq, wk, wv)):
            out[rows, t * hw : (t + 1) * hw] = w[c]
        out[rows, 3 * hw :] = wo[c].T


def pack_attn(wq, wk, wv, wo):
    sets, own, hw = wq.shape
    piece = (sets * own, 4 * hw)
    return kernel_call(
        pack_attn_body,
        (1,),
        (wq, wk, wv, wo),
        [whole(w.shape) for w in (wq, wk, wv, wo)],
        [out_of(piece)],
        [whole(piece)],
        0,
    )[0]


def pack_ffn_body(wg, wu, wd, out):
    units = wg.shape[2]
    out[:, :units] = wg[0]
    out[:, units : 2 * units] = wu[0]
    out[:, 2 * units :] = wd[0].T


def pack_ffn(wg, wu, wd, c):
    own, units = wg.shape[1:]
    piece = (own, 3 * units)
    into = pl.BlockSpec((1, own, units), lambda i: (c, 0, 0))
    back = pl.BlockSpec((1, units, own), lambda i: (c, 0, 0))
    return kernel_call(
        pack_ffn_body,
        (1,),
        (wg, wu, wd),
        [into, into, back],
        [out_of(piece)],
        [whole(piece)],
        0,
    )[0]


def norm(value):
    scale = lax.rsqrt(jnp.mean(value * value, axis=-1, keepdims=True) + EPS)
    return value * scale, scale


def lanes_low(shape):
    return lax.broadcasted_iota(jnp.int32, shape, 1) < HDIM


def stack_heads(pair):
    low = lanes_low(pair.shape)
    zero = jnp.zeros_like(pair)
    return jnp.concatenate([jnp.where(low, pair, zero), jnp.where(low, zero, pair)], axis=0)


def pick_heads(stacked):
    half = stacked.shape[0] // 2
    low = lanes_low((half, stacked.shape[1]))
    return jnp.where(low, stacked[:half], stacked[half:])


def hidden_keys(rows, keys, steps, turned=False):
    shape, axis = ((keys, rows), 1) if turned else ((rows, keys), 0)
    row = lax.broadcasted_iota(jnp.int32, shape, axis) & (SUB - 1)
    spot = lax.broadcasted_iota(jnp.int32, shape, 1 - axis)
    key = spot & (SUB - 1)
    shift = steps.bit_length() - 1
    seen = lax.shift_right_logical(row, shift) == lax.shift_right_logical(key, shift)
    own = spot >= keys - SUB
    seen = seen & ((row >= key) | jnp.logical_not(own))
    return jnp.where(seen, 0.0, NEG)


def softmax(query, keys, hidden):
    raw = mm(query, keys, NT) + hidden
    power = jnp.exp(raw - jnp.max(raw, axis=-1, keepdims=True))
    return power * (1.0 / jnp.sum(power, axis=-1, keepdims=True))


def softmax_turned(query, keys, hidden):
    raw = mm(keys, query, NT) + hidden
    power = jnp.exp(raw - jnp.max(raw, axis=0, keepdims=True))
    return power * (1.0 / jnp.sum(power, axis=0, keepdims=True))


class Pieces:
    def __init__(self, entries, own, groups):
        self.entries = entries
        self.own = own
        self.groups = groups
        self.arrays = []
        for array, *_ in entries:
            if not any(array is a for a in self.arrays):
                self.arrays.append(array)
        self.count = len(self.arrays)
        self.shape = (sum(e[4] for e in entries), entries[0][0].shape[1])
        self.scratch = [pltpu.VMEM(self.shape, BF), pltpu.SemaphoreType.DMA((groups, len(entries)))]

    def copies(self, refs, places, memory, sems, group):
        wide = self.shape[1] // self.groups
        cols = pl.ds(group * wide, wide)
        for k, (array, slot, row, first, rows) in enumerate(self.entries):
            ref = [r for r, a in zip(refs, self.arrays) if a is array][0]
            start = row if slot is None else pl.multiple_of(places[slot] * self.own + row, rows)
            source = ref.at[pl.ds(first, rows), cols]
            yield pltpu.make_async_copy(source, memory.at[pl.ds(start, rows), cols], sems.at[group, k])

    def start(self, refs, places, memory, sems, order):
        @pl.when(pl.program_id(0) == 0)
        def _():
            for group in order:
                for copy in self.copies(refs, places, memory, sems, group):
                    copy.start()

    def wait(self, refs, places, memory, sems, group):
        @pl.when(pl.program_id(0) == 0)
        def _():
            for copy in self.copies(refs, places, memory, sems, group):
                copy.wait()


def attend_body(pieces, halves, steps, hw, later, filled, places, *refs):
    x_ref, gain_ref, *refs = refs
    if later:
        before_ref, *refs = refs
    w_refs, refs = refs[: pieces.count], refs[pieces.count :]
    h_ref, qkv_ref, mixed_ref, *part_refs, w_ref, sems = refs[filled:]
    pieces.start(w_refs, places, w_ref, sems, range(1))
    normed, _ = norm(x_ref[...].astype(F32))
    hidden = (normed * gain_ref[...]).astype(BF)
    h_ref[...] = hidden
    pieces.wait(w_refs, places, w_ref, sems, 0)
    qkv = mm(hidden, w_ref[:, : 3 * hw]).astype(BF)
    qkv_ref[...] = qkv
    scale = jnp.asarray(HDIM ** (-0.5), BF)
    hidden_scores = hidden_keys(2 * SUB, 2 * SUB if later else SUB, steps)
    for s in range(x_ref.shape[0] // SUB):
        rows = slice(s * SUB, (s + 1) * SUB)
        for j in range(hw // PAIR):
            q, k, v = (qkv[rows, t * hw + j * PAIR : t * hw + (j + 1) * PAIR] for t in range(3))
            if later:
                k_old, v_old = (
                    before_ref[rows, t * hw + j * PAIR : t * hw + (j + 1) * PAIR] for t in (1, 2)
                )
                k = jnp.concatenate([k_old, k], axis=0)
                v = jnp.concatenate([v_old, v], axis=0)
            probs = softmax(stack_heads(q) * scale, k, hidden_scores).astype(BF)
            mixed_ref[rows, j * PAIR : (j + 1) * PAIR] = pick_heads(mm(probs, v)).astype(BF)
    part = mm(mixed_ref[...], w_ref[:, 3 * hw :], NT).astype(BF)
    if len(part_refs) == 2:
        halves.put(part_refs, part)
    else:
        part_refs[0][...] = part


def attend(places, x, gain, before, w, steps, half=None, filled=()):
    tokens, width = x.shape
    pieces, halves = Pieces(*w, 1), Halves(tokens)
    hw = pieces.shape[1] // 4
    spec = halves.both if half is None else functools.partial(halves.one, half=half)
    ins = [x, gain]
    specs = [spec(width), whole(gain.shape)]
    if before is not None:
        ins.append(before)
        specs.append(spec(3 * hw))
    ins += [*pieces.arrays, *filled]
    specs += [HBM] * (pieces.count + len(filled))
    widths = (width, 3 * hw, hw)
    *out, part = kernel_call(
        functools.partial(attend_body, pieces, halves, steps, hw, before is not None, len(filled)),
        halves.grid if half is None else (halves.count,),
        ins,
        specs,
        [out_of((tokens, n)) for n in widths] + [out_of((tokens // 2, width))] * (2 if half is None else 1),
        [spec(n) for n in widths] + (halves.pair(width) if half is None else [rows_of(ROWS, width)]),
        2 * tokens * width * 4 * hw,
        pieces.scratch,
        places,
        {len(ins) - len(filled) + 1 + k: k for k in range(len(filled))},
    )
    if half is None:
        return *out[:3], (out[3], part)
    return *out, part


def units_body(pieces, halves, units, places, *refs):
    x_ref, att0, att1, g_ref, gain_ref, *refs = refs
    w_refs, refs = refs[: pieces.count], refs[pieces.count :]
    h_ref, inner_ref, dboth_ref, dh0, dh1, mlp0, mlp1, w_ref, sems = refs
    pieces.start(w_refs, places, w_ref, sems, (2, 0, 1))
    normed, _ = norm(x_ref[...].astype(F32) + halves.pick((att0, att1)).astype(F32))
    hidden = (normed * gain_ref[...]).astype(BF)
    h_ref[...] = hidden
    cut = 256
    cols = [
        [slice(t * units + u * cut, t * units + (u + 1) * cut) for t in range(3)] for u in range(units // cut)
    ]
    pieces.wait(w_refs, places, w_ref, sems, 2)
    d_inners = [mm(g_ref[...], w_ref[:, c[2]]) for c in cols]
    pieces.wait(w_refs, places, w_ref, sems, 0)
    pieces.wait(w_refs, places, w_ref, sems, 1)
    for c, d_inner in zip(cols, d_inners):
        gate = mm(hidden, w_ref[:, c[0]])
        up = mm(hidden, w_ref[:, c[1]])
        sigma = 1.0 / (1.0 + jnp.exp(-gate))
        active = gate * sigma
        inner_ref[:, c[0]] = (active * up).astype(BF)
        dboth_ref[:, c[1]] = (d_inner * active).astype(BF)
        dboth_ref[:, c[0]] = (d_inner * up * (sigma + active * (1.0 - sigma))).astype(BF)
    halves.put((dh0, dh1), mm(dboth_ref[...], w_ref[:, : 2 * units], NT).astype(BF))
    halves.put((mlp0, mlp1), mm(inner_ref[...], w_ref[:, 2 * units :], NT).astype(BF))


def hidden_units(places, x, att, g, gain, w):
    tokens, width = x.shape
    pieces, halves = Pieces(*w, 3), Halves(tokens)
    units = pieces.shape[1] // 3
    part = halves.both(width)
    widths = (width, units, 2 * units)
    *out, dh0, dh1, mlp0, mlp1 = kernel_call(
        functools.partial(units_body, pieces, halves, units),
        halves.grid,
        (x, *att, g, gain, *pieces.arrays),
        [part, *halves.pair(width), part, whole(gain.shape), *[HBM] * pieces.count],
        [out_of((tokens, n)) for n in widths] + [out_of((tokens // 2, width))] * 4,
        [halves.both(n) for n in widths] + halves.pair(width) * 2,
        12 * tokens * width * units,
        pieces.scratch,
        places,
    )
    return *out, (dh0, dh1), (mlp0, mlp1)


def grads_body(runs, cut, steps, places, *refs):
    inputs = max(right for columns in runs for _, right in columns) + 1
    ins, outs = refs[:inputs], refs[inputs:]
    values = []
    for columns in runs:
        values.append([])
        for slots, k in columns:
            rows = [ins[s][...] for s in slots]
            rows = jnp.concatenate(rows, axis=1) if len(rows) > 1 else rows[0]
            values[-1].append(mm(rows, ins[k][...], TN).astype(BF))
    if not cut:
        at = 0
        for value in values[0]:
            outs[0][:, at : at + value.shape[1]] = value
            at += value.shape[1]
        return
    *outs, buffer, sems = outs
    height = outs[0].shape[0]
    own = height // len(runs)
    slots = ROWS // own

    def copies(block):
        at = 0
        for k in range(slots):
            t = block * slots + k
            for ref in outs[t : t + 1] if t < cut else outs[t : t + 2] if t == cut else outs[t + 1 : t + 2]:
                rows = buffer.at[block % 2, pl.ds(at, ref.shape[0])]
                yield pltpu.make_async_copy(rows, ref, sems.at[block % 2, at // (height // 2)])
                at += ref.shape[0]

    for block in range(steps):

        @pl.when(pl.program_id(0) == block)
        def _():
            if block >= 2:
                for copy in copies(block - 2):
                    copy.wait()
            for k in range(slots):
                for r, columns in enumerate(values):
                    at = 0
                    first = (k * len(runs) + r) * own
                    for value in columns:
                        cols = slice(at, at + value.shape[1])
                        buffer[block % 2, first : first + own, cols] = value[k * own : (k + 1) * own]
                        at += value.shape[1]
            for copy in copies(block):
                copy.start()
            if block == steps - 1:
                for last in range(max(0, steps - 2), steps):
                    for copy in copies(last):
                        copy.wait()


def weight_grads(places, runs, cut):
    count = places.shape[0] - 1
    tokens, width = runs[0][0][0].shape
    own = width // count
    steps = width // ROWS
    slots = ROWS // own if cut else 1
    ins, specs, marks = [], [], []
    for columns in runs:
        for left, _ in columns:
            mark = []
            for k in range(slots):
                place = (lambda i, p, k=k: (0, p[i * slots + k])) if cut else (lambda i, p: (0, i))
                ins.append(left)
                specs.append(pl.BlockSpec((tokens, ROWS // slots), place))
                mark.append(len(ins) - 1)
            marks.append(tuple(mark))
    pairs = []
    for columns in runs:
        pairs.append([])
        for _, right in columns:
            ins.append(right)
            specs.append(whole(right.shape))
            pairs[-1].append((marks.pop(0), len(ins) - 1))
    total = sum(right.shape[1] for _, right in runs[0])
    if cut:
        height = own * len(runs)
        heights = [height] * cut + [height // 2] * 2 + [height] * (count - cut - 1)
        outs = [out_of((h, total)) for h in heights]
        out_specs = [HBM] * len(outs)
        scratch = [
            pltpu.VMEM((2, slots * height, total), BF),
            pltpu.SemaphoreType.DMA((2, 2 * slots)),
        ]
    else:
        outs, out_specs, scratch = [out_of((width, total))], [rows_of(ROWS, total)], []
    return kernel_call(
        functools.partial(grads_body, pairs, cut, steps),
        (steps,),
        ins,
        specs,
        outs,
        out_specs,
        2 * tokens * width * total,
        scratch,
        places,
    )


def norm_back(grad_hidden, value, gain):
    normed, scale = norm(value)
    scaled = grad_hidden * gain
    back = scale * (scaled - normed * jnp.mean(scaled * normed, axis=-1, keepdims=True))
    return back, jnp.sum(grad_hidden * normed, axis=0, keepdims=True)


def add_up(ref, value):
    @pl.when(pl.program_id(0) == 0)
    def _():
        ref[...] = jnp.zeros_like(ref)

    ref[...] += value


def middle_body(halves, _, x_ref, att0, att1, g_ref, dh0, dh1, gain_ref, dm_ref, dgain_ref):
    value = x_ref[...].astype(F32) + halves.pick((att0, att1)).astype(F32)
    back, d_gain = norm_back(halves.pick((dh0, dh1)).astype(F32), value, gain_ref[...])
    dm_ref[...] = (g_ref[...].astype(F32) + back).astype(BF)
    add_up(dgain_ref, d_gain)


def middle_back(places, x, att, g, dh, gain):
    tokens, width = x.shape
    halves = Halves(tokens)
    part, pair = halves.both(width), halves.pair(width)
    return kernel_call(
        functools.partial(middle_body, halves),
        halves.grid,
        (x, *att, g, *dh, gain),
        [part, *pair, part, *pair, whole(gain.shape)],
        [out_of((tokens, width)), out_of((1, width), F32)],
        [part, whole((1, width))],
        0,
        (),
        places,
    )


def attend_back_body(pieces, shared, halves, steps, hw, places, x0, x1, dm0, dm1, qkv0, qkv1, *refs):
    sides = [
        [r for a in p.arrays for r, b in zip(refs, shared.arrays) if a is b] for p in pieces
    ]
    parts = refs[-6 - 2 * halves.count : -6]
    dqkv0, dqkv1 = refs[-8 - 2 * halves.count : -6 - 2 * halves.count]
    dgain, w0, sems0, w1, sems1, d_hidden = refs[-6:]
    for p, s, w, sems in zip(pieces, sides, (w0, w1), (sems0, sems1)):
        p.start(s, places, w, sems, range(1))
    normed = [norm(x[...].astype(F32))[0] for x in (x0, x1)]
    for p, s, w, sems in zip(pieces, sides, (w0, w1), (sems0, sems1)):
        p.wait(s, places, w, sems, 0)
    scale = HDIM ** (-0.5)
    low_scale = jnp.asarray(scale, BF)
    hidden = [hidden_keys(2 * SUB, (1 + c) * SUB, steps, True) for c in range(2)]
    d_mixed = [mm(d[...], w[:, 3 * hw :]).astype(BF) for d, w in ((dm0, w0), (dm1, w1))]
    for s in range(dm0.shape[0] // SUB):
        rows = slice(s * SUB, (s + 1) * SUB)
        for j in range(hw // PAIR):
            cols = [slice(t * hw + j * PAIR, t * hw + (j + 1) * PAIR) for t in range(3)]
            q0, k0, v0 = (qkv0[rows, c] for c in cols)
            q1, k1, v1 = (qkv1[rows, c] for c in cols)
            keys = (k0, jnp.concatenate([k0, k1], axis=0))
            values = (v0, jnp.concatenate([v0, v1], axis=0))
            d_k, d_v = [], []
            for c, (q, out_ref) in enumerate(((q0, dqkv0), (q1, dqkv1))):
                q_two = stack_heads(q) * low_scale
                d_two = stack_heads(d_mixed[c][rows, cols[0]])
                soft = softmax_turned(q_two, keys[c], hidden[c])
                d_probs = mm(values[c], d_two, NT)
                inside = jnp.sum(soft * d_probs, axis=0, keepdims=True)
                d_scores = (soft * (d_probs - inside)).astype(BF)
                d_q = pick_heads(mm(d_scores, keys[c], TN)) * scale
                out_ref[rows, cols[0]] = d_q.astype(BF)
                d_k.append(mm(d_scores, q_two))
                d_v.append(mm(soft.astype(BF), d_two))
            dqkv0[rows, cols[1]] = (d_k[0] + d_k[1][:SUB]).astype(BF)
            dqkv1[rows, cols[1]] = d_k[1][SUB:].astype(BF)
            dqkv0[rows, cols[2]] = (d_v[0] + d_v[1][:SUB]).astype(BF)
            dqkv1[rows, cols[2]] = d_v[1][SUB:].astype(BF)
    gains = []
    for c, (d, w) in enumerate(((dqkv0, w0), (dqkv1, w1))):
        grad = mm(d[...], w[:, : 3 * hw], NT)
        gains.append(jnp.sum(grad * normed[c], axis=0, keepdims=True))
        d_hidden[c] = grad.astype(BF)

    for k, ref in enumerate(parts):

        @pl.when(pl.program_id(0) == k)
        def _():
            ref[...] = d_hidden[...]

    add_up(dgain, jnp.concatenate(gains, axis=0))


def attend_back(places, x, dm, qkv, w, steps):
    tokens, width = dm[0].shape
    halves = Halves(tokens)
    pieces = [Pieces(*side, 1) for side in w]
    shared = Pieces(w[0][0] + w[1][0], w[0][1], 1)
    hw = pieces[0].shape[1] // 4
    flat, thin = halves.both(width), halves.both(3 * hw)
    part = (2, ROWS, width)
    d0, d1, *parts, d_gain = kernel_call(
        functools.partial(attend_back_body, pieces, shared, halves, steps, hw),
        halves.grid,
        [*x, *dm, *qkv, *shared.arrays],
        [flat] * 4 + [thin] * 2 + [HBM] * shared.count,
        [out_of((tokens, 3 * hw))] * 2 + [out_of(part)] * (2 * halves.count) + [out_of((2, width), F32)],
        [thin] * 2 + [whole(part)] * (2 * halves.count) + [whole((2, width))],
        8 * tokens * width * 4 * hw,
        pieces[0].scratch + pieces[1].scratch + [pltpu.VMEM(part, BF)],
        places,
    )
    parts = [part.reshape(-1, width) for part in parts]
    return (d0, d1), list(zip(parts[halves.count :], parts)), d_gain


def store_frames(out_ref, sums):
    frames, _, width = out_ref.shape
    both = [p.reshape(frames, 1, p.shape[0] // frames, width) for p in sums]
    out_ref[...] = jnp.concatenate(both, axis=1).reshape(frames, -1, width).astype(BF)


def output_body(halves, _, x0, x1, *refs):
    *refs, out_ref = refs
    pairs = [halves.pick(refs[k : k + 2]).astype(F32) for k in range(0, 8, 2)]
    sums = [x[...].astype(F32) + pairs[2 * c] + pairs[2 * c + 1] for c, x in enumerate((x0, x1))]
    store_frames(out_ref, sums)


def output_of(places, x, att, mlp, shape):
    frames, steps, width = shape
    halves = Halves(x[0].shape[0])
    sides = [a for c in range(2) for pair in (att[c], mlp[c]) for a in pair]
    cube = pl.BlockSpec((2 * ROWS // steps, steps, width), lambda i, p: (halves.block(i, p), 0, 0))
    return kernel_call(
        functools.partial(output_body, halves),
        halves.grid,
        [*x, *sides],
        [halves.both(width)] * 2 + halves.pair(width) * 4,
        [out_of(shape)],
        [cube],
        0,
        (),
        places,
    )[0]


def input_body(_, x0, x1, dm0, dm1, mine, other, gain_ref, *refs):
    sums = []
    dh = jnp.where(pl.program_id(0) == 0, other[...], mine[...]).astype(F32)
    for c, (x, dm) in enumerate(((x0, dm0), (x1, dm1))):
        rows = slice(c * ROWS, (c + 1) * ROWS)
        back, _ = norm_back(dh[rows], x[...].astype(F32), gain_ref[c : c + 1])
        sums.append(dm[...].astype(F32) + back)
    store_frames(refs[-1], sums)


def input_back(places, x, dm, dh, gain, part, before, shape):
    frames, steps, width = shape
    halves = Halves(x[0].shape[0])
    block = lambda i, p: halves.block(i * halves.count, p) + part
    flat = pl.BlockSpec((ROWS, width), lambda i, p: (block(i, p), 0))
    cube = pl.BlockSpec((2 * ROWS // steps, steps, width), lambda i, p: (block(i, p), 0, 0))
    ins = [*x, *dm, *dh, gain]
    specs = [flat] * 4 + [whole(d.shape) for d in dh] + [whole(gain.shape)]
    alias = {}
    if before is not None:
        ins.append(before)
        specs.append(HBM)
        alias = {len(ins): 0}
    return kernel_call(input_body, (2,), ins, specs, [out_of(shape)], [cube], 0, (), places, alias)[0]


def finish_body(layout, turned, *refs):
    count = 1 + max(k for terms, _ in layout for k in terms)
    ins, outs = refs[:count], refs[count:]
    own, wide = outs[0].shape[1:]
    for c, (terms, first) in enumerate(layout):
        rows = slice(first, first + own)
        for t, ref in enumerate(outs):
            cols = slice(t * wide, (t + 1) * wide)
            total = ins[terms[0]][rows, cols].astype(F32)
            for k in terms[1:]:
                total = total + ins[k][rows, cols].astype(F32)
            ref[c] = total.T if t == turned else total


def finish(sides, kinds, own):
    arrays, layout = [], []
    for terms, first in sides:
        spots = []
        for term in terms:
            found = [k for k, a in enumerate(arrays) if a is term]
            if not found:
                arrays.append(term)
            spots.append(found[0] if found else len(arrays) - 1)
        layout.append((spots, first))
    wide = arrays[0].shape[1] // kinds
    shapes = [(len(sides), own, wide)] * (kinds - 1) + [(len(sides), wide, own)]
    return kernel_call(
        functools.partial(finish_body, layout, kinds - 1),
        (1,),
        arrays,
        [whole(a.shape) for a in arrays],
        [out_of(s, F32) for s in shapes],
        [whole(s) for s in shapes],
        0,
    )


class Ring:
    def __init__(self, size):
        self.size = size
        self.rings = size <= 16
        half = size // 2
        order = [2 * q for q in range(half)] + [2 * (size - 1 - q) + 1 for q in range(half, size)]
        self.ahead = [(order[q], order[(q + 1) % size]) for q in range(size)]
        self.behind = [(b, a) for a, b in self.ahead]
        self.me = lax.axis_index("dp")
        place = jnp.where(self.me % 2 == 0, self.me // 2, size - 1 - self.me // 2)
        q = lax.rem(place + jnp.arange(size, dtype=jnp.int32), size)
        self.order = jnp.where(q < half, 2 * q, 2 * (size - 1 - q) + 1).astype(jnp.int32)


class Rounds:
    def __init__(self):
        self.done = ()

    def now(self, value):
        return lax.optimization_barrier((value, *self.done))[0] if self.done else value

    def close(self, *arrays):
        self.done = arrays


class Gather:
    def __init__(self, rounds, ring, shard):
        self.rounds, self.ring = rounds, ring
        self.a, self.b = [shard], [shard]

    def step(self):
        a, b = self.a[-1], self.b[-1]
        if len(self.a) == self.ring.size // 2:
            half = a.shape[0] // 2
            a, b = a[:half], b[half:]
        self.a.append(lax.ppermute(self.rounds.now(a), "dp", self.ring.ahead))
        self.b.append(lax.ppermute(self.rounds.now(b), "dp", self.ring.behind))
        return self.a[-1], self.b[-1]

    def entries(self, part=0, parts=1):
        n = self.ring.size
        own = self.a[0].shape[0] // parts
        found = []
        for t in range(n):
            if t != n // 2:
                found.append((self.b[t] if t < n // 2 else self.a[n - t], t, 0, part * own, own))
            elif parts == 1:
                found.append((self.a[t], t, 0, 0, own // 2))
                found.append((self.b[t], t, own // 2, 0, own // 2))
            else:
                found.append(((self.a[t], self.b[t])[part], t, 0, 0, own))
        return found, own


class Scatter:
    def __init__(self, rounds, ring, blocks):
        self.rounds, self.ring = rounds, ring
        far = ring.size // 2
        self.a, self.b = blocks[far], blocks[far + 1]
        self.blocks = [*blocks[:far], None, *blocks[far + 2 :]]
        self.k = far

    def step(self):
        n = self.ring.size
        if self.k < n // 2:
            one, two = self.blocks[self.k].astype(F32), self.blocks[n - self.k].astype(F32)
            a, b = self.a.astype(F32), self.b.astype(F32)
            if self.k == n // 2 - 1:
                half = a.shape[0]
                a = jnp.pad(a, ((0, half), (0, 0)))
                b = jnp.pad(b, ((half, 0), (0, 0)))
            self.a, self.b = (one + a).astype(BF), (two + b).astype(BF)
        self.k -= 1
        self.a = lax.ppermute(self.rounds.now(self.a), "dp", self.ring.ahead)
        self.b = lax.ppermute(self.rounds.now(self.b), "dp", self.ring.behind)
        return self.a, self.b

    def terms(self):
        return [self.blocks[0], self.a, self.b]


class HeadSum:
    def __init__(self, rounds, pair):
        size = lax.axis_size("mp")
        self.rounds, self.pair, self.got = rounds, pair, []
        self.near_moves = [(i, i ^ 1) for i in range(size)]
        self.far_moves = [(i, i ^ 2) for i in range(size)]

    def add(self, one, two):
        return (one.astype(F32) + two.astype(F32)).astype(BF)

    def near(self):
        got = lax.ppermute(self.rounds.now(self.pair[1]), "mp", self.near_moves)
        self.mine = self.add(self.pair[0], got)
        return self.mine

    def far(self, part=1.0):
        start = sum(got.shape[0] for got in self.got)
        rows = int(self.mine.shape[0] * part)
        moved = self.rounds.now(self.mine[start : start + rows])
        self.got.append(lax.ppermute(moved, "mp", self.far_moves))
        return self.got[-1]

    def last(self):
        got = [self.rounds.now(got) for got in self.got]
        self.mine = self.add(self.mine, jnp.concatenate(got, 0))
        self.sum = (self.mine, lax.ppermute(self.mine, "mp", self.near_moves))
        return self.sum[1]


def exchange_steps(axes):
    for axis in axes:
        size, step = lax.axis_size(axis), 1
        while step < size:
            yield axis, [(i, i ^ step) for i in range(size)], step
            step *= 2


def on_device(
    layer_input, frame_mask, gain_attn, w_query, w_key, w_value, w_out, gain_ffn, w_gate, w_up,
    w_down, cotangent,
):
    sets, width = gain_attn.shape[0], layer_input.shape[2]
    shape = layer_input.shape
    each = shape[1] // sets
    ring = Ring(lax.axis_size("dp"))
    rings, n = ring.rings, ring.size
    far = n // 2 if rings else 0
    own = width // n
    places = jnp.concatenate([ring.order, (lax.axis_index("mp") % 2).astype(jnp.int32)[None]])
    gather = lambda value: lax.all_gather(value, "dp", tiled=True)
    scatter = lambda value: lax.psum_scatter(value, "dp", scatter_dimension=0, tiled=True)
    rounds = Rounds()
    now, close = rounds.now, rounds.close

    attn_own = pack_attn(w_query, w_key, w_value, w_out)
    small = jnp.concatenate([gain_attn, gain_ffn], 0).astype(F32)[None]
    steps = list(exchange_steps(("dp",)))
    ffn_own, x, g = [], [], []

    def gain_step(value):
        axis, moves, step = steps.pop(0)
        other = lax.ppermute(now(value), axis, moves)
        bit = (ring.me // step) % 2
        both = [jnp.concatenate(pair, 0) for pair in ((value, other), (other, value))]
        return jnp.where(bit == 0, *both)

    masks = frame_mask.astype(BF)[:, None, None]
    chores = [
        lambda: ffn_own.append(pack_ffn(now(w_gate), w_up, w_down, 0)),
        lambda: x.append(split_sets(now(layer_input), sets)[0]),
        lambda: ffn_own.append(pack_ffn(now(w_gate), w_up, w_down, 1)),
        lambda: x.append(split_sets(now(layer_input), sets)[1]),
        lambda: g.append(split_sets(now(cotangent) * masks, sets)[0]),
        lambda: g.append(split_sets(now(cotangent) * masks, sets)[1]),
    ]
    attn = Gather(rounds, ring, attn_own)
    for k in range(max(far, 3)):
        moved = attn.step() if rings else ()
        if rings and k == far - 1:
            rows = [Gather(rounds, ring, shard) for shard in ffn_own]
            moved += rows[0].step()
        for chore in chores[:2]:
            chore()
        del chores[:2]
        if steps:
            small = gain_step(small)
        close(small, *moved, *[v[-1] for v in (ffn_own, x, g) if v])
    while steps:
        small = gain_step(small)
    gains = small.transpose(1, 0, 2).reshape(2 * sets, width)
    g_attn, g_ffn = [[gains[k * sets + c][None] for c in range(sets)] for k in range(2)]
    if rings:
        w_attn = [attn.entries(c, sets) for c in range(sets)]
    else:
        both = gather(attn_own).reshape(n, sets, own, -1)
        w_attn = [([(both[:, c].reshape(width, -1), None, 0, 0, width)], width) for c in range(sets)]

    def move(c):
        return rows[c].step() if rings else ()

    def weights(c):
        if rings:
            return rows[c].entries()
        return [(gather(ffn_own[c]), None, 0, 0, width)], width

    h1, qkv, mixed, heads = [None] * 2, [None] * 2, [None] * 2, [None] * 2
    moved = move(0)
    h1[0], qkv[0], mixed[0], part = attend(now(places), x[0], g_attn[0], None, w_attn[0], each)
    heads[0] = HeadSum(rounds, part)
    close(*moved, part[0])
    close(heads[0].near())
    moved = move(0)
    got = heads[0].far()
    h1[1], qkv[1], mixed[1], part = attend(now(places), x[1], g_attn[1], qkv[0], w_attn[1], each)
    heads[1] = HeadSum(rounds, part)
    held, rounds.done = rounds.done, (*rounds.done, part[0])
    moved += move(0)
    rounds.done = held
    close(*moved, part[0], got)
    close(heads[1].near(), heads[0].last())

    def grads_of(c, out):
        columns = [(out[0], out[2]), (g[c], out[1])]
        return weight_grads(now(places), [columns], far)

    dh, mlp, grads, dm, d_gain_ffn = ([None] * 2 for _ in range(5))
    moved = move(1)
    got = heads[1].far()
    out = hidden_units(now(places), x[0], heads[0].sum, g[0], g_ffn[0], weights(0))
    dh[0], mlp[0] = HeadSum(rounds, out[3]), HeadSum(rounds, out[4])
    close(*moved, out[0], got)
    moved = move(1)
    grads[0] = grads_of(0, out)
    close(*moved, grads[0][0], dh[0].near(), mlp[0].near(), heads[1].last())
    att = [head.sum for head in heads]
    sums = [Scatter(rounds, ring, grads[0])] if rings else []
    add = lambda k: sums[k].step() if rings else ()
    close(*move(1), mlp[0].far(0.5))
    close(*move(1), *add(0), mlp[0].far(0.5))

    moved = add(0)
    got = dh[0].far()
    out = hidden_units(now(places), x[1], att[1], g[1], g_ffn[1], weights(1))
    dh[1], mlp[1] = HeadSum(rounds, out[3]), HeadSum(rounds, out[4])
    close(*moved, out[0], got)
    close(dh[1].near(), dh[0].last(), mlp[0].last(), mlp[1].near())
    moved = add(0)
    got = dh[1].far()
    grads[1] = grads_of(1, out)
    if rings:
        sums.append(Scatter(rounds, ring, grads[1]))
        moved += add(1)
    dm[0], d_gain_ffn[0] = middle_back(now(places), x[0], att[0], g[0], dh[0].sum, g_ffn[0])
    close(*moved, grads[1][0], dm[0], got)

    close(dh[1].last())

    moved = (*add(0), *add(1))
    got = mlp[1].far()
    dm[1], d_gain_ffn[1] = middle_back(now(places), x[1], att[1], g[1], dh[1].sum, g_ffn[1])
    d_qkv, part, d_gain_attn = attend_back(now(places), x, dm, qkv, w_attn, each)
    back = [HeadSum(rounds, p) for p in part]
    close(*moved, part[0][0], got)

    shared = lax.axis_size("mp")
    d_gains = jnp.concatenate([d_gain_attn, *[d / shared for d in d_gain_ffn]], 0)
    steps = list(exchange_steps(("mp", "dp")))

    def sum_step(value, *earlier):
        axis, moves, _ = steps.pop(0)
        got = lax.ppermute(now(value), axis, moves)
        return value + lax.optimization_barrier((got, *earlier))[0]

    moved = add(1)
    mlp[1].last()
    d_gains = sum_step(sum_step(d_gains))
    runs = [[(h1[c], d_qkv[c]), (dm[c], mixed[c])] for c in range(sets)]
    if rings:
        blocks = weight_grads(now(places), runs, far)
        sums.append(Scatter(rounds, ring, blocks))
    else:
        blocks = [weight_grads(now(places), [run], far)[0] for run in runs]
    close(*moved, blocks[0], *[b.near() for b in back], d_gains)
    moved = (*add(2), *add(1))
    got = back[0].far()
    output = output_of(now(places), x, att, [m.sum for m in mlp], shape)
    close(*moved, got, output)
    moved = add(2)
    d_gains = sum_step(d_gains)
    got = back[1].far(0.5)
    if rings:
        ffn_sums = [([now(t) for t in s.terms()], 0) for s in sums[:2]]
    else:
        ffn_sums = [([scatter(b[0])], 0) for b in grads]
    d_gate_w, d_up_w, d_down_w = finish(ffn_sums, 3, own)
    close(*moved, d_gains, d_gate_w, got, back[0].last())
    moved = add(2)
    d_gains = sum_step(d_gains)
    got = back[1].far(0.5)
    grad_input = input_back(now(places), x, dm, back[0].sum, gains[:sets], 0, None, shape)
    close(*moved, grad_input, d_gains, got)
    moved = add(2)
    back[1].last()
    grad_input = input_back(now(places), x, dm, back[1].sum, gains[:sets], 1, grad_input, shape)
    while steps:
        d_gains = sum_step(d_gains, grad_input)
    close(*moved, grad_input, d_gains)
    if rings:
        terms = [now(t) for t in sums[2].terms()]
        attn_sums = [(terms, c * own) for c in range(sets)]
    else:
        attn_sums = [([scatter(b)], 0) for b in blocks]
    d_query, d_key, d_value, d_out = finish(attn_sums, 4, own)
    d_gains = lax.dynamic_slice_in_dim(d_gains, ring.me * own, own, 1)
    return (
        output, grad_input, d_gains[:sets], d_query, d_key, d_value, d_out,
        d_gains[sets:], d_gate_w, d_up_w, d_down_w,
    )


def solution(mesh):
    rows = P("dp", None, None)
    gain = P(None, "dp")
    into = P(None, "dp", "mp")
    back = P(None, "mp", "dp")
    weights = (gain, into, into, into, back, gain, into, into, back)
    return jax.shard_map(
        on_device,
        mesh=mesh,
        in_specs=(rows, P("dp"), *weights, rows),
        out_specs=(rows, rows, *weights),
        check_vma=False,
    )
```

```python
import functools

import jax
import jax.numpy as jnp
from jax import lax
from jax.experimental import pallas as pl
from jax.experimental.pallas import tpu as pltpu
from jax.sharding import PartitionSpec as P

HDIM = 64
EPS = 1e-05
NEG = -1e30
BF = jnp.bfloat16
F32 = jnp.float32
NN = (((1,), (0,)), ((), ()))
NT = (((1,), (1,)), ((), ()))
TN = (((0,), (0,)), ((), ()))
MIB = 1024 * 1024
SUB = 128
PAIR = 2 * HDIM
ROWS = 256
HBM = pl.BlockSpec(memory_space=pl.ANY)


def mm(left, right, dims=NN):
    return lax.dot_general(left, right, dims, preferred_element_type=F32)


def kernel_call(body, grid, ins, in_specs, outs, out_specs, flops, scratch=(), scalars=None, alias=None):
    moved = sum(a.size * a.dtype.itemsize for a in ins) + sum(
        o.size * jnp.dtype(o.dtype).itemsize for o in outs
    )
    spec = pltpu.PrefetchScalarGridSpec(
        num_scalar_prefetch=0 if scalars is None else 1,
        grid=grid,
        in_specs=in_specs,
        out_specs=out_specs,
        scratch_shapes=scratch,
    )
    args = ins if scalars is None else (scalars, *ins)
    return pl.pallas_call(
        body,
        grid_spec=spec,
        out_shape=outs,
        input_output_aliases=alias or {},
        compiler_params=pltpu.CompilerParams(vmem_limit_bytes=56 * MIB),
        cost_estimate=pl.CostEstimate(flops=1, bytes_accessed=1, transcendentals=0),
    )(*args)


def whole(shape):
    return pl.BlockSpec(shape, lambda *i: (0,) * len(shape))


def rows_of(rows, width, start=0):
    return pl.BlockSpec((rows, width), lambda i, *_: (i + start, 0))


def out_of(shape, kind=BF):
    return jax.ShapeDtypeStruct(shape, kind)


class Halves:
    def __init__(self, tokens):
        self.count = tokens // 2 // ROWS
        self.grid = (2 * self.count,)

    def block(self, i, places):
        half = (1 - i // self.count + places[places.shape[0] - 1]) % 2
        return half * self.count + i % self.count

    def both(self, width):
        return pl.BlockSpec((ROWS, width), lambda i, p: (self.block(i, p), 0))

    def pair(self, width):
        return [
            pl.BlockSpec((ROWS, width), lambda i, p: (jnp.maximum(i - self.count, 0), 0)),
            pl.BlockSpec((ROWS, width), lambda i, p: (jnp.minimum(i, self.count - 1), 0)),
        ]

    def pick(self, pair):
        return jnp.where(pl.program_id(0) < self.count, pair[1][...], pair[0][...])

    def one(self, width, half):
        shift = 0 if half else self.count
        return pl.BlockSpec((ROWS, width), lambda i, p: (self.block(i + shift, p), 0))

    def put(self, pair, value):
        pair[0][...] = value

        @pl.when(pl.program_id(0) < self.count)
        def _():
            pair[1][...] = pair[0][...]


def split_sets(value, sets):
    frames, steps, width = value.shape
    parts = value.reshape(frames, sets, steps // sets, width)
    return [parts[:, c].reshape(-1, width) for c in range(sets)]


def pack_attn_body(wq, wk, wv, wo, out):
    own, hw = wq.shape[1:]
    for c in range(2):
        rows = slice(c * own, (c + 1) * own)
        for t, w in enumerate((wq, wk, wv)):
            out[rows, t * hw : (t + 1) * hw] = w[c]
        out[rows, 3 * hw :] = wo[c].T


def pack_attn(wq, wk, wv, wo):
    sets, own, hw = wq.shape
    piece = (sets * own, 4 * hw)
    return kernel_call(
        pack_attn_body,
        (1,),
        (wq, wk, wv, wo),
        [whole(w.shape) for w in (wq, wk, wv, wo)],
        [out_of(piece)],
        [whole(piece)],
        0,
    )[0]


def pack_ffn_body(wg, wu, wd, out):
    units = wg.shape[2]
    out[:, :units] = wg[0]
    out[:, units : 2 * units] = wu[0]
    out[:, 2 * units :] = wd[0].T


def pack_ffn(wg, wu, wd, c):
    own, units = wg.shape[1:]
    piece = (own, 3 * units)
    into = pl.BlockSpec((1, own, units), lambda i: (c, 0, 0))
    back = pl.BlockSpec((1, units, own), lambda i: (c, 0, 0))
    return kernel_call(
        pack_ffn_body,
        (1,),
        (wg, wu, wd),
        [into, into, back],
        [out_of(piece)],
        [whole(piece)],
        0,
    )[0]


def norm(value):
    scale = lax.rsqrt(jnp.mean(value * value, axis=-1, keepdims=True) + EPS)
    return value * scale, scale


def lanes_low(shape):
    return lax.broadcasted_iota(jnp.int32, shape, 1) < HDIM


def stack_heads(pair):
    low = lanes_low(pair.shape)
    zero = jnp.zeros_like(pair)
    return jnp.concatenate([jnp.where(low, pair, zero), jnp.where(low, zero, pair)], axis=0)


def pick_heads(stacked):
    half = stacked.shape[0] // 2
    low = lanes_low((half, stacked.shape[1]))
    return jnp.where(low, stacked[:half], stacked[half:])


def hidden_keys(rows, keys, steps, turned=False):
    shape, axis = ((keys, rows), 1) if turned else ((rows, keys), 0)
    row = lax.broadcasted_iota(jnp.int32, shape, axis) & (SUB - 1)
    spot = lax.broadcasted_iota(jnp.int32, shape, 1 - axis)
    key = spot & (SUB - 1)
    shift = steps.bit_length() - 1
    seen = lax.shift_right_logical(row, shift) == lax.shift_right_logical(key, shift)
    own = spot >= keys - SUB
    seen = seen & ((row >= key) | jnp.logical_not(own))
    return jnp.where(seen, 0.0, NEG)


def softmax(query, keys, hidden):
    raw = mm(query, keys, NT) + hidden
    power = jnp.exp(raw - jnp.max(raw, axis=-1, keepdims=True))
    return power * (1.0 / jnp.sum(power, axis=-1, keepdims=True))


def softmax_turned(query, keys, hidden):
    raw = mm(keys, query, NT) + hidden
    power = jnp.exp(raw - jnp.max(raw, axis=0, keepdims=True))
    return power * (1.0 / jnp.sum(power, axis=0, keepdims=True))


class Pieces:
    def __init__(self, entries, own, groups):
        self.entries = entries
        self.own = own
        self.groups = groups
        self.arrays = []
        for array, *_ in entries:
            if not any(array is a for a in self.arrays):
                self.arrays.append(array)
        self.count = len(self.arrays)
        self.shape = (sum(e[4] for e in entries), entries[0][0].shape[1])
        self.scratch = [pltpu.VMEM(self.shape, BF), pltpu.SemaphoreType.DMA((groups, len(entries)))]

    def copies(self, refs, places, memory, sems, group):
        wide = self.shape[1] // self.groups
        cols = pl.ds(group * wide, wide)
        for k, (array, slot, row, first, rows) in enumerate(self.entries):
            ref = [r for r, a in zip(refs, self.arrays) if a is array][0]
            start = row if slot is None else pl.multiple_of(places[slot] * self.own + row, rows)
            source = ref.at[pl.ds(first, rows), cols]
            yield pltpu.make_async_copy(source, memory.at[pl.ds(start, rows), cols], sems.at[group, k])

    def start(self, refs, places, memory, sems, order):
        @pl.when(pl.program_id(0) == 0)
        def _():
            for group in order:
                for copy in self.copies(refs, places, memory, sems, group):
                    copy.start()

    def wait(self, refs, places, memory, sems, group):
        @pl.when(pl.program_id(0) == 0)
        def _():
            for copy in self.copies(refs, places, memory, sems, group):
                copy.wait()


def attend_body(pieces, halves, steps, hw, later, filled, places, *refs):
    x_ref, gain_ref, *refs = refs
    if later:
        before_ref, *refs = refs
    w_refs, refs = refs[: pieces.count], refs[pieces.count :]
    h_ref, qkv_ref, mixed_ref, *part_refs, w_ref, sems = refs[filled:]
    pieces.start(w_refs, places, w_ref, sems, range(1))
    normed, _ = norm(x_ref[...].astype(F32))
    hidden = (normed * gain_ref[...]).astype(BF)
    h_ref[...] = hidden
    pieces.wait(w_refs, places, w_ref, sems, 0)
    qkv = mm(hidden, w_ref[:, : 3 * hw]).astype(BF)
    qkv_ref[...] = qkv
    scale = jnp.asarray(HDIM ** (-0.5), BF)
    hidden_scores = hidden_keys(2 * SUB, 2 * SUB if later else SUB, steps)
    for s in range(x_ref.shape[0] // SUB):
        rows = slice(s * SUB, (s + 1) * SUB)
        for j in range(hw // PAIR):
            q, k, v = (qkv[rows, t * hw + j * PAIR : t * hw + (j + 1) * PAIR] for t in range(3))
            if later:
                k_old, v_old = (
                    before_ref[rows, t * hw + j * PAIR : t * hw + (j + 1) * PAIR] for t in (1, 2)
                )
                k = jnp.concatenate([k_old, k], axis=0)
                v = jnp.concatenate([v_old, v], axis=0)
            probs = softmax(stack_heads(q) * scale, k, hidden_scores).astype(BF)
            mixed_ref[rows, j * PAIR : (j + 1) * PAIR] = pick_heads(mm(probs, v)).astype(BF)
    part = mm(mixed_ref[...], w_ref[:, 3 * hw :], NT).astype(BF)
    if len(part_refs) == 2:
        halves.put(part_refs, part)
    else:
        part_refs[0][...] = part


def attend(places, x, gain, before, w, steps, half=None, filled=()):
    tokens, width = x.shape
    pieces, halves = Pieces(*w, 1), Halves(tokens)
    hw = pieces.shape[1] // 4
    spec = halves.both if half is None else functools.partial(halves.one, half=half)
    ins = [x, gain]
    specs = [spec(width), whole(gain.shape)]
    if before is not None:
        ins.append(before)
        specs.append(spec(3 * hw))
    ins += [*pieces.arrays, *filled]
    specs += [HBM] * (pieces.count + len(filled))
    widths = (width, 3 * hw, hw)
    *out, part = kernel_call(
        functools.partial(attend_body, pieces, halves, steps, hw, before is not None, len(filled)),
        halves.grid if half is None else (halves.count,),
        ins,
        specs,
        [out_of((tokens, n)) for n in widths] + [out_of((tokens // 2, width))] * (2 if half is None else 1),
        [spec(n) for n in widths] + (halves.pair(width) if half is None else [rows_of(ROWS, width)]),
        2 * tokens * width * 4 * hw,
        pieces.scratch,
        places,
        {len(ins) - len(filled) + 1 + k: k for k in range(len(filled))},
    )
    if half is None:
        return *out[:3], (out[3], part)
    return *out, part


def units_body(pieces, halves, units, half, filled, places, x_ref, *refs):
    if half is None:
        att0, att1, *refs = refs
        att = halves.pick((att0, att1))
    else:
        att_ref, *refs = refs
        att = att_ref[...]
    g_ref, gain_ref, *refs = refs
    w_refs, refs = refs[: pieces.count], refs[pieces.count + filled :]
    h_ref, inner_ref, dboth_ref, *sum_refs, w_ref, sems = refs
    pieces.start(w_refs, places, w_ref, sems, (2, 0, 1))
    normed, _ = norm(x_ref[...].astype(F32) + att.astype(F32))
    hidden = (normed * gain_ref[...]).astype(BF)
    h_ref[...] = hidden
    cut = 256
    cols = [
        [slice(t * units + u * cut, t * units + (u + 1) * cut) for t in range(3)] for u in range(units // cut)
    ]
    pieces.wait(w_refs, places, w_ref, sems, 2)
    d_inners = [mm(g_ref[...], w_ref[:, c[2]]) for c in cols]
    pieces.wait(w_refs, places, w_ref, sems, 0)
    pieces.wait(w_refs, places, w_ref, sems, 1)
    for c, d_inner in zip(cols, d_inners):
        gate = mm(hidden, w_ref[:, c[0]])
        up = mm(hidden, w_ref[:, c[1]])
        sigma = 1.0 / (1.0 + jnp.exp(-gate))
        active = gate * sigma
        inner_ref[:, c[0]] = (active * up).astype(BF)
        dboth_ref[:, c[1]] = (d_inner * active).astype(BF)
        dboth_ref[:, c[0]] = (d_inner * up * (sigma + active * (1.0 - sigma))).astype(BF)
    d_hidden = mm(dboth_ref[...], w_ref[:, : 2 * units], NT).astype(BF)
    if half is None:
        halves.put(sum_refs[:2], d_hidden)
        halves.put(sum_refs[2:], mm(inner_ref[...], w_ref[:, 2 * units :], NT).astype(BF))
    else:
        sum_refs[0][...] = d_hidden
        sum_refs[1][...] = mm(inner_ref[...], w_ref[:, 2 * units :], NT).astype(BF)


def hidden_units(places, x, att, g, gain, w, half=None, filled=()):
    tokens, width = x.shape
    pieces, halves = Pieces(*w, 3), Halves(tokens)
    units = pieces.shape[1] // 3
    spec = halves.both if half is None else functools.partial(halves.one, half=half)
    part = spec(width)
    widths = (width, units, 2 * units)
    sides = [*att, g, gain] if half is None else [att[half], g, gain]
    side_specs = halves.pair(width) if half is None else [rows_of(ROWS, width)]
    ins = [x, *sides, *pieces.arrays, *filled]
    out = kernel_call(
        functools.partial(units_body, pieces, halves, units, half, len(filled)),
        halves.grid if half is None else (halves.count,),
        ins,
        [part, *side_specs, part, whole(gain.shape)] + [HBM] * (pieces.count + len(filled)),
        [out_of((tokens, n)) for n in widths] + [out_of((tokens // 2, width))] * (4 if half is None else 2),
        [spec(n) for n in widths] + (halves.pair(width) * 2 if half is None else [rows_of(ROWS, width)] * 2),
        12 * tokens * width * units,
        pieces.scratch,
        places,
        {len(ins) - len(filled) + 1 + k: k for k in range(len(filled))},
    )
    if half is None:
        return *out[:3], tuple(out[3:5]), tuple(out[5:])
    return out[:3], *out[3:]


def grads_body(runs, cut, steps, places, *refs):
    inputs = max(right for columns in runs for _, right in columns) + 1
    ins, outs = refs[:inputs], refs[inputs:]
    values = []
    for columns in runs:
        values.append([])
        for slots, k in columns:
            rows = [ins[s][...] for s in slots]
            rows = jnp.concatenate(rows, axis=1) if len(rows) > 1 else rows[0]
            values[-1].append(mm(rows, ins[k][...], TN).astype(BF))
    if not cut:
        at = 0
        for value in values[0]:
            outs[0][:, at : at + value.shape[1]] = value
            at += value.shape[1]
        return
    *outs, buffer, sems = outs
    height = outs[0].shape[0]
    own = height // len(runs)
    slots = ROWS // own

    def copies(block):
        at = 0
        for k in range(slots):
            t = block * slots + k
            for ref in outs[t : t + 1] if t < cut else outs[t : t + 2] if t == cut else outs[t + 1 : t + 2]:
                rows = buffer.at[block % 2, pl.ds(at, ref.shape[0])]
                yield pltpu.make_async_copy(rows, ref, sems.at[block % 2, at // (height // 2)])
                at += ref.shape[0]

    for block in range(steps):

        @pl.when(pl.program_id(0) == block)
        def _():
            if block >= 2:
                for copy in copies(block - 2):
                    copy.wait()
            for k in range(slots):
                for r, columns in enumerate(values):
                    at = 0
                    first = (k * len(runs) + r) * own
                    for value in columns:
                        cols = slice(at, at + value.shape[1])
                        buffer[block % 2, first : first + own, cols] = value[k * own : (k + 1) * own]
                        at += value.shape[1]
            for copy in copies(block):
                copy.start()
            if block == steps - 1:
                for last in range(max(0, steps - 2), steps):
                    for copy in copies(last):
                        copy.wait()


def weight_grads(places, runs, cut):
    count = places.shape[0] - 1
    tokens, width = runs[0][0][0].shape
    own = width // count
    steps = width // ROWS
    slots = ROWS // own if cut else 1
    ins, specs, marks = [], [], []
    for columns in runs:
        for left, _ in columns:
            mark = []
            for k in range(slots):
                place = (lambda i, p, k=k: (0, p[i * slots + k])) if cut else (lambda i, p: (0, i))
                ins.append(left)
                specs.append(pl.BlockSpec((tokens, ROWS // slots), place))
                mark.append(len(ins) - 1)
            marks.append(tuple(mark))
    pairs = []
    for columns in runs:
        pairs.append([])
        for _, right in columns:
            ins.append(right)
            specs.append(whole(right.shape))
            pairs[-1].append((marks.pop(0), len(ins) - 1))
    total = sum(right.shape[1] for _, right in runs[0])
    if cut:
        height = own * len(runs)
        heights = [height] * cut + [height // 2] * 2 + [height] * (count - cut - 1)
        outs = [out_of((h, total)) for h in heights]
        out_specs = [HBM] * len(outs)
        scratch = [
            pltpu.VMEM((2, slots * height, total), BF),
            pltpu.SemaphoreType.DMA((2, 2 * slots)),
        ]
    else:
        outs, out_specs, scratch = [out_of((width, total))], [rows_of(ROWS, total)], []
    return kernel_call(
        functools.partial(grads_body, pairs, cut, steps),
        (steps,),
        ins,
        specs,
        outs,
        out_specs,
        2 * tokens * width * total,
        scratch,
        places,
    )


def norm_back(grad_hidden, value, gain):
    normed, scale = norm(value)
    scaled = grad_hidden * gain
    back = scale * (scaled - normed * jnp.mean(scaled * normed, axis=-1, keepdims=True))
    return back, jnp.sum(grad_hidden * normed, axis=0, keepdims=True)


def add_up(ref, value):
    @pl.when(pl.program_id(0) == 0)
    def _():
        ref[...] = jnp.zeros_like(ref)

    ref[...] += value


def middle_body(halves, _, x_ref, att0, att1, g_ref, dh0, dh1, gain_ref, dm_ref, dgain_ref):
    value = x_ref[...].astype(F32) + halves.pick((att0, att1)).astype(F32)
    back, d_gain = norm_back(halves.pick((dh0, dh1)).astype(F32), value, gain_ref[...])
    dm_ref[...] = (g_ref[...].astype(F32) + back).astype(BF)
    add_up(dgain_ref, d_gain)


def middle_back(places, x, att, g, dh, gain):
    tokens, width = x.shape
    halves = Halves(tokens)
    part, pair = halves.both(width), halves.pair(width)
    return kernel_call(
        functools.partial(middle_body, halves),
        halves.grid,
        (x, *att, g, *dh, gain),
        [part, *pair, part, *pair, whole(gain.shape)],
        [out_of((tokens, width)), out_of((1, width), F32)],
        [part, whole((1, width))],
        0,
        (),
        places,
    )


def attend_back_body(pieces, shared, steps, hw, places, x0, x1, g1, dm0, att0, att1, dh0, dh1, gain, qkv0, qkv1, *refs):
    sides = [
        [r for a in p.arrays for r, b in zip(refs, shared.arrays) if a is b] for p in pieces
    ]
    dqkv0, dqkv1, dm1, mine, other, dgain, dgain_ffn, w0, sems0, w1, sems1, d_hidden = refs[-12:]
    for p, s, w, sems in zip(pieces, sides, (w0, w1), (sems0, sems1)):
        p.start(s, places, w, sems, range(1))
    first = pl.program_id(0) == 0
    value = x1[...].astype(F32) + jnp.where(first, att1[...], att0[...]).astype(F32)
    back, d_gain = norm_back(jnp.where(first, dh1[...], dh0[...]).astype(F32), value, gain[...])
    dm1[...] = (g1[...].astype(F32) + back).astype(BF)
    add_up(dgain_ffn, d_gain)
    normed = [norm(x[...].astype(F32))[0] for x in (x0, x1)]
    for p, s, w, sems in zip(pieces, sides, (w0, w1), (sems0, sems1)):
        p.wait(s, places, w, sems, 0)
    scale = HDIM ** (-0.5)
    low_scale = jnp.asarray(scale, BF)
    hidden = [hidden_keys(2 * SUB, (1 + c) * SUB, steps, True) for c in range(2)]
    d_mixed = [mm(d[...], w[:, 3 * hw :]).astype(BF) for d, w in ((dm0, w0), (dm1, w1))]
    for s in range(dm0.shape[0] // SUB):
        rows = slice(s * SUB, (s + 1) * SUB)
        for j in range(hw // PAIR):
            cols = [slice(t * hw + j * PAIR, t * hw + (j + 1) * PAIR) for t in range(3)]
            q0, k0, v0 = (qkv0[rows, c] for c in cols)
            q1, k1, v1 = (qkv1[rows, c] for c in cols)
            keys = (k0, jnp.concatenate([k0, k1], axis=0))
            values = (v0, jnp.concatenate([v0, v1], axis=0))
            d_k, d_v = [], []
            for c, (q, out_ref) in enumerate(((q0, dqkv0), (q1, dqkv1))):
                q_two = stack_heads(q) * low_scale
                d_two = stack_heads(d_mixed[c][rows, cols[0]])
                soft = softmax_turned(q_two, keys[c], hidden[c])
                d_probs = mm(values[c], d_two, NT)
                inside = jnp.sum(soft * d_probs, axis=0, keepdims=True)
                d_scores = (soft * (d_probs - inside)).astype(BF)
                d_q = pick_heads(mm(d_scores, keys[c], TN)) * scale
                out_ref[rows, cols[0]] = d_q.astype(BF)
                d_k.append(mm(d_scores, q_two))
                d_v.append(mm(soft.astype(BF), d_two))
            dqkv0[rows, cols[1]] = (d_k[0] + d_k[1][:SUB]).astype(BF)
            dqkv1[rows, cols[1]] = d_k[1][SUB:].astype(BF)
            dqkv0[rows, cols[2]] = (d_v[0] + d_v[1][:SUB]).astype(BF)
            dqkv1[rows, cols[2]] = d_v[1][SUB:].astype(BF)
    gains = []
    for c, (d, w) in enumerate(((dqkv0, w0), (dqkv1, w1))):
        grad = mm(d[...], w[:, : 3 * hw], NT)
        gains.append(jnp.sum(grad * normed[c], axis=0, keepdims=True))
        d_hidden[c] = grad.astype(BF)

    for k, ref in enumerate((other, mine)):

        @pl.when(pl.program_id(0) == k)
        def _():
            ref[...] = d_hidden[...]

    add_up(dgain, jnp.concatenate(gains, axis=0))


def attend_back(places, x, g1, dm0, att1, dh1, gain, qkv, w, part, before, steps):
    tokens, width = dm0.shape
    halves = Halves(tokens)
    pieces = [Pieces(*side, 1) for side in w]
    shared = Pieces(w[0][0] + w[1][0], w[0][1], 1)
    hw = pieces[0].shape[1] // 4
    spot = lambda i, p: (halves.block(i * halves.count, p) + part, 0)
    flat, thin = pl.BlockSpec((ROWS, width), spot), pl.BlockSpec((ROWS, 3 * hw), spot)
    sums = pl.BlockSpec((ROWS, width), lambda i, p: (part, 0))
    block = (2, ROWS, width)
    ins = [*x, g1, dm0, *att1, *dh1, gain, *qkv, *shared.arrays, *before]
    specs = [flat] * 4 + [sums] * 4 + [whole(gain.shape)] + [thin] * 2
    d0, d1, dm1, mine, other, d_gain, d_gain_ffn = kernel_call(
        functools.partial(attend_back_body, pieces, shared, steps, hw),
        (2,),
        ins,
        specs + [HBM] * (len(ins) - len(specs)),
        [out_of((tokens, 3 * hw))] * 2
        + [out_of((tokens, width))]
        + [out_of(block)] * 2
        + [out_of((2, width), F32), out_of((1, width), F32)],
        [thin] * 2 + [flat] + [whole(block)] * 2 + [whole((2, width)), whole((1, width))],
        8 * ROWS * width * 4 * hw,
        pieces[0].scratch + pieces[1].scratch + [pltpu.VMEM(block, BF)],
        places,
        {len(ins) - len(before) + 1 + k: k for k in range(len(before))},
    )
    return (d0, d1, dm1), [part.reshape(-1, width) for part in (mine, other)], (d_gain, d_gain_ffn)


def store_frames(out_ref, sums):
    frames, _, width = out_ref.shape
    both = [p.reshape(frames, 1, p.shape[0] // frames, width) for p in sums]
    out_ref[...] = jnp.concatenate(both, axis=1).reshape(frames, -1, width).astype(BF)


def output_body(halves, _, x0, x1, *refs):
    *refs, out_ref = refs
    pairs = [halves.pick(refs[k : k + 2]).astype(F32) for k in range(0, 8, 2)]
    sums = [x[...].astype(F32) + pairs[2 * c] + pairs[2 * c + 1] for c, x in enumerate((x0, x1))]
    store_frames(out_ref, sums)


def output_of(places, x, att, mlp, shape):
    frames, steps, width = shape
    halves = Halves(x[0].shape[0])
    sides = [a for c in range(2) for pair in (att[c], mlp[c]) for a in pair]
    cube = pl.BlockSpec((2 * ROWS // steps, steps, width), lambda i, p: (halves.block(i, p), 0, 0))
    return kernel_call(
        functools.partial(output_body, halves),
        halves.grid,
        [*x, *sides],
        [halves.both(width)] * 2 + halves.pair(width) * 4,
        [out_of(shape)],
        [cube],
        0,
        (),
        places,
    )[0]


def input_body(_, x0, x1, dm0, dm1, mine, other, gain_ref, *refs):
    sums = []
    dh = jnp.where(pl.program_id(0) == 0, other[...], mine[...]).astype(F32)
    for c, (x, dm) in enumerate(((x0, dm0), (x1, dm1))):
        rows = slice(c * ROWS, (c + 1) * ROWS)
        back, _ = norm_back(dh[rows], x[...].astype(F32), gain_ref[c : c + 1])
        sums.append(dm[...].astype(F32) + back)
    store_frames(refs[-1], sums)


def input_back(places, x, dm, dh, gain, part, before, shape):
    frames, steps, width = shape
    halves = Halves(x[0].shape[0])
    block = lambda i, p: halves.block(i * halves.count, p) + part
    flat = pl.BlockSpec((ROWS, width), lambda i, p: (block(i, p), 0))
    cube = pl.BlockSpec((2 * ROWS // steps, steps, width), lambda i, p: (block(i, p), 0, 0))
    ins = [*x, *dm, *dh, gain]
    specs = [flat] * 4 + [whole(d.shape) for d in dh] + [whole(gain.shape)]
    alias = {}
    if before is not None:
        ins.append(before)
        specs.append(HBM)
        alias = {len(ins): 0}
    return kernel_call(input_body, (2,), ins, specs, [out_of(shape)], [cube], 0, (), places, alias)[0]


def finish_body(layout, turned, *refs):
    count = 1 + max(k for terms, _ in layout for k in terms)
    ins, outs = refs[:count], refs[count:]
    own, wide = outs[0].shape[1:]
    for c, (terms, first) in enumerate(layout):
        rows = slice(first, first + own)
        for t, ref in enumerate(outs):
            cols = slice(t * wide, (t + 1) * wide)
            total = ins[terms[0]][rows, cols].astype(F32)
            for k in terms[1:]:
                total = total + ins[k][rows, cols].astype(F32)
            ref[c] = total.T if t == turned else total


def finish(sides, kinds, own):
    arrays, layout = [], []
    for terms, first in sides:
        spots = []
        for term in terms:
            found = [k for k, a in enumerate(arrays) if a is term]
            if not found:
                arrays.append(term)
            spots.append(found[0] if found else len(arrays) - 1)
        layout.append((spots, first))
    wide = arrays[0].shape[1] // kinds
    shapes = [(len(sides), own, wide)] * (kinds - 1) + [(len(sides), wide, own)]
    return kernel_call(
        functools.partial(finish_body, layout, kinds - 1),
        (1,),
        arrays,
        [whole(a.shape) for a in arrays],
        [out_of(s, F32) for s in shapes],
        [whole(s) for s in shapes],
        0,
    )


def add_body(one, a, two, b, one_out, two_out):
    one_out[...] = (one[...].astype(F32) + a[...].astype(F32)).astype(BF)
    two_out[...] = (two[...].astype(F32) + b[...].astype(F32)).astype(BF)


def add_ends(one, a, two, b):
    rows, width = a.shape
    first = pl.BlockSpec((rows, width), lambda i: (0, 0))
    last = pl.BlockSpec((rows, width), lambda i: (one.shape[0] // rows - 1, 0))
    return kernel_call(
        add_body,
        (1,),
        (one, a, two, b),
        [first, first, last, first],
        [out_of(one.shape)] * 2,
        [first, last],
        0,
        alias={0: 0, 2: 1},
    )


class Ring:
    def __init__(self, size):
        self.size = size
        self.rings = size <= 16
        half = size // 2
        order = [2 * q for q in range(half)] + [2 * (size - 1 - q) + 1 for q in range(half, size)]
        self.ahead = [(order[q], order[(q + 1) % size]) for q in range(size)]
        self.behind = [(b, a) for a, b in self.ahead]
        self.me = lax.axis_index("dp")
        place = jnp.where(self.me % 2 == 0, self.me // 2, size - 1 - self.me // 2)
        q = lax.rem(place + jnp.arange(size, dtype=jnp.int32), size)
        self.order = jnp.where(q < half, 2 * q, 2 * (size - 1 - q) + 1).astype(jnp.int32)


class Rounds:
    def __init__(self):
        self.done = ()

    def now(self, value):
        return lax.optimization_barrier((value, *self.done))[0] if self.done else value

    def close(self, *arrays):
        self.done = arrays


class Gather:
    def __init__(self, rounds, ring, shard):
        self.rounds, self.ring = rounds, ring
        self.a, self.b = [shard], [shard]

    def step(self):
        a, b = self.a[-1], self.b[-1]
        if len(self.a) == self.ring.size // 2:
            half = a.shape[0] // 2
            a, b = a[:half], b[half:]
        self.a.append(lax.ppermute(self.rounds.now(a), "dp", self.ring.ahead))
        self.b.append(lax.ppermute(self.rounds.now(b), "dp", self.ring.behind))
        return self.a[-1], self.b[-1]

    def entries(self, part=0, parts=1):
        n = self.ring.size
        own = self.a[0].shape[0] // parts
        found = []
        for t in range(n):
            if t != n // 2:
                found.append((self.b[t] if t < n // 2 else self.a[n - t], t, 0, part * own, own))
            elif parts == 1:
                found.append((self.a[t], t, 0, 0, own // 2))
                found.append((self.b[t], t, own // 2, 0, own // 2))
            else:
                found.append(((self.a[t], self.b[t])[part], t, 0, 0, own))
        return found, own


class Scatter:
    def __init__(self, rounds, ring, blocks):
        self.rounds, self.ring = rounds, ring
        far = ring.size // 2
        self.a, self.b = blocks[far], blocks[far + 1]
        self.blocks = [*blocks[:far], None, *blocks[far + 2 :]]
        self.k = far

    def step(self):
        n = self.ring.size
        if self.k < n // 2:
            one, two = self.blocks[self.k], self.blocks[n - self.k]
            if self.k == n // 2 - 1:
                self.a, self.b = add_ends(one, self.a, two, self.b)
            else:
                self.a = (one.astype(F32) + self.a.astype(F32)).astype(BF)
                self.b = (two.astype(F32) + self.b.astype(F32)).astype(BF)
        self.k -= 1
        self.a = lax.ppermute(self.rounds.now(self.a), "dp", self.ring.ahead)
        self.b = lax.ppermute(self.rounds.now(self.b), "dp", self.ring.behind)
        return self.a, self.b

    def terms(self):
        return [self.blocks[0], self.a, self.b]


class HeadSum:
    def __init__(self, rounds, pair):
        size = lax.axis_size("mp")
        self.rounds, self.pair, self.got = rounds, pair, []
        self.near_moves = [(i, i ^ 1) for i in range(size)]
        self.far_moves = [(i, i ^ 2) for i in range(size)]

    def add(self, one, two):
        return (one.astype(F32) + two.astype(F32)).astype(BF)

    def near_start(self):
        self.near_got = lax.ppermute(self.rounds.now(self.pair[1]), "mp", self.near_moves)
        return self.near_got

    def near_add(self, mine):
        self.mine = self.add(mine, self.near_got)
        return self.mine

    def near(self):
        self.near_start()
        return self.near_add(self.pair[0])

    def far(self, part=1.0):
        start = sum(got.shape[0] for got in self.got)
        rows = int(self.mine.shape[0] * part)
        moved = self.rounds.now(self.mine[start : start + rows])
        self.got.append(lax.ppermute(moved, "mp", self.far_moves))
        return self.got[-1]

    def last(self):
        got = [self.rounds.now(got) for got in self.got]
        self.mine = self.add(self.mine, jnp.concatenate(got, 0))
        self.sum = (self.mine, lax.ppermute(self.mine, "mp", self.near_moves))
        return self.sum[1]


def exchange_steps(axes):
    for axis in axes:
        size, step = lax.axis_size(axis), 1
        while step < size:
            yield axis, [(i, i ^ step) for i in range(size)], step
            step *= 2


def on_device(
    layer_input, frame_mask, gain_attn, w_query, w_key, w_value, w_out, gain_ffn, w_gate, w_up,
    w_down, cotangent,
):
    sets, width = gain_attn.shape[0], layer_input.shape[2]
    shape = layer_input.shape
    each = shape[1] // sets
    ring = Ring(lax.axis_size("dp"))
    rings, n = ring.rings, ring.size
    far = n // 2 if rings else 0
    own = width // n
    places = jnp.concatenate([ring.order, (lax.axis_index("mp") % 2).astype(jnp.int32)[None]])
    gather = lambda value: lax.all_gather(value, "dp", tiled=True)
    scatter = lambda value: lax.psum_scatter(value, "dp", scatter_dimension=0, tiled=True)
    rounds = Rounds()
    now, close = rounds.now, rounds.close

    attn_own = pack_attn(w_query, w_key, w_value, w_out)
    small = jnp.concatenate([gain_attn, gain_ffn], 0).astype(F32)[None]
    steps = list(exchange_steps(("dp",)))
    ffn_own, x, g = [], [], []

    def gain_step(value):
        axis, moves, step = steps.pop(0)
        other = lax.ppermute(now(value), axis, moves)
        bit = (ring.me // step) % 2
        both = [jnp.concatenate(pair, 0) for pair in ((value, other), (other, value))]
        return jnp.where(bit == 0, *both)

    masks = frame_mask.astype(BF)[:, None, None]
    chores = [
        lambda: ffn_own.append(pack_ffn(now(w_gate), w_up, w_down, 0)),
        lambda: x.append(split_sets(now(layer_input), sets)[0]),
        lambda: ffn_own.append(pack_ffn(now(w_gate), w_up, w_down, 1)),
        lambda: x.append(split_sets(now(layer_input), sets)[1]),
        lambda: g.append(split_sets(now(cotangent) * masks, sets)[0]),
        lambda: g.append(split_sets(now(cotangent) * masks, sets)[1]),
    ]
    attn = Gather(rounds, ring, attn_own)
    for k in range(max(far, 3)):
        moved = attn.step() if rings else ()
        if rings and k == far - 1:
            rows = [Gather(rounds, ring, shard) for shard in ffn_own]
            moved += rows[0].step()
        for chore in chores[:2]:
            chore()
        del chores[:2]
        if steps:
            small = gain_step(small)
        close(small, *moved, *[v[-1] for v in (ffn_own, x, g) if v])
    while steps:
        small = gain_step(small)
    gains = small.transpose(1, 0, 2).reshape(2 * sets, width)
    g_attn, g_ffn = [[gains[k * sets + c][None] for c in range(sets)] for k in range(2)]
    if rings:
        w_attn = [attn.entries(c, sets) for c in range(sets)]
    else:
        both = gather(attn_own).reshape(n, sets, own, -1)
        w_attn = [([(both[:, c].reshape(width, -1), None, 0, 0, width)], width) for c in range(sets)]

    def move(c):
        return rows[c].step() if rings else ()

    def weights(c):
        if rings:
            return rows[c].entries()
        return [(gather(ffn_own[c]), None, 0, 0, width)], width

    h1, qkv, mixed, heads = [None] * 2, [None] * 2, [None] * 2, [None] * 2
    moved = move(0)
    h1[0], qkv[0], mixed[0], part = attend(now(places), x[0], g_attn[0], None, w_attn[0], each)
    heads[0] = HeadSum(rounds, part)
    close(*moved, part[0])
    moved = move(0)
    heads[0].near()
    got = heads[0].far()
    h1[1], qkv[1], mixed[1], part = attend(now(places), x[1], g_attn[1], qkv[0], w_attn[1], each)
    heads[1] = HeadSum(rounds, part)
    held, rounds.done = rounds.done, (*rounds.done, part[0])
    moved += move(0)
    rounds.done = held
    close(*moved, part[0], got)
    close(heads[1].near(), heads[0].last())

    def grads_of(c, out):
        columns = [(out[0], out[2]), (g[c], out[1])]
        return weight_grads(now(places), [columns], far)

    dh, mlp, grads, dm, d_gain_ffn = ([None] * 2 for _ in range(5))
    moved = move(1)
    got = heads[1].far(0.5)
    ffn = (x[0], heads[0].sum, g[0], g_ffn[0], weights(0))
    out, dh_other, mlp_other = hidden_units(now(places), *ffn, half=1)
    close(*moved, dh_other, got)
    moved = move(1)
    got = heads[1].far(0.5)
    dh[0] = HeadSum(rounds, (None, dh_other))
    mlp[0] = HeadSum(rounds, (None, mlp_other))
    near = dh[0].near_start(), mlp[0].near_start()
    out, dh_mine, mlp_mine = hidden_units(now(places), *ffn, half=0, filled=out)
    close(*moved, dh_mine, got, *near)
    dh[0].near_add(dh_mine)
    mlp[0].near_add(mlp_mine)
    moved = move(1)
    got = dh[0].far(0.5)
    grads[0] = grads_of(0, out)
    close(*moved, grads[0][0], got, heads[1].last())
    att = [head.sum for head in heads]
    sums = [Scatter(rounds, ring, grads[0])] if rings else []
    add = lambda k: sums[k].step() if rings else ()
    close(*move(1), *add(0), dh[0].far(0.5))

    moved = (*add(0), dh[0].last())
    got = mlp[0].far(0.5)
    ffn = (x[1], att[1], g[1], g_ffn[1], weights(1))
    out, dh_other, mlp_other = hidden_units(now(places), *ffn, half=1)
    close(*moved, dh_other, got)
    moved = add(0)
    got = mlp[0].far(0.5)
    dh[1] = HeadSum(rounds, (None, dh_other))
    mlp[1] = HeadSum(rounds, (None, mlp_other))
    near = dh[1].near_start(), mlp[1].near_start()
    out, dh_mine, mlp_mine = hidden_units(now(places), *ffn, half=0, filled=out)
    close(*moved, dh_mine, got, *near)
    dh[1].near_add(dh_mine)
    mlp[1].near_add(mlp_mine)
    moved = add(0)
    got = dh[1].far()
    grads[1] = grads_of(1, out)
    if rings:
        sums.append(Scatter(rounds, ring, grads[1]))
        moved += add(1)
    dm[0], d_gain_ffn[0] = middle_back(now(places), x[0], att[0], g[0], dh[0].sum, g_ffn[0])
    close(*moved, grads[1][0], dm[0], got)
    close(dh[1].last(), mlp[0].last())

    moved = add(1)
    got = mlp[1].far(0.75)
    backward = (x, g[1], dm[0], att[1], dh[1].sum, g_ffn[1], qkv, w_attn)
    found, part, d_gain0 = attend_back(now(places), *backward, 0, (), each)
    back = [HeadSum(rounds, part)]
    close(*moved, part[0], got)
    moved = (*add(1), back[0].near(), mlp[1].far(0.25))
    (*d_qkv, dm[1]), part, d_gain1 = attend_back(now(places), *backward, 1, found, each)
    back.append(HeadSum(rounds, part))
    close(*moved, part[0])

    shared = lax.axis_size("mp")
    d_gain_attn, d_gain_ffn[1] = (one + two for one, two in zip(d_gain0, d_gain1))
    d_gains = jnp.concatenate([d_gain_attn, *[d / shared for d in d_gain_ffn]], 0)
    steps = list(exchange_steps(("mp", "dp")))

    def sum_step(value, *earlier):
        axis, moves, _ = steps.pop(0)
        got = lax.ppermute(now(value), axis, moves)
        return value + lax.optimization_barrier((got, *earlier))[0]

    moved = (*add(1), back[1].near())
    got = back[0].far(0.75)
    d_gains = sum_step(sum_step(d_gains))
    runs = [[(h1[c], d_qkv[c]), (dm[c], mixed[c])] for c in range(sets)]
    if rings:
        blocks = weight_grads(now(places), runs, far)
        sums.append(Scatter(rounds, ring, blocks))
    else:
        blocks = [weight_grads(now(places), [run], far)[0] for run in runs]
    close(*moved, blocks[0], got, d_gains)
    moved = (*add(2), mlp[1].last())
    got = back[0].far(0.25)
    d_gains = sum_step(d_gains)
    if rings:
        ffn_sums = [([now(t) for t in s.terms()], 0) for s in sums[:2]]
    else:
        ffn_sums = [([scatter(b[0])], 0) for b in grads]
    d_gate_w, d_up_w, d_down_w = finish(ffn_sums, 3, own)
    close(*moved, d_gains, d_gate_w, got)
    moved = (*add(2), back[0].last())
    d_gains = sum_step(d_gains)
    got = back[1].far(0.5)
    output = output_of(now(places), x, att, [m.sum for m in mlp], shape)
    close(*moved, d_gains, got, output)
    moved = add(2)
    while steps:
        d_gains = sum_step(d_gains)
    got = back[1].far(0.5)
    grad_input = input_back(now(places), x, dm, back[0].sum, gains[:sets], 0, None, shape)
    close(*moved, grad_input, d_gains, got)
    moved = add(2)
    back[1].last()
    grad_input = input_back(now(places), x, dm, back[1].sum, gains[:sets], 1, grad_input, shape)
    close(*moved, grad_input)
    if rings:
        terms = [now(t) for t in sums[2].terms()]
        attn_sums = [(terms, c * own) for c in range(sets)]
    else:
        attn_sums = [([scatter(b)], 0) for b in blocks]
    d_query, d_key, d_value, d_out = finish(attn_sums, 4, own)
    d_gains = lax.dynamic_slice_in_dim(d_gains, ring.me * own, own, 1)
    return (
        output, grad_input, d_gains[:sets], d_query, d_key, d_value, d_out,
        d_gains[sets:], d_gate_w, d_up_w, d_down_w,
    )


def solution(mesh):
    rows = P("dp", None, None)
    gain = P(None, "dp")
    into = P(None, "dp", "mp")
    back = P(None, "mp", "dp")
    weights = (gain, into, into, into, back, gain, into, into, back)
    return jax.shard_map(
        on_device,
        mesh=mesh,
        in_specs=(rows, P("dp"), *weights, rows),
        out_specs=(rows, rows, *weights),
        check_vma=False,
    )
```

```python
import functools

import jax
import jax.numpy as jnp
from jax import lax
from jax.experimental import pallas as pl
from jax.experimental.pallas import tpu as pltpu
from jax.sharding import PartitionSpec as P

HDIM = 64
EPS = 1e-05
NEG = -1e30
BF = jnp.bfloat16
F32 = jnp.float32
NN = (((1,), (0,)), ((), ()))
NT = (((1,), (1,)), ((), ()))
TN = (((0,), (0,)), ((), ()))
MIB = 1024 * 1024
SUB = 128
PAIR = 2 * HDIM
ROWS = 256
HBM = pl.BlockSpec(memory_space=pl.ANY)


def mm(left, right, dims=NN):
    return lax.dot_general(left, right, dims, preferred_element_type=F32)


def kernel_call(body, grid, ins, in_specs, outs, out_specs, flops, scratch=(), scalars=None, alias=None):
    moved = sum(a.size * a.dtype.itemsize for a in ins) + sum(
        o.size * jnp.dtype(o.dtype).itemsize for o in outs
    )
    spec = pltpu.PrefetchScalarGridSpec(
        num_scalar_prefetch=0 if scalars is None else 1,
        grid=grid,
        in_specs=in_specs,
        out_specs=out_specs,
        scratch_shapes=scratch,
    )
    args = ins if scalars is None else (scalars, *ins)
    return pl.pallas_call(
        body,
        grid_spec=spec,
        out_shape=outs,
        input_output_aliases=alias or {},
        compiler_params=pltpu.CompilerParams(vmem_limit_bytes=56 * MIB),
        cost_estimate=pl.CostEstimate(flops=1, bytes_accessed=1, transcendentals=0),
    )(*args)


def whole(shape):
    return pl.BlockSpec(shape, lambda *i: (0,) * len(shape))


def rows_of(rows, width, start=0):
    return pl.BlockSpec((rows, width), lambda i, *_: (i + start, 0))


def out_of(shape, kind=BF):
    return jax.ShapeDtypeStruct(shape, kind)


class Halves:
    def __init__(self, tokens):
        self.count = tokens // 2 // ROWS
        self.grid = (2 * self.count,)

    def block(self, i, places):
        half = (1 - i // self.count + places[places.shape[0] - 1]) % 2
        return half * self.count + i % self.count

    def both(self, width):
        return pl.BlockSpec((ROWS, width), lambda i, p: (self.block(i, p), 0))

    def pair(self, width):
        return [
            pl.BlockSpec((ROWS, width), lambda i, p: (jnp.maximum(i - self.count, 0), 0)),
            pl.BlockSpec((ROWS, width), lambda i, p: (jnp.minimum(i, self.count - 1), 0)),
        ]

    def pick(self, pair):
        return jnp.where(pl.program_id(0) < self.count, pair[1][...], pair[0][...])

    def one(self, width, half):
        shift = 0 if half else self.count
        return pl.BlockSpec((ROWS, width), lambda i, p: (self.block(i + shift, p), 0))

    def put(self, pair, value):
        pair[0][...] = value

        @pl.when(pl.program_id(0) < self.count)
        def _():
            pair[1][...] = pair[0][...]


def split_sets(value, sets):
    frames, steps, width = value.shape
    parts = value.reshape(frames, sets, steps // sets, width)
    return [parts[:, c].reshape(-1, width) for c in range(sets)]


def pack_attn_body(wq, wk, wv, wo, out):
    own, hw = wq.shape[1:]
    for c in range(2):
        rows = slice(c * own, (c + 1) * own)
        for t, w in enumerate((wq, wk, wv)):
            out[rows, t * hw : (t + 1) * hw] = w[c]
        out[rows, 3 * hw :] = wo[c].T


def pack_attn(wq, wk, wv, wo):
    sets, own, hw = wq.shape
    piece = (sets * own, 4 * hw)
    return kernel_call(
        pack_attn_body,
        (1,),
        (wq, wk, wv, wo),
        [whole(w.shape) for w in (wq, wk, wv, wo)],
        [out_of(piece)],
        [whole(piece)],
        0,
    )[0]


def pack_ffn_body(wg, wu, wd, out):
    units = wg.shape[2]
    out[:, :units] = wg[0]
    out[:, units : 2 * units] = wu[0]
    out[:, 2 * units :] = wd[0].T


def pack_ffn(wg, wu, wd, c):
    own, units = wg.shape[1:]
    piece = (own, 3 * units)
    into = pl.BlockSpec((1, own, units), lambda i: (c, 0, 0))
    back = pl.BlockSpec((1, units, own), lambda i: (c, 0, 0))
    return kernel_call(
        pack_ffn_body,
        (1,),
        (wg, wu, wd),
        [into, into, back],
        [out_of(piece)],
        [whole(piece)],
        0,
    )[0]


def norm(value):
    scale = lax.rsqrt(jnp.mean(value * value, axis=-1, keepdims=True) + EPS)
    return value * scale, scale


def lanes_low(shape):
    return lax.broadcasted_iota(jnp.int32, shape, 1) < HDIM


def stack_heads(pair):
    low = lanes_low(pair.shape)
    zero = jnp.zeros_like(pair)
    return jnp.concatenate([jnp.where(low, pair, zero), jnp.where(low, zero, pair)], axis=0)


def pick_heads(stacked):
    half = stacked.shape[0] // 2
    low = lanes_low((half, stacked.shape[1]))
    return jnp.where(low, stacked[:half], stacked[half:])


def hidden_keys(rows, keys, steps, turned=False):
    shape, axis = ((keys, rows), 1) if turned else ((rows, keys), 0)
    row = lax.broadcasted_iota(jnp.int32, shape, axis) & (SUB - 1)
    spot = lax.broadcasted_iota(jnp.int32, shape, 1 - axis)
    key = spot & (SUB - 1)
    shift = steps.bit_length() - 1
    seen = lax.shift_right_logical(row, shift) == lax.shift_right_logical(key, shift)
    own = spot >= keys - SUB
    seen = seen & ((row >= key) | jnp.logical_not(own))
    return jnp.where(seen, 0.0, NEG)


def softmax(query, keys, hidden):
    raw = mm(query, keys, NT) + hidden
    power = jnp.exp(raw - jnp.max(raw, axis=-1, keepdims=True))
    return power * (1.0 / jnp.sum(power, axis=-1, keepdims=True))


def softmax_turned(query, keys, hidden):
    raw = mm(keys, query, NT) + hidden
    power = jnp.exp(raw - jnp.max(raw, axis=0, keepdims=True))
    return power * (1.0 / jnp.sum(power, axis=0, keepdims=True))


class Pieces:
    def __init__(self, entries, own, groups):
        self.entries = entries
        self.own = own
        self.groups = groups
        self.arrays = []
        for array, *_ in entries:
            if not any(array is a for a in self.arrays):
                self.arrays.append(array)
        self.count = len(self.arrays)
        self.shape = (sum(e[4] for e in entries), entries[0][0].shape[1])
        self.scratch = [pltpu.VMEM(self.shape, BF), pltpu.SemaphoreType.DMA((groups, len(entries)))]

    def copies(self, refs, places, memory, sems, group):
        wide = self.shape[1] // self.groups
        cols = pl.ds(group * wide, wide)
        for k, (array, slot, row, first, rows) in enumerate(self.entries):
            ref = [r for r, a in zip(refs, self.arrays) if a is array][0]
            start = row if slot is None else pl.multiple_of(places[slot] * self.own + row, rows)
            source = ref.at[pl.ds(first, rows), cols]
            yield pltpu.make_async_copy(source, memory.at[pl.ds(start, rows), cols], sems.at[group, k])

    def start(self, refs, places, memory, sems, order):
        @pl.when(pl.program_id(0) == 0)
        def _():
            for group in order:
                for copy in self.copies(refs, places, memory, sems, group):
                    copy.start()

    def wait(self, refs, places, memory, sems, group):
        @pl.when(pl.program_id(0) == 0)
        def _():
            for copy in self.copies(refs, places, memory, sems, group):
                copy.wait()


def attend_body(pieces, halves, steps, hw, later, filled, places, *refs):
    x_ref, gain_ref, *refs = refs
    if later:
        before_ref, *refs = refs
    w_refs, refs = refs[: pieces.count], refs[pieces.count :]
    h_ref, qkv_ref, mixed_ref, *part_refs, w_ref, sems = refs[filled:]
    pieces.start(w_refs, places, w_ref, sems, range(1))
    normed, _ = norm(x_ref[...].astype(F32))
    hidden = (normed * gain_ref[...]).astype(BF)
    h_ref[...] = hidden
    pieces.wait(w_refs, places, w_ref, sems, 0)
    qkv = mm(hidden, w_ref[:, : 3 * hw]).astype(BF)
    qkv_ref[...] = qkv
    scale = jnp.asarray(HDIM ** (-0.5), BF)
    hidden_scores = hidden_keys(2 * SUB, 2 * SUB if later else SUB, steps)
    for s in range(x_ref.shape[0] // SUB):
        rows = slice(s * SUB, (s + 1) * SUB)
        for j in range(hw // PAIR):
            q, k, v = (qkv[rows, t * hw + j * PAIR : t * hw + (j + 1) * PAIR] for t in range(3))
            if later:
                k_old, v_old = (
                    before_ref[rows, t * hw + j * PAIR : t * hw + (j + 1) * PAIR] for t in (1, 2)
                )
                k = jnp.concatenate([k_old, k], axis=0)
                v = jnp.concatenate([v_old, v], axis=0)
            probs = softmax(stack_heads(q) * scale, k, hidden_scores).astype(BF)
            mixed_ref[rows, j * PAIR : (j + 1) * PAIR] = pick_heads(mm(probs, v)).astype(BF)
    part = mm(mixed_ref[...], w_ref[:, 3 * hw :], NT).astype(BF)
    if len(part_refs) == 2:
        halves.put(part_refs, part)
    else:
        part_refs[0][...] = part


def attend(places, x, gain, before, w, steps, half=None, filled=()):
    tokens, width = x.shape
    pieces, halves = Pieces(*w, 1), Halves(tokens)
    hw = pieces.shape[1] // 4
    spec = halves.both if half is None else functools.partial(halves.one, half=half)
    ins = [x, gain]
    specs = [spec(width), whole(gain.shape)]
    if before is not None:
        ins.append(before)
        specs.append(spec(3 * hw))
    ins += [*pieces.arrays, *filled]
    specs += [HBM] * (pieces.count + len(filled))
    widths = (width, 3 * hw, hw)
    *out, part = kernel_call(
        functools.partial(attend_body, pieces, halves, steps, hw, before is not None, len(filled)),
        halves.grid if half is None else (halves.count,),
        ins,
        specs,
        [out_of((tokens, n)) for n in widths] + [out_of((tokens // 2, width))] * (2 if half is None else 1),
        [spec(n) for n in widths] + (halves.pair(width) if half is None else [rows_of(ROWS, width)]),
        2 * tokens * width * 4 * hw,
        pieces.scratch,
        places,
        {len(ins) - len(filled) + 1 + k: k for k in range(len(filled))},
    )
    if half is None:
        return *out[:3], (out[3], part)
    return *out, part


def units_body(pieces, halves, units, half, filled, places, x_ref, *refs):
    if half is None:
        att0, att1, *refs = refs
        att = halves.pick((att0, att1))
    else:
        att_ref, *refs = refs
        att = att_ref[...]
    g_ref, gain_ref, *refs = refs
    w_refs, refs = refs[: pieces.count], refs[pieces.count + filled :]
    h_ref, inner_ref, dboth_ref, *sum_refs, w_ref, sems = refs
    pieces.start(w_refs, places, w_ref, sems, (2, 0, 1))
    normed, _ = norm(x_ref[...].astype(F32) + att.astype(F32))
    hidden = (normed * gain_ref[...]).astype(BF)
    h_ref[...] = hidden
    cut = 256
    cols = [
        [slice(t * units + u * cut, t * units + (u + 1) * cut) for t in range(3)] for u in range(units // cut)
    ]
    pieces.wait(w_refs, places, w_ref, sems, 2)
    d_inners = [mm(g_ref[...], w_ref[:, c[2]]) for c in cols]
    pieces.wait(w_refs, places, w_ref, sems, 0)
    pieces.wait(w_refs, places, w_ref, sems, 1)
    for c, d_inner in zip(cols, d_inners):
        gate = mm(hidden, w_ref[:, c[0]])
        up = mm(hidden, w_ref[:, c[1]])
        sigma = 1.0 / (1.0 + jnp.exp(-gate))
        active = gate * sigma
        inner_ref[:, c[0]] = (active * up).astype(BF)
        dboth_ref[:, c[1]] = (d_inner * active).astype(BF)
        dboth_ref[:, c[0]] = (d_inner * up * (sigma + active * (1.0 - sigma))).astype(BF)
    d_hidden = mm(dboth_ref[...], w_ref[:, : 2 * units], NT).astype(BF)
    if half is None:
        halves.put(sum_refs[:2], d_hidden)
        halves.put(sum_refs[2:], mm(inner_ref[...], w_ref[:, 2 * units :], NT).astype(BF))
    else:
        sum_refs[0][...] = d_hidden
        sum_refs[1][...] = mm(inner_ref[...], w_ref[:, 2 * units :], NT).astype(BF)


def hidden_units(places, x, att, g, gain, w, half=None, filled=()):
    tokens, width = x.shape
    pieces, halves = Pieces(*w, 3), Halves(tokens)
    units = pieces.shape[1] // 3
    spec = halves.both if half is None else functools.partial(halves.one, half=half)
    part = spec(width)
    widths = (width, units, 2 * units)
    sides = [*att, g, gain] if half is None else [att[half], g, gain]
    side_specs = halves.pair(width) if half is None else [rows_of(ROWS, width)]
    ins = [x, *sides, *pieces.arrays, *filled]
    out = kernel_call(
        functools.partial(units_body, pieces, halves, units, half, len(filled)),
        halves.grid if half is None else (halves.count,),
        ins,
        [part, *side_specs, part, whole(gain.shape)] + [HBM] * (pieces.count + len(filled)),
        [out_of((tokens, n)) for n in widths] + [out_of((tokens // 2, width))] * (4 if half is None else 2),
        [spec(n) for n in widths] + (halves.pair(width) * 2 if half is None else [rows_of(ROWS, width)] * 2),
        12 * tokens * width * units,
        pieces.scratch,
        places,
        {len(ins) - len(filled) + 1 + k: k for k in range(len(filled))},
    )
    if half is None:
        return *out[:3], tuple(out[3:5]), tuple(out[5:])
    return out[:3], *out[3:]


def grads_body(runs, cut, steps, places, *refs):
    inputs = max(right for columns in runs for _, right in columns) + 1
    ins, outs = refs[:inputs], refs[inputs:]
    values = []
    for columns in runs:
        values.append([])
        for slots, k in columns:
            rows = [ins[s][...] for s in slots]
            rows = jnp.concatenate(rows, axis=1) if len(rows) > 1 else rows[0]
            values[-1].append(mm(rows, ins[k][...], TN).astype(BF))
    if not cut:
        at = 0
        for value in values[0]:
            outs[0][:, at : at + value.shape[1]] = value
            at += value.shape[1]
        return
    *outs, buffer, sems = outs
    height = outs[0].shape[0]
    own = height // len(runs)
    slots = ROWS // own

    def copies(block):
        at = 0
        for k in range(slots):
            t = block * slots + k
            for ref in outs[t : t + 1] if t < cut else outs[t : t + 2] if t == cut else outs[t + 1 : t + 2]:
                rows = buffer.at[block % 2, pl.ds(at, ref.shape[0])]
                yield pltpu.make_async_copy(rows, ref, sems.at[block % 2, at // (height // 2)])
                at += ref.shape[0]

    for block in range(steps):

        @pl.when(pl.program_id(0) == block)
        def _():
            if block >= 2:
                for copy in copies(block - 2):
                    copy.wait()
            for k in range(slots):
                for r, columns in enumerate(values):
                    at = 0
                    first = (k * len(runs) + r) * own
                    for value in columns:
                        cols = slice(at, at + value.shape[1])
                        buffer[block % 2, first : first + own, cols] = value[k * own : (k + 1) * own]
                        at += value.shape[1]
            for copy in copies(block):
                copy.start()
            if block == steps - 1:
                for last in range(max(0, steps - 2), steps):
                    for copy in copies(last):
                        copy.wait()


def weight_grads(places, runs, cut):
    count = places.shape[0] - 1
    tokens, width = runs[0][0][0].shape
    own = width // count
    steps = width // ROWS
    slots = ROWS // own if cut else 1
    ins, specs, marks = [], [], []
    for columns in runs:
        for left, _ in columns:
            mark = []
            for k in range(slots):
                place = (lambda i, p, k=k: (0, p[i * slots + k])) if cut else (lambda i, p: (0, i))
                ins.append(left)
                specs.append(pl.BlockSpec((tokens, ROWS // slots), place))
                mark.append(len(ins) - 1)
            marks.append(tuple(mark))
    pairs = []
    for columns in runs:
        pairs.append([])
        for _, right in columns:
            ins.append(right)
            specs.append(whole(right.shape))
            pairs[-1].append((marks.pop(0), len(ins) - 1))
    total = sum(right.shape[1] for _, right in runs[0])
    if cut:
        height = own * len(runs)
        heights = [height] * cut + [height // 2] * 2 + [height] * (count - cut - 1)
        outs = [out_of((h, total)) for h in heights]
        out_specs = [HBM] * len(outs)
        scratch = [
            pltpu.VMEM((2, slots * height, total), BF),
            pltpu.SemaphoreType.DMA((2, 2 * slots)),
        ]
    else:
        outs, out_specs, scratch = [out_of((width, total))], [rows_of(ROWS, total)], []
    return kernel_call(
        functools.partial(grads_body, pairs, cut, steps),
        (steps,),
        ins,
        specs,
        outs,
        out_specs,
        2 * tokens * width * total,
        scratch,
        places,
    )


def norm_back(grad_hidden, value, gain):
    normed, scale = norm(value)
    scaled = grad_hidden * gain
    back = scale * (scaled - normed * jnp.mean(scaled * normed, axis=-1, keepdims=True))
    return back, jnp.sum(grad_hidden * normed, axis=0, keepdims=True)


def add_up(ref, value):
    @pl.when(pl.program_id(0) == 0)
    def _():
        ref[...] = jnp.zeros_like(ref)

    ref[...] += value


def middle_body(halves, _, x_ref, att0, att1, g_ref, dh0, dh1, gain_ref, dm_ref, dgain_ref):
    value = x_ref[...].astype(F32) + halves.pick((att0, att1)).astype(F32)
    back, d_gain = norm_back(halves.pick((dh0, dh1)).astype(F32), value, gain_ref[...])
    dm_ref[...] = (g_ref[...].astype(F32) + back).astype(BF)
    add_up(dgain_ref, d_gain)


def middle_back(places, x, att, g, dh, gain):
    tokens, width = x.shape
    halves = Halves(tokens)
    part, pair = halves.both(width), halves.pair(width)
    return kernel_call(
        functools.partial(middle_body, halves),
        halves.grid,
        (x, *att, g, *dh, gain),
        [part, *pair, part, *pair, whole(gain.shape)],
        [out_of((tokens, width)), out_of((1, width), F32)],
        [part, whole((1, width))],
        0,
        (),
        places,
    )


def attend_back_body(pieces, shared, steps, hw, places, x0, x1, g1, dm0, att0, att1, dh0, dh1, gain, qkv0, qkv1, *refs):
    sides = [
        [r for a in p.arrays for r, b in zip(refs, shared.arrays) if a is b] for p in pieces
    ]
    dqkv0, dqkv1, dm1, mine, other, dgain, dgain_ffn, w0, sems0, w1, sems1, d_hidden = refs[-12:]
    for p, s, w, sems in zip(pieces, sides, (w0, w1), (sems0, sems1)):
        p.start(s, places, w, sems, range(1))
    first = pl.program_id(0) == 0
    value = x1[...].astype(F32) + jnp.where(first, att1[...], att0[...]).astype(F32)
    back, d_gain = norm_back(jnp.where(first, dh1[...], dh0[...]).astype(F32), value, gain[...])
    dm1[...] = (g1[...].astype(F32) + back).astype(BF)
    add_up(dgain_ffn, d_gain)
    normed = [norm(x[...].astype(F32))[0] for x in (x0, x1)]
    for p, s, w, sems in zip(pieces, sides, (w0, w1), (sems0, sems1)):
        p.wait(s, places, w, sems, 0)
    scale = HDIM ** (-0.5)
    low_scale = jnp.asarray(scale, BF)
    hidden = [hidden_keys(2 * SUB, (1 + c) * SUB, steps, True) for c in range(2)]
    d_mixed = [mm(d[...], w[:, 3 * hw :]).astype(BF) for d, w in ((dm0, w0), (dm1, w1))]
    for s in range(dm0.shape[0] // SUB):
        rows = slice(s * SUB, (s + 1) * SUB)
        for j in range(hw // PAIR):
            cols = [slice(t * hw + j * PAIR, t * hw + (j + 1) * PAIR) for t in range(3)]
            q0, k0, v0 = (qkv0[rows, c] for c in cols)
            q1, k1, v1 = (qkv1[rows, c] for c in cols)
            keys = (k0, jnp.concatenate([k0, k1], axis=0))
            values = (v0, jnp.concatenate([v0, v1], axis=0))
            d_k, d_v = [], []
            for c, (q, out_ref) in enumerate(((q0, dqkv0), (q1, dqkv1))):
                q_two = stack_heads(q) * low_scale
                d_two = stack_heads(d_mixed[c][rows, cols[0]])
                soft = softmax_turned(q_two, keys[c], hidden[c])
                d_probs = mm(values[c], d_two, NT)
                inside = jnp.sum(soft * d_probs, axis=0, keepdims=True)
                d_scores = (soft * (d_probs - inside)).astype(BF)
                d_q = pick_heads(mm(d_scores, keys[c], TN)) * scale
                out_ref[rows, cols[0]] = d_q.astype(BF)
                d_k.append(mm(d_scores, q_two))
                d_v.append(mm(soft.astype(BF), d_two))
            dqkv0[rows, cols[1]] = (d_k[0] + d_k[1][:SUB]).astype(BF)
            dqkv1[rows, cols[1]] = d_k[1][SUB:].astype(BF)
            dqkv0[rows, cols[2]] = (d_v[0] + d_v[1][:SUB]).astype(BF)
            dqkv1[rows, cols[2]] = d_v[1][SUB:].astype(BF)
    gains = []
    for c, (d, w) in enumerate(((dqkv0, w0), (dqkv1, w1))):
        grad = mm(d[...], w[:, : 3 * hw], NT)
        gains.append(jnp.sum(grad * normed[c], axis=0, keepdims=True))
        d_hidden[c] = grad.astype(BF)

    for k, ref in enumerate((other, mine)):

        @pl.when(pl.program_id(0) == k)
        def _():
            ref[...] = d_hidden[...]

    add_up(dgain, jnp.concatenate(gains, axis=0))


def attend_back(places, x, g1, dm0, att1, dh1, gain, qkv, w, part, before, steps):
    tokens, width = dm0.shape
    halves = Halves(tokens)
    pieces = [Pieces(*side, 1) for side in w]
    shared = Pieces(w[0][0] + w[1][0], w[0][1], 1)
    hw = pieces[0].shape[1] // 4
    spot = lambda i, p: (halves.block(i * halves.count, p) + part, 0)
    flat, thin = pl.BlockSpec((ROWS, width), spot), pl.BlockSpec((ROWS, 3 * hw), spot)
    sums = pl.BlockSpec((ROWS, width), lambda i, p: (part, 0))
    block = (2, ROWS, width)
    ins = [*x, g1, dm0, *att1, *dh1, gain, *qkv, *shared.arrays, *before]
    specs = [flat] * 4 + [sums] * 4 + [whole(gain.shape)] + [thin] * 2
    d0, d1, dm1, mine, other, d_gain, d_gain_ffn = kernel_call(
        functools.partial(attend_back_body, pieces, shared, steps, hw),
        (2,),
        ins,
        specs + [HBM] * (len(ins) - len(specs)),
        [out_of((tokens, 3 * hw))] * 2
        + [out_of((tokens, width))]
        + [out_of(block)] * 2
        + [out_of((2, width), F32), out_of((1, width), F32)],
        [thin] * 2 + [flat] + [whole(block)] * 2 + [whole((2, width)), whole((1, width))],
        8 * ROWS * width * 4 * hw,
        pieces[0].scratch + pieces[1].scratch + [pltpu.VMEM(block, BF)],
        places,
        {len(ins) - len(before) + 1 + k: k for k in range(len(before))},
    )
    return (d0, d1, dm1), [part.reshape(-1, width) for part in (mine, other)], (d_gain, d_gain_ffn)


def store_frames(out_ref, sums):
    frames, _, width = out_ref.shape
    both = [p.reshape(frames, 1, p.shape[0] // frames, width) for p in sums]
    out_ref[...] = jnp.concatenate(both, axis=1).reshape(frames, -1, width).astype(BF)


def output_body(halves, _, x0, x1, *refs):
    *refs, out_ref = refs
    pairs = [halves.pick(refs[k : k + 2]).astype(F32) for k in range(0, 8, 2)]
    sums = [x[...].astype(F32) + pairs[2 * c] + pairs[2 * c + 1] for c, x in enumerate((x0, x1))]
    store_frames(out_ref, sums)


def output_of(places, x, att, mlp, shape):
    frames, steps, width = shape
    halves = Halves(x[0].shape[0])
    sides = [a for c in range(2) for pair in (att[c], mlp[c]) for a in pair]
    cube = pl.BlockSpec((2 * ROWS // steps, steps, width), lambda i, p: (halves.block(i, p), 0, 0))
    return kernel_call(
        functools.partial(output_body, halves),
        halves.grid,
        [*x, *sides],
        [halves.both(width)] * 2 + halves.pair(width) * 4,
        [out_of(shape)],
        [cube],
        0,
        (),
        places,
    )[0]


def input_body(_, x0, x1, dm0, dm1, mine, other, gain_ref, *refs):
    sums = []
    dh = jnp.where(pl.program_id(0) == 0, other[...], mine[...]).astype(F32)
    for c, (x, dm) in enumerate(((x0, dm0), (x1, dm1))):
        rows = slice(c * ROWS, (c + 1) * ROWS)
        back, _ = norm_back(dh[rows], x[...].astype(F32), gain_ref[c : c + 1])
        sums.append(dm[...].astype(F32) + back)
    store_frames(refs[-1], sums)


def input_back(places, x, dm, dh, gain, part, before, shape):
    frames, steps, width = shape
    halves = Halves(x[0].shape[0])
    block = lambda i, p: halves.block(i * halves.count, p) + part
    flat = pl.BlockSpec((ROWS, width), lambda i, p: (block(i, p), 0))
    cube = pl.BlockSpec((2 * ROWS // steps, steps, width), lambda i, p: (block(i, p), 0, 0))
    ins = [*x, *dm, *dh, gain]
    specs = [flat] * 4 + [whole(d.shape) for d in dh] + [whole(gain.shape)]
    alias = {}
    if before is not None:
        ins.append(before)
        specs.append(HBM)
        alias = {len(ins): 0}
    return kernel_call(input_body, (2,), ins, specs, [out_of(shape)], [cube], 0, (), places, alias)[0]


def finish_body(layout, turned, *refs):
    count = 1 + max(k for terms, _ in layout for k in terms)
    ins, outs = refs[:count], refs[count:]
    own, wide = outs[0].shape[1:]
    for c, (terms, first) in enumerate(layout):
        rows = slice(first, first + own)
        for t, ref in enumerate(outs):
            cols = slice(t * wide, (t + 1) * wide)
            total = ins[terms[0]][rows, cols].astype(F32)
            for k in terms[1:]:
                total = total + ins[k][rows, cols].astype(F32)
            ref[c] = total.T if t == turned else total


def finish(sides, kinds, own):
    arrays, layout = [], []
    for terms, first in sides:
        spots = []
        for term in terms:
            found = [k for k, a in enumerate(arrays) if a is term]
            if not found:
                arrays.append(term)
            spots.append(found[0] if found else len(arrays) - 1)
        layout.append((spots, first))
    wide = arrays[0].shape[1] // kinds
    shapes = [(len(sides), own, wide)] * (kinds - 1) + [(len(sides), wide, own)]
    return kernel_call(
        functools.partial(finish_body, layout, kinds - 1),
        (1,),
        arrays,
        [whole(a.shape) for a in arrays],
        [out_of(s, F32) for s in shapes],
        [whole(s) for s in shapes],
        0,
    )


def add_body(one, a, two, b, one_out, two_out):
    one_out[...] = (one[...].astype(F32) + a[...].astype(F32)).astype(BF)
    two_out[...] = (two[...].astype(F32) + b[...].astype(F32)).astype(BF)


def add_ends(one, a, two, b):
    rows, width = a.shape
    first = pl.BlockSpec((rows, width), lambda i: (0, 0))
    last = pl.BlockSpec((rows, width), lambda i: (one.shape[0] // rows - 1, 0))
    return kernel_call(
        add_body,
        (1,),
        (one, a, two, b),
        [first, first, last, first],
        [out_of(one.shape)] * 2,
        [first, last],
        0,
        alias={0: 0, 2: 1},
    )


class Ring:
    def __init__(self, size):
        self.size = size
        self.rings = size <= 16
        half = size // 2
        order = [2 * q for q in range(half)] + [2 * (size - 1 - q) + 1 for q in range(half, size)]
        self.ahead = [(order[q], order[(q + 1) % size]) for q in range(size)]
        self.behind = [(b, a) for a, b in self.ahead]
        self.me = lax.axis_index("dp")
        place = jnp.where(self.me % 2 == 0, self.me // 2, size - 1 - self.me // 2)
        q = lax.rem(place + jnp.arange(size, dtype=jnp.int32), size)
        self.order = jnp.where(q < half, 2 * q, 2 * (size - 1 - q) + 1).astype(jnp.int32)


class Rounds:
    def __init__(self):
        self.done = ()

    def now(self, value):
        return lax.optimization_barrier((value, *self.done))[0] if self.done else value

    def close(self, *arrays):
        self.done = arrays


class Gather:
    def __init__(self, rounds, ring, shard):
        self.rounds, self.ring = rounds, ring
        self.a, self.b = [shard], [shard]

    def step(self):
        a, b = self.a[-1], self.b[-1]
        if len(self.a) == self.ring.size // 2:
            half = a.shape[0] // 2
            a, b = a[:half], b[half:]
        self.a.append(lax.ppermute(self.rounds.now(a), "dp", self.ring.ahead))
        self.b.append(lax.ppermute(self.rounds.now(b), "dp", self.ring.behind))
        return self.a[-1], self.b[-1]

    def entries(self, part=0, parts=1):
        n = self.ring.size
        own = self.a[0].shape[0] // parts
        found = []
        for t in range(n):
            if t != n // 2:
                found.append((self.b[t] if t < n // 2 else self.a[n - t], t, 0, part * own, own))
            elif parts == 1:
                found.append((self.a[t], t, 0, 0, own // 2))
                found.append((self.b[t], t, own // 2, 0, own // 2))
            else:
                found.append(((self.a[t], self.b[t])[part], t, 0, 0, own))
        return found, own


class Scatter:
    def __init__(self, rounds, ring, blocks):
        self.rounds, self.ring = rounds, ring
        far = ring.size // 2
        self.a, self.b = blocks[far], blocks[far + 1]
        self.blocks = [*blocks[:far], None, *blocks[far + 2 :]]
        self.k = far

    def step(self):
        n = self.ring.size
        if self.k < n // 2:
            one, two = self.blocks[self.k], self.blocks[n - self.k]
            if self.k == n // 2 - 1:
                self.a, self.b = add_ends(one, self.a, two, self.b)
            else:
                self.a = (one.astype(F32) + self.a.astype(F32)).astype(BF)
                self.b = (two.astype(F32) + self.b.astype(F32)).astype(BF)
        self.k -= 1
        self.a = lax.ppermute(self.rounds.now(self.a), "dp", self.ring.ahead)
        self.b = lax.ppermute(self.rounds.now(self.b), "dp", self.ring.behind)
        return self.a, self.b

    def terms(self):
        return [self.blocks[0], self.a, self.b]


class HeadSum:
    def __init__(self, rounds, pair):
        size = lax.axis_size("mp")
        self.rounds, self.pair, self.got = rounds, pair, []
        self.near_moves = [(i, i ^ 1) for i in range(size)]
        self.far_moves = [(i, i ^ 2) for i in range(size)]

    def add(self, one, two):
        return (one.astype(F32) + two.astype(F32)).astype(BF)

    def near_start(self):
        self.near_got = lax.ppermute(self.rounds.now(self.pair[1]), "mp", self.near_moves)
        return self.near_got

    def near_add(self, mine):
        self.mine = self.add(mine, self.near_got)
        return self.mine

    def near(self):
        self.near_start()
        return self.near_add(self.pair[0])

    def far(self, part=1.0):
        start = sum(got.shape[0] for got in self.got)
        rows = int(self.mine.shape[0] * part)
        moved = self.rounds.now(self.mine[start : start + rows])
        self.got.append(lax.ppermute(moved, "mp", self.far_moves))
        return self.got[-1]

    def last(self):
        got = [self.rounds.now(got) for got in self.got]
        self.mine = self.add(self.mine, jnp.concatenate(got, 0))
        self.sum = (self.mine, lax.ppermute(self.mine, "mp", self.near_moves))
        return self.sum[1]


def exchange_steps(axes):
    for axis in axes:
        size, step = lax.axis_size(axis), 1
        while step < size:
            yield axis, [(i, i ^ step) for i in range(size)], step
            step *= 2


def on_device(
    layer_input, frame_mask, gain_attn, w_query, w_key, w_value, w_out, gain_ffn, w_gate, w_up,
    w_down, cotangent,
):
    sets, width = gain_attn.shape[0], layer_input.shape[2]
    shape = layer_input.shape
    each = shape[1] // sets
    ring = Ring(lax.axis_size("dp"))
    rings, n = ring.rings, ring.size
    far = n // 2 if rings else 0
    own = width // n
    places = jnp.concatenate([ring.order, (lax.axis_index("mp") % 2).astype(jnp.int32)[None]])
    gather = lambda value: lax.all_gather(value, "dp", tiled=True)
    scatter = lambda value: lax.psum_scatter(value, "dp", scatter_dimension=0, tiled=True)
    rounds = Rounds()
    now, close = rounds.now, rounds.close

    attn_own = pack_attn(w_query, w_key, w_value, w_out)
    small = jnp.concatenate([gain_attn, gain_ffn], 0).astype(F32)[None]
    steps = list(exchange_steps(("dp",)))
    ffn_own, x, g = [], [], []

    def gain_step(value):
        axis, moves, step = steps.pop(0)
        other = lax.ppermute(now(value), axis, moves)
        bit = (ring.me // step) % 2
        both = [jnp.concatenate(pair, 0) for pair in ((value, other), (other, value))]
        return jnp.where(bit == 0, *both)

    masks = frame_mask.astype(BF)[:, None, None]
    chores = [
        lambda: ffn_own.append(pack_ffn(now(w_gate), w_up, w_down, 0)),
        lambda: x.append(split_sets(now(layer_input), sets)[0]),
        lambda: ffn_own.append(pack_ffn(now(w_gate), w_up, w_down, 1)),
        lambda: x.append(split_sets(now(layer_input), sets)[1]),
        lambda: g.append(split_sets(now(cotangent) * masks, sets)[0]),
        lambda: g.append(split_sets(now(cotangent) * masks, sets)[1]),
    ]
    attn = Gather(rounds, ring, attn_own)
    for k in range(max(far, 3)):
        moved = attn.step() if rings else ()
        if rings and k == far - 1:
            rows = [Gather(rounds, ring, shard) for shard in ffn_own]
            moved += rows[0].step()
        for chore in chores[:2]:
            chore()
        del chores[:2]
        if steps:
            small = gain_step(small)
        close(small, *moved, *[v[-1] for v in (ffn_own, x, g) if v])
    while steps:
        small = gain_step(small)
    gains = small.transpose(1, 0, 2).reshape(2 * sets, width)
    g_attn, g_ffn = [[gains[k * sets + c][None] for c in range(sets)] for k in range(2)]
    if rings:
        w_attn = [attn.entries(c, sets) for c in range(sets)]
    else:
        both = gather(attn_own).reshape(n, sets, own, -1)
        w_attn = [([(both[:, c].reshape(width, -1), None, 0, 0, width)], width) for c in range(sets)]

    def move(c):
        return rows[c].step() if rings else ()

    def weights(c):
        if rings:
            return rows[c].entries()
        return [(gather(ffn_own[c]), None, 0, 0, width)], width

    h1, qkv, mixed, heads = [None] * 2, [None] * 2, [None] * 2, [None] * 2
    moved = move(0)
    h1[0], qkv[0], mixed[0], part = attend(now(places), x[0], g_attn[0], None, w_attn[0], each)
    heads[0] = HeadSum(rounds, part)
    close(*moved, part[0])
    moved = move(0)
    heads[0].near()
    got = heads[0].far()
    h1[1], qkv[1], mixed[1], part = attend(now(places), x[1], g_attn[1], qkv[0], w_attn[1], each)
    heads[1] = HeadSum(rounds, part)
    held, rounds.done = rounds.done, (*rounds.done, part[0])
    moved += move(0)
    rounds.done = held
    close(*moved, part[0], got)
    moved = move(1)
    close(heads[1].near(), heads[0].last())

    def grads_of(c, out):
        columns = [(out[0], out[2]), (g[c], out[1])]
        return weight_grads(now(places), [columns], far)

    dh, mlp, grads, dm, d_gain_ffn = ([None] * 2 for _ in range(5))
    got = heads[1].far(0.5)
    ffn = (x[0], heads[0].sum, g[0], g_ffn[0], weights(0))
    out, dh_other, mlp_other = hidden_units(now(places), *ffn, half=1)
    close(*moved, dh_other, got)
    moved = move(1)
    got = heads[1].far(0.5)
    dh[0] = HeadSum(rounds, (None, dh_other))
    mlp[0] = HeadSum(rounds, (None, mlp_other))
    near = dh[0].near_start(), mlp[0].near_start()
    out, dh_mine, mlp_mine = hidden_units(now(places), *ffn, half=0, filled=out)
    close(*moved, dh_mine, got, *near)
    dh[0].near_add(dh_mine)
    mlp[0].near_add(mlp_mine)
    moved = move(1)
    got = dh[0].far(0.5)
    grads[0] = grads_of(0, out)
    close(*moved, grads[0][0], got, heads[1].last())
    att = [head.sum for head in heads]
    sums = [Scatter(rounds, ring, grads[0])] if rings else []
    add = lambda k: sums[k].step() if rings else ()
    close(*move(1), *add(0), dh[0].far(0.5))

    moved = (*add(0), dh[0].last())
    got = mlp[0].far(0.5)
    ffn = (x[1], att[1], g[1], g_ffn[1], weights(1))
    out, dh_other, mlp_other = hidden_units(now(places), *ffn, half=1)
    close(*moved, dh_other, got)
    moved = add(0)
    got = mlp[0].far(0.5)
    dh[1] = HeadSum(rounds, (None, dh_other))
    mlp[1] = HeadSum(rounds, (None, mlp_other))
    near = dh[1].near_start(), mlp[1].near_start()
    out, dh_mine, mlp_mine = hidden_units(now(places), *ffn, half=0, filled=out)
    close(*moved, dh_mine, got, *near)
    dh[1].near_add(dh_mine)
    mlp[1].near_add(mlp_mine)
    moved = add(0)
    got = dh[1].far()
    grads[1] = grads_of(1, out)
    if rings:
        sums.append(Scatter(rounds, ring, grads[1]))
        moved += add(1)
    dm[0], d_gain_ffn[0] = middle_back(now(places), x[0], att[0], g[0], dh[0].sum, g_ffn[0])
    close(*moved, grads[1][0], dm[0], got)
    close(dh[1].last(), mlp[0].last())

    moved = add(1)
    got = mlp[1].far(0.75)
    backward = (x, g[1], dm[0], att[1], dh[1].sum, g_ffn[1], qkv, w_attn)
    found, part, d_gain0 = attend_back(now(places), *backward, 0, (), each)
    back = [HeadSum(rounds, part)]
    close(*moved, part[0], got)
    moved = (*add(1), back[0].near(), mlp[1].far(0.25))
    (*d_qkv, dm[1]), part, d_gain1 = attend_back(now(places), *backward, 1, found, each)
    back.append(HeadSum(rounds, part))
    close(*moved, part[0])

    shared = lax.axis_size("mp")
    d_gain_attn, d_gain_ffn[1] = (one + two for one, two in zip(d_gain0, d_gain1))
    d_gains = jnp.concatenate([d_gain_attn, *[d / shared for d in d_gain_ffn]], 0)
    steps = list(exchange_steps(("mp", "dp")))

    def sum_step(value, *earlier):
        axis, moves, _ = steps.pop(0)
        got = lax.ppermute(now(value), axis, moves)
        return value + lax.optimization_barrier((got, *earlier))[0]

    moved = (*add(1), back[1].near())
    got = back[0].far(0.75)
    d_gains = sum_step(sum_step(d_gains))
    runs = [[(h1[c], d_qkv[c]), (dm[c], mixed[c])] for c in range(sets)]
    if rings:
        blocks = weight_grads(now(places), runs, far)
        sums.append(Scatter(rounds, ring, blocks))
    else:
        blocks = [weight_grads(now(places), [run], far)[0] for run in runs]
    close(*moved, blocks[0], got, d_gains)
    moved = (*add(2), mlp[1].last())
    got = back[0].far(0.25)
    d_gains = sum_step(d_gains)
    if rings:
        ffn_sums = [([now(t) for t in s.terms()], 0) for s in sums[:2]]
    else:
        ffn_sums = [([scatter(b[0])], 0) for b in grads]
    d_gate_w, d_up_w, d_down_w = finish(ffn_sums, 3, own)
    close(*moved, d_gains, d_gate_w, got)
    moved = (*add(2), back[0].last())
    d_gains = sum_step(d_gains)
    got = back[1].far(0.5)
    output = output_of(now(places), x, att, [m.sum for m in mlp], shape)
    close(*moved, d_gains, got, output)
    moved = add(2)
    while steps:
        d_gains = sum_step(d_gains)
    got = back[1].far(0.5)
    grad_input = input_back(now(places), x, dm, back[0].sum, gains[:sets], 0, None, shape)
    close(*moved, grad_input, d_gains, got)
    moved = add(2)
    back[1].last()
    grad_input = input_back(now(places), x, dm, back[1].sum, gains[:sets], 1, grad_input, shape)
    close(*moved, grad_input)
    if rings:
        terms = [now(t) for t in sums[2].terms()]
        attn_sums = [(terms, c * own) for c in range(sets)]
    else:
        attn_sums = [([scatter(b)], 0) for b in blocks]
    d_query, d_key, d_value, d_out = finish(attn_sums, 4, own)
    d_gains = lax.dynamic_slice_in_dim(d_gains, ring.me * own, own, 1)
    return (
        output, grad_input, d_gains[:sets], d_query, d_key, d_value, d_out,
        d_gains[sets:], d_gate_w, d_up_w, d_down_w,
    )


def solution(mesh):
    rows = P("dp", None, None)
    gain = P(None, "dp")
    into = P(None, "dp", "mp")
    back = P(None, "mp", "dp")
    weights = (gain, into, into, into, back, gain, into, into, back)
    return jax.shard_map(
        on_device,
        mesh=mesh,
        in_specs=(rows, P("dp"), *weights, rows),
        out_specs=(rows, rows, *weights),
        check_vma=False,
    )
```

```python
import functools

import jax
import jax.numpy as jnp
from jax import lax
from jax.experimental import pallas as pl
from jax.experimental.pallas import tpu as pltpu
from jax.sharding import PartitionSpec as P

HDIM = 64
EPS = 1e-05
NEG = -1e30
BF = jnp.bfloat16
F32 = jnp.float32
NN = (((1,), (0,)), ((), ()))
NT = (((1,), (1,)), ((), ()))
TN = (((0,), (0,)), ((), ()))
MIB = 1024 * 1024
SUB = 128
PAIR = 2 * HDIM
ROWS = 256
HBM = pl.BlockSpec(memory_space=pl.ANY)


def mm(left, right, dims=NN):
    return lax.dot_general(left, right, dims, preferred_element_type=F32)


def kernel_call(body, grid, ins, in_specs, outs, out_specs, flops, scratch=(), scalars=None, alias=None):
    moved = sum(a.size * a.dtype.itemsize for a in ins) + sum(
        o.size * jnp.dtype(o.dtype).itemsize for o in outs
    )
    spec = pltpu.PrefetchScalarGridSpec(
        num_scalar_prefetch=0 if scalars is None else 1,
        grid=grid,
        in_specs=in_specs,
        out_specs=out_specs,
        scratch_shapes=scratch,
    )
    args = ins if scalars is None else (scalars, *ins)
    return pl.pallas_call(
        body,
        grid_spec=spec,
        out_shape=outs,
        input_output_aliases=alias or {},
        compiler_params=pltpu.CompilerParams(vmem_limit_bytes=56 * MIB),
        cost_estimate=pl.CostEstimate(flops=500000000, bytes_accessed=1, transcendentals=0),
    )(*args)


def whole(shape):
    return pl.BlockSpec(shape, lambda *i: (0,) * len(shape))


def rows_of(rows, width, start=0):
    return pl.BlockSpec((rows, width), lambda i, *_: (i + start, 0))


def out_of(shape, kind=BF):
    return jax.ShapeDtypeStruct(shape, kind)


class Halves:
    def __init__(self, tokens):
        self.count = tokens // 2 // ROWS
        self.grid = (2 * self.count,)

    def block(self, i, places):
        half = (1 - i // self.count + places[places.shape[0] - 1]) % 2
        return half * self.count + i % self.count

    def both(self, width):
        return pl.BlockSpec((ROWS, width), lambda i, p: (self.block(i, p), 0))

    def pair(self, width):
        return [
            pl.BlockSpec((ROWS, width), lambda i, p: (jnp.maximum(i - self.count, 0), 0)),
            pl.BlockSpec((ROWS, width), lambda i, p: (jnp.minimum(i, self.count - 1), 0)),
        ]

    def pick(self, pair):
        return jnp.where(pl.program_id(0) < self.count, pair[1][...], pair[0][...])

    def one(self, width, half):
        shift = 0 if half else self.count
        return pl.BlockSpec((ROWS, width), lambda i, p: (self.block(i + shift, p), 0))

    def put(self, pair, value):
        pair[0][...] = value

        @pl.when(pl.program_id(0) < self.count)
        def _():
            pair[1][...] = pair[0][...]


def split_sets(value, sets):
    frames, steps, width = value.shape
    parts = value.reshape(frames, sets, steps // sets, width)
    return [parts[:, c].reshape(-1, width) for c in range(sets)]


def pack_attn_body(wq, wk, wv, wo, out):
    own, hw = wq.shape[1:]
    for c in range(2):
        rows = slice(c * own, (c + 1) * own)
        for t, w in enumerate((wq, wk, wv)):
            out[rows, t * hw : (t + 1) * hw] = w[c]
        out[rows, 3 * hw :] = wo[c].T


def pack_attn(wq, wk, wv, wo):
    sets, own, hw = wq.shape
    piece = (sets * own, 4 * hw)
    return kernel_call(
        pack_attn_body,
        (1,),
        (wq, wk, wv, wo),
        [whole(w.shape) for w in (wq, wk, wv, wo)],
        [out_of(piece)],
        [whole(piece)],
        0,
    )[0]


def pack_ffn_body(wg, wu, wd, out):
    units = wg.shape[2]
    out[:, :units] = wg[0]
    out[:, units : 2 * units] = wu[0]
    out[:, 2 * units :] = wd[0].T


def pack_ffn(wg, wu, wd, c):
    own, units = wg.shape[1:]
    piece = (own, 3 * units)
    into = pl.BlockSpec((1, own, units), lambda i: (c, 0, 0))
    back = pl.BlockSpec((1, units, own), lambda i: (c, 0, 0))
    return kernel_call(
        pack_ffn_body,
        (1,),
        (wg, wu, wd),
        [into, into, back],
        [out_of(piece)],
        [whole(piece)],
        0,
    )[0]


def norm(value):
    scale = lax.rsqrt(jnp.mean(value * value, axis=-1, keepdims=True) + EPS)
    return value * scale, scale


def lanes_low(shape):
    return lax.broadcasted_iota(jnp.int32, shape, 1) < HDIM


def stack_heads(pair):
    low = lanes_low(pair.shape)
    zero = jnp.zeros_like(pair)
    return jnp.concatenate([jnp.where(low, pair, zero), jnp.where(low, zero, pair)], axis=0)


def pick_heads(stacked):
    half = stacked.shape[0] // 2
    low = lanes_low((half, stacked.shape[1]))
    return jnp.where(low, stacked[:half], stacked[half:])


def hidden_keys(rows, keys, steps, turned=False):
    shape, axis = ((keys, rows), 1) if turned else ((rows, keys), 0)
    row = lax.broadcasted_iota(jnp.int32, shape, axis) & (SUB - 1)
    spot = lax.broadcasted_iota(jnp.int32, shape, 1 - axis)
    key = spot & (SUB - 1)
    shift = steps.bit_length() - 1
    seen = lax.shift_right_logical(row, shift) == lax.shift_right_logical(key, shift)
    own = spot >= keys - SUB
    seen = seen & ((row >= key) | jnp.logical_not(own))
    return jnp.where(seen, 0.0, NEG)


def softmax(query, keys, hidden):
    raw = mm(query, keys, NT) + hidden
    power = jnp.exp(raw - jnp.max(raw, axis=-1, keepdims=True))
    return power * (1.0 / jnp.sum(power, axis=-1, keepdims=True))


def softmax_turned(query, keys, hidden):
    raw = mm(keys, query, NT) + hidden
    power = jnp.exp(raw - jnp.max(raw, axis=0, keepdims=True))
    return power * (1.0 / jnp.sum(power, axis=0, keepdims=True))


class Pieces:
    def __init__(self, entries, own, groups):
        self.entries = entries
        self.own = own
        self.groups = groups
        self.arrays = []
        for array, *_ in entries:
            if not any(array is a for a in self.arrays):
                self.arrays.append(array)
        self.count = len(self.arrays)
        self.shape = (sum(e[4] for e in entries), entries[0][0].shape[1])
        self.scratch = [pltpu.VMEM(self.shape, BF), pltpu.SemaphoreType.DMA((groups, len(entries)))]

    def copies(self, refs, places, memory, sems, group):
        wide = self.shape[1] // self.groups
        cols = pl.ds(group * wide, wide)
        for k, (array, slot, row, first, rows) in enumerate(self.entries):
            ref = [r for r, a in zip(refs, self.arrays) if a is array][0]
            start = row if slot is None else pl.multiple_of(places[slot] * self.own + row, rows)
            source = ref.at[pl.ds(first, rows), cols]
            yield pltpu.make_async_copy(source, memory.at[pl.ds(start, rows), cols], sems.at[group, k])

    def start(self, refs, places, memory, sems, order):
        @pl.when(pl.program_id(0) == 0)
        def _():
            for group in order:
                for copy in self.copies(refs, places, memory, sems, group):
                    copy.start()

    def wait(self, refs, places, memory, sems, group):
        @pl.when(pl.program_id(0) == 0)
        def _():
            for copy in self.copies(refs, places, memory, sems, group):
                copy.wait()


def attend_body(pieces, halves, steps, hw, later, filled, places, *refs):
    x_ref, gain_ref, *refs = refs
    if later:
        before_ref, *refs = refs
    w_refs, refs = refs[: pieces.count], refs[pieces.count :]
    h_ref, qkv_ref, mixed_ref, *part_refs, w_ref, sems = refs[filled:]
    pieces.start(w_refs, places, w_ref, sems, range(1))
    normed, _ = norm(x_ref[...].astype(F32))
    hidden = (normed * gain_ref[...]).astype(BF)
    h_ref[...] = hidden
    pieces.wait(w_refs, places, w_ref, sems, 0)
    qkv = mm(hidden, w_ref[:, : 3 * hw]).astype(BF)
    qkv_ref[...] = qkv
    scale = jnp.asarray(HDIM ** (-0.5), BF)
    hidden_scores = hidden_keys(2 * SUB, 2 * SUB if later else SUB, steps)
    for s in range(x_ref.shape[0] // SUB):
        rows = slice(s * SUB, (s + 1) * SUB)
        for j in range(hw // PAIR):
            q, k, v = (qkv[rows, t * hw + j * PAIR : t * hw + (j + 1) * PAIR] for t in range(3))
            if later:
                k_old, v_old = (
                    before_ref[rows, t * hw + j * PAIR : t * hw + (j + 1) * PAIR] for t in (1, 2)
                )
                k = jnp.concatenate([k_old, k], axis=0)
                v = jnp.concatenate([v_old, v], axis=0)
            probs = softmax(stack_heads(q) * scale, k, hidden_scores).astype(BF)
            mixed_ref[rows, j * PAIR : (j + 1) * PAIR] = pick_heads(mm(probs, v)).astype(BF)
    part = mm(mixed_ref[...], w_ref[:, 3 * hw :], NT).astype(BF)
    if len(part_refs) == 2:
        halves.put(part_refs, part)
    else:
        part_refs[0][...] = part


def attend(places, x, gain, before, w, steps, half=None, filled=()):
    tokens, width = x.shape
    pieces, halves = Pieces(*w, 1), Halves(tokens)
    hw = pieces.shape[1] // 4
    spec = halves.both if half is None else functools.partial(halves.one, half=half)
    ins = [x, gain]
    specs = [spec(width), whole(gain.shape)]
    if before is not None:
        ins.append(before)
        specs.append(spec(3 * hw))
    ins += [*pieces.arrays, *filled]
    specs += [HBM] * (pieces.count + len(filled))
    widths = (width, 3 * hw, hw)
    *out, part = kernel_call(
        functools.partial(attend_body, pieces, halves, steps, hw, before is not None, len(filled)),
        halves.grid if half is None else (halves.count,),
        ins,
        specs,
        [out_of((tokens, n)) for n in widths] + [out_of((tokens // 2, width))] * (2 if half is None else 1),
        [spec(n) for n in widths] + (halves.pair(width) if half is None else [rows_of(ROWS, width)]),
        2 * tokens * width * 4 * hw,
        pieces.scratch,
        places,
        {len(ins) - len(filled) + 1 + k: k for k in range(len(filled))},
    )
    if half is None:
        return *out[:3], (out[3], part)
    return *out, part


def units_body(pieces, halves, units, half, filled, places, x_ref, *refs):
    if half is None:
        att0, att1, *refs = refs
        att = halves.pick((att0, att1))
    else:
        att_ref, *refs = refs
        att = att_ref[...]
    g_ref, gain_ref, *refs = refs
    w_refs, refs = refs[: pieces.count], refs[pieces.count + filled :]
    h_ref, inner_ref, dboth_ref, *sum_refs, w_ref, sems = refs
    pieces.start(w_refs, places, w_ref, sems, (2, 0, 1))
    normed, _ = norm(x_ref[...].astype(F32) + att.astype(F32))
    hidden = (normed * gain_ref[...]).astype(BF)
    h_ref[...] = hidden
    cut = 256
    cols = [
        [slice(t * units + u * cut, t * units + (u + 1) * cut) for t in range(3)] for u in range(units // cut)
    ]
    pieces.wait(w_refs, places, w_ref, sems, 2)
    d_inners = [mm(g_ref[...], w_ref[:, c[2]]) for c in cols]
    pieces.wait(w_refs, places, w_ref, sems, 0)
    pieces.wait(w_refs, places, w_ref, sems, 1)
    for c, d_inner in zip(cols, d_inners):
        gate = mm(hidden, w_ref[:, c[0]])
        up = mm(hidden, w_ref[:, c[1]])
        sigma = 1.0 / (1.0 + jnp.exp(-gate))
        active = gate * sigma
        inner_ref[:, c[0]] = (active * up).astype(BF)
        dboth_ref[:, c[1]] = (d_inner * active).astype(BF)
        dboth_ref[:, c[0]] = (d_inner * up * (sigma + active * (1.0 - sigma))).astype(BF)
    d_hidden = mm(dboth_ref[...], w_ref[:, : 2 * units], NT).astype(BF)
    if half is None:
        halves.put(sum_refs[:2], d_hidden)
        halves.put(sum_refs[2:], mm(inner_ref[...], w_ref[:, 2 * units :], NT).astype(BF))
    else:
        sum_refs[0][...] = d_hidden
        sum_refs[1][...] = mm(inner_ref[...], w_ref[:, 2 * units :], NT).astype(BF)


def hidden_units(places, x, att, g, gain, w, half=None, filled=()):
    tokens, width = x.shape
    pieces, halves = Pieces(*w, 3), Halves(tokens)
    units = pieces.shape[1] // 3
    spec = halves.both if half is None else functools.partial(halves.one, half=half)
    part = spec(width)
    widths = (width, units, 2 * units)
    sides = [*att, g, gain] if half is None else [att[half], g, gain]
    side_specs = halves.pair(width) if half is None else [rows_of(ROWS, width)]
    ins = [x, *sides, *pieces.arrays, *filled]
    out = kernel_call(
        functools.partial(units_body, pieces, halves, units, half, len(filled)),
        halves.grid if half is None else (halves.count,),
        ins,
        [part, *side_specs, part, whole(gain.shape)] + [HBM] * (pieces.count + len(filled)),
        [out_of((tokens, n)) for n in widths] + [out_of((tokens // 2, width))] * (4 if half is None else 2),
        [spec(n) for n in widths] + (halves.pair(width) * 2 if half is None else [rows_of(ROWS, width)] * 2),
        12 * tokens * width * units,
        pieces.scratch,
        places,
        {len(ins) - len(filled) + 1 + k: k for k in range(len(filled))},
    )
    if half is None:
        return *out[:3], tuple(out[3:5]), tuple(out[5:])
    return out[:3], *out[3:]


def grads_body(runs, cut, steps, places, *refs):
    inputs = max(right for columns in runs for _, right in columns) + 1
    ins, outs = refs[:inputs], refs[inputs:]
    values = []
    for columns in runs:
        values.append([])
        for slots, k in columns:
            rows = [ins[s][...] for s in slots]
            rows = jnp.concatenate(rows, axis=1) if len(rows) > 1 else rows[0]
            values[-1].append(mm(rows, ins[k][...], TN).astype(BF))
    if not cut:
        at = 0
        for value in values[0]:
            outs[0][:, at : at + value.shape[1]] = value
            at += value.shape[1]
        return
    *outs, buffer, sems = outs
    height = outs[0].shape[0]
    own = height // len(runs)
    slots = ROWS // own

    def copies(block):
        at = 0
        for k in range(slots):
            t = block * slots + k
            for ref in outs[t : t + 1] if t < cut else outs[t : t + 2] if t == cut else outs[t + 1 : t + 2]:
                rows = buffer.at[block % 2, pl.ds(at, ref.shape[0])]
                yield pltpu.make_async_copy(rows, ref, sems.at[block % 2, at // (height // 2)])
                at += ref.shape[0]

    for block in range(steps):

        @pl.when(pl.program_id(0) == block)
        def _():
            if block >= 2:
                for copy in copies(block - 2):
                    copy.wait()
            for k in range(slots):
                for r, columns in enumerate(values):
                    at = 0
                    first = (k * len(runs) + r) * own
                    for value in columns:
                        cols = slice(at, at + value.shape[1])
                        buffer[block % 2, first : first + own, cols] = value[k * own : (k + 1) * own]
                        at += value.shape[1]
            for copy in copies(block):
                copy.start()
            if block == steps - 1:
                for last in range(max(0, steps - 2), steps):
                    for copy in copies(last):
                        copy.wait()


def weight_grads(places, runs, cut):
    count = places.shape[0] - 1
    tokens, width = runs[0][0][0].shape
    own = width // count
    steps = width // ROWS
    slots = ROWS // own if cut else 1
    ins, specs, marks = [], [], []
    for columns in runs:
        for left, _ in columns:
            mark = []
            for k in range(slots):
                place = (lambda i, p, k=k: (0, p[i * slots + k])) if cut else (lambda i, p: (0, i))
                ins.append(left)
                specs.append(pl.BlockSpec((tokens, ROWS // slots), place))
                mark.append(len(ins) - 1)
            marks.append(tuple(mark))
    pairs = []
    for columns in runs:
        pairs.append([])
        for _, right in columns:
            ins.append(right)
            specs.append(whole(right.shape))
            pairs[-1].append((marks.pop(0), len(ins) - 1))
    total = sum(right.shape[1] for _, right in runs[0])
    if cut:
        height = own * len(runs)
        heights = [height] * cut + [height // 2] * 2 + [height] * (count - cut - 1)
        outs = [out_of((h, total)) for h in heights]
        out_specs = [HBM] * len(outs)
        scratch = [
            pltpu.VMEM((2, slots * height, total), BF),
            pltpu.SemaphoreType.DMA((2, 2 * slots)),
        ]
    else:
        outs, out_specs, scratch = [out_of((width, total))], [rows_of(ROWS, total)], []
    return kernel_call(
        functools.partial(grads_body, pairs, cut, steps),
        (steps,),
        ins,
        specs,
        outs,
        out_specs,
        2 * tokens * width * total,
        scratch,
        places,
    )


def norm_back(grad_hidden, value, gain):
    normed, scale = norm(value)
    scaled = grad_hidden * gain
    back = scale * (scaled - normed * jnp.mean(scaled * normed, axis=-1, keepdims=True))
    return back, jnp.sum(grad_hidden * normed, axis=0, keepdims=True)


def add_up(ref, value):
    @pl.when(pl.program_id(0) == 0)
    def _():
        ref[...] = jnp.zeros_like(ref)

    ref[...] += value


def middle_body(halves, _, x_ref, att0, att1, g_ref, dh0, dh1, gain_ref, dm_ref, dgain_ref):
    value = x_ref[...].astype(F32) + halves.pick((att0, att1)).astype(F32)
    back, d_gain = norm_back(halves.pick((dh0, dh1)).astype(F32), value, gain_ref[...])
    dm_ref[...] = (g_ref[...].astype(F32) + back).astype(BF)
    add_up(dgain_ref, d_gain)


def middle_back(places, x, att, g, dh, gain):
    tokens, width = x.shape
    halves = Halves(tokens)
    part, pair = halves.both(width), halves.pair(width)
    return kernel_call(
        functools.partial(middle_body, halves),
        halves.grid,
        (x, *att, g, *dh, gain),
        [part, *pair, part, *pair, whole(gain.shape)],
        [out_of((tokens, width)), out_of((1, width), F32)],
        [part, whole((1, width))],
        0,
        (),
        places,
    )


def attend_back_body(pieces, shared, steps, hw, places, x0, x1, g1, dm0, att0, att1, dh0, dh1, gain, qkv0, qkv1, *refs):
    sides = [
        [r for a in p.arrays for r, b in zip(refs, shared.arrays) if a is b] for p in pieces
    ]
    dqkv0, dqkv1, dm1, mine, other, dgain, dgain_ffn, w0, sems0, w1, sems1, d_hidden = refs[-12:]
    for p, s, w, sems in zip(pieces, sides, (w0, w1), (sems0, sems1)):
        p.start(s, places, w, sems, range(1))
    first = pl.program_id(0) == 0
    value = x1[...].astype(F32) + jnp.where(first, att1[...], att0[...]).astype(F32)
    back, d_gain = norm_back(jnp.where(first, dh1[...], dh0[...]).astype(F32), value, gain[...])
    dm1[...] = (g1[...].astype(F32) + back).astype(BF)
    add_up(dgain_ffn, d_gain)
    normed = [norm(x[...].astype(F32))[0] for x in (x0, x1)]
    for p, s, w, sems in zip(pieces, sides, (w0, w1), (sems0, sems1)):
        p.wait(s, places, w, sems, 0)
    scale = HDIM ** (-0.5)
    low_scale = jnp.asarray(scale, BF)
    hidden = [hidden_keys(2 * SUB, (1 + c) * SUB, steps, True) for c in range(2)]
    d_mixed = [mm(d[...], w[:, 3 * hw :]).astype(BF) for d, w in ((dm0, w0), (dm1, w1))]
    for s in range(dm0.shape[0] // SUB):
        rows = slice(s * SUB, (s + 1) * SUB)
        for j in range(hw // PAIR):
            cols = [slice(t * hw + j * PAIR, t * hw + (j + 1) * PAIR) for t in range(3)]
            q0, k0, v0 = (qkv0[rows, c] for c in cols)
            q1, k1, v1 = (qkv1[rows, c] for c in cols)
            keys = (k0, jnp.concatenate([k0, k1], axis=0))
            values = (v0, jnp.concatenate([v0, v1], axis=0))
            d_k, d_v = [], []
            for c, (q, out_ref) in enumerate(((q0, dqkv0), (q1, dqkv1))):
                q_two = stack_heads(q) * low_scale
                d_two = stack_heads(d_mixed[c][rows, cols[0]])
                soft = softmax_turned(q_two, keys[c], hidden[c])
                d_probs = mm(values[c], d_two, NT)
                inside = jnp.sum(soft * d_probs, axis=0, keepdims=True)
                d_scores = (soft * (d_probs - inside)).astype(BF)
                d_q = pick_heads(mm(d_scores, keys[c], TN)) * scale
                out_ref[rows, cols[0]] = d_q.astype(BF)
                d_k.append(mm(d_scores, q_two))
                d_v.append(mm(soft.astype(BF), d_two))
            dqkv0[rows, cols[1]] = (d_k[0] + d_k[1][:SUB]).astype(BF)
            dqkv1[rows, cols[1]] = d_k[1][SUB:].astype(BF)
            dqkv0[rows, cols[2]] = (d_v[0] + d_v[1][:SUB]).astype(BF)
            dqkv1[rows, cols[2]] = d_v[1][SUB:].astype(BF)
    gains = []
    for c, (d, w) in enumerate(((dqkv0, w0), (dqkv1, w1))):
        grad = mm(d[...], w[:, : 3 * hw], NT)
        gains.append(jnp.sum(grad * normed[c], axis=0, keepdims=True))
        d_hidden[c] = grad.astype(BF)

    for k, ref in enumerate((other, mine)):

        @pl.when(pl.program_id(0) == k)
        def _():
            ref[...] = d_hidden[...]

    add_up(dgain, jnp.concatenate(gains, axis=0))


def attend_back(places, x, g1, dm0, att1, dh1, gain, qkv, w, part, before, steps):
    tokens, width = dm0.shape
    halves = Halves(tokens)
    pieces = [Pieces(*side, 1) for side in w]
    shared = Pieces(w[0][0] + w[1][0], w[0][1], 1)
    hw = pieces[0].shape[1] // 4
    spot = lambda i, p: (halves.block(i * halves.count, p) + part, 0)
    flat, thin = pl.BlockSpec((ROWS, width), spot), pl.BlockSpec((ROWS, 3 * hw), spot)
    sums = pl.BlockSpec((ROWS, width), lambda i, p: (part, 0))
    block = (2, ROWS, width)
    ins = [*x, g1, dm0, *att1, *dh1, gain, *qkv, *shared.arrays, *before]
    specs = [flat] * 4 + [sums] * 4 + [whole(gain.shape)] + [thin] * 2
    d0, d1, dm1, mine, other, d_gain, d_gain_ffn = kernel_call(
        functools.partial(attend_back_body, pieces, shared, steps, hw),
        (2,),
        ins,
        specs + [HBM] * (len(ins) - len(specs)),
        [out_of((tokens, 3 * hw))] * 2
        + [out_of((tokens, width))]
        + [out_of(block)] * 2
        + [out_of((2, width), F32), out_of((1, width), F32)],
        [thin] * 2 + [flat] + [whole(block)] * 2 + [whole((2, width)), whole((1, width))],
        8 * ROWS * width * 4 * hw,
        pieces[0].scratch + pieces[1].scratch + [pltpu.VMEM(block, BF)],
        places,
        {len(ins) - len(before) + 1 + k: k for k in range(len(before))},
    )
    return (d0, d1, dm1), [part.reshape(-1, width) for part in (mine, other)], (d_gain, d_gain_ffn)


def store_frames(out_ref, sums):
    frames, _, width = out_ref.shape
    both = [p.reshape(frames, 1, p.shape[0] // frames, width) for p in sums]
    out_ref[...] = jnp.concatenate(both, axis=1).reshape(frames, -1, width).astype(BF)


def output_body(halves, _, x0, x1, *refs):
    *refs, out_ref = refs
    pairs = [halves.pick(refs[k : k + 2]).astype(F32) for k in range(0, 8, 2)]
    sums = [x[...].astype(F32) + pairs[2 * c] + pairs[2 * c + 1] for c, x in enumerate((x0, x1))]
    store_frames(out_ref, sums)


def output_of(places, x, att, mlp, shape):
    frames, steps, width = shape
    halves = Halves(x[0].shape[0])
    sides = [a for c in range(2) for pair in (att[c], mlp[c]) for a in pair]
    cube = pl.BlockSpec((2 * ROWS // steps, steps, width), lambda i, p: (halves.block(i, p), 0, 0))
    return kernel_call(
        functools.partial(output_body, halves),
        halves.grid,
        [*x, *sides],
        [halves.both(width)] * 2 + halves.pair(width) * 4,
        [out_of(shape)],
        [cube],
        0,
        (),
        places,
    )[0]


def input_body(_, x0, x1, dm0, dm1, mine, other, gain_ref, *refs):
    sums = []
    dh = jnp.where(pl.program_id(0) == 0, other[...], mine[...]).astype(F32)
    for c, (x, dm) in enumerate(((x0, dm0), (x1, dm1))):
        rows = slice(c * ROWS, (c + 1) * ROWS)
        back, _ = norm_back(dh[rows], x[...].astype(F32), gain_ref[c : c + 1])
        sums.append(dm[...].astype(F32) + back)
    store_frames(refs[-1], sums)


def input_back(places, x, dm, dh, gain, part, before, shape):
    frames, steps, width = shape
    halves = Halves(x[0].shape[0])
    block = lambda i, p: halves.block(i * halves.count, p) + part
    flat = pl.BlockSpec((ROWS, width), lambda i, p: (block(i, p), 0))
    cube = pl.BlockSpec((2 * ROWS // steps, steps, width), lambda i, p: (block(i, p), 0, 0))
    ins = [*x, *dm, *dh, gain]
    specs = [flat] * 4 + [whole(d.shape) for d in dh] + [whole(gain.shape)]
    alias = {}
    if before is not None:
        ins.append(before)
        specs.append(HBM)
        alias = {len(ins): 0}
    return kernel_call(input_body, (2,), ins, specs, [out_of(shape)], [cube], 0, (), places, alias)[0]


def finish_body(layout, turned, *refs):
    count = 1 + max(k for terms, _ in layout for k in terms)
    ins, outs = refs[:count], refs[count:]
    own, wide = outs[0].shape[1:]
    for c, (terms, first) in enumerate(layout):
        rows = slice(first, first + own)
        for t, ref in enumerate(outs):
            cols = slice(t * wide, (t + 1) * wide)
            total = ins[terms[0]][rows, cols].astype(F32)
            for k in terms[1:]:
                total = total + ins[k][rows, cols].astype(F32)
            ref[c] = total.T if t == turned else total


def finish(sides, kinds, own):
    arrays, layout = [], []
    for terms, first in sides:
        spots = []
        for term in terms:
            found = [k for k, a in enumerate(arrays) if a is term]
            if not found:
                arrays.append(term)
            spots.append(found[0] if found else len(arrays) - 1)
        layout.append((spots, first))
    wide = arrays[0].shape[1] // kinds
    shapes = [(len(sides), own, wide)] * (kinds - 1) + [(len(sides), wide, own)]
    return kernel_call(
        functools.partial(finish_body, layout, kinds - 1),
        (1,),
        arrays,
        [whole(a.shape) for a in arrays],
        [out_of(s, F32) for s in shapes],
        [whole(s) for s in shapes],
        0,
    )


def add_body(one, a, two, b, one_out, two_out):
    one_out[...] = (one[...].astype(F32) + a[...].astype(F32)).astype(BF)
    two_out[...] = (two[...].astype(F32) + b[...].astype(F32)).astype(BF)


def add_ends(one, a, two, b):
    rows, width = a.shape
    first = pl.BlockSpec((rows, width), lambda i: (0, 0))
    last = pl.BlockSpec((rows, width), lambda i: (one.shape[0] // rows - 1, 0))
    return kernel_call(
        add_body,
        (1,),
        (one, a, two, b),
        [first, first, last, first],
        [out_of(one.shape)] * 2,
        [first, last],
        0,
        alias={0: 0, 2: 1},
    )


class Ring:
    def __init__(self, size):
        self.size = size
        self.rings = size <= 16
        half = size // 2
        order = [2 * q for q in range(half)] + [2 * (size - 1 - q) + 1 for q in range(half, size)]
        self.ahead = [(order[q], order[(q + 1) % size]) for q in range(size)]
        self.behind = [(b, a) for a, b in self.ahead]
        self.me = lax.axis_index("dp")
        place = jnp.where(self.me % 2 == 0, self.me // 2, size - 1 - self.me // 2)
        q = lax.rem(place + jnp.arange(size, dtype=jnp.int32), size)
        self.order = jnp.where(q < half, 2 * q, 2 * (size - 1 - q) + 1).astype(jnp.int32)


class Rounds:
    def __init__(self):
        self.done = ()

    def now(self, value):
        return lax.optimization_barrier((value, *self.done))[0] if self.done else value

    def close(self, *arrays):
        self.done = arrays


class Gather:
    def __init__(self, rounds, ring, shard):
        self.rounds, self.ring = rounds, ring
        self.a, self.b = [shard], [shard]

    def step(self):
        a, b = self.a[-1], self.b[-1]
        if len(self.a) == self.ring.size // 2:
            half = a.shape[0] // 2
            a, b = a[:half], b[half:]
        self.a.append(lax.ppermute(self.rounds.now(a), "dp", self.ring.ahead))
        self.b.append(lax.ppermute(self.rounds.now(b), "dp", self.ring.behind))
        return self.a[-1], self.b[-1]

    def entries(self, part=0, parts=1):
        n = self.ring.size
        own = self.a[0].shape[0] // parts
        found = []
        for t in range(n):
            if t != n // 2:
                found.append((self.b[t] if t < n // 2 else self.a[n - t], t, 0, part * own, own))
            elif parts == 1:
                found.append((self.a[t], t, 0, 0, own // 2))
                found.append((self.b[t], t, own // 2, 0, own // 2))
            else:
                found.append(((self.a[t], self.b[t])[part], t, 0, 0, own))
        return found, own


class Scatter:
    def __init__(self, rounds, ring, blocks):
        self.rounds, self.ring = rounds, ring
        far = ring.size // 2
        self.a, self.b = blocks[far], blocks[far + 1]
        self.blocks = [*blocks[:far], None, *blocks[far + 2 :]]
        self.k = far

    def step(self):
        n = self.ring.size
        if self.k < n // 2:
            one, two = self.blocks[self.k], self.blocks[n - self.k]
            if self.k == n // 2 - 1:
                self.a, self.b = add_ends(one, self.a, two, self.b)
            else:
                self.a = (one.astype(F32) + self.a.astype(F32)).astype(BF)
                self.b = (two.astype(F32) + self.b.astype(F32)).astype(BF)
        self.k -= 1
        self.a = lax.ppermute(self.rounds.now(self.a), "dp", self.ring.ahead)
        self.b = lax.ppermute(self.rounds.now(self.b), "dp", self.ring.behind)
        return self.a, self.b

    def terms(self):
        return [self.blocks[0], self.a, self.b]


class HeadSum:
    def __init__(self, rounds, pair):
        size = lax.axis_size("mp")
        self.rounds, self.pair, self.got = rounds, pair, []
        self.near_moves = [(i, i ^ 1) for i in range(size)]
        self.far_moves = [(i, i ^ 2) for i in range(size)]

    def add(self, one, two):
        return (one.astype(F32) + two.astype(F32)).astype(BF)

    def near_start(self):
        self.near_got = lax.ppermute(self.rounds.now(self.pair[1]), "mp", self.near_moves)
        return self.near_got

    def near_add(self, mine):
        self.mine = self.add(mine, self.near_got)
        return self.mine

    def near(self):
        self.near_start()
        return self.near_add(self.pair[0])

    def far(self, part=1.0):
        start = sum(got.shape[0] for got in self.got)
        rows = int(self.mine.shape[0] * part)
        moved = self.rounds.now(self.mine[start : start + rows])
        self.got.append(lax.ppermute(moved, "mp", self.far_moves))
        return self.got[-1]

    def last(self):
        got = [self.rounds.now(got) for got in self.got]
        self.mine = self.add(self.mine, jnp.concatenate(got, 0))
        self.sum = (self.mine, lax.ppermute(self.mine, "mp", self.near_moves))
        return self.sum[1]


def exchange_steps(axes):
    for axis in axes:
        size, step = lax.axis_size(axis), 1
        while step < size:
            yield axis, [(i, i ^ step) for i in range(size)], step
            step *= 2


def on_device(
    layer_input, frame_mask, gain_attn, w_query, w_key, w_value, w_out, gain_ffn, w_gate, w_up,
    w_down, cotangent,
):
    sets, width = gain_attn.shape[0], layer_input.shape[2]
    shape = layer_input.shape
    each = shape[1] // sets
    ring = Ring(lax.axis_size("dp"))
    rings, n = ring.rings, ring.size
    far = n // 2 if rings else 0
    own = width // n
    places = jnp.concatenate([ring.order, (lax.axis_index("mp") % 2).astype(jnp.int32)[None]])
    gather = lambda value: lax.all_gather(value, "dp", tiled=True)
    scatter = lambda value: lax.psum_scatter(value, "dp", scatter_dimension=0, tiled=True)
    rounds = Rounds()
    now, close = rounds.now, rounds.close

    attn_own = pack_attn(w_query, w_key, w_value, w_out)
    small = jnp.concatenate([gain_attn, gain_ffn], 0).astype(F32)[None]
    steps = list(exchange_steps(("dp",)))
    ffn_own, x, g = [], [], []

    def gain_step(value):
        axis, moves, step = steps.pop(0)
        other = lax.ppermute(now(value), axis, moves)
        bit = (ring.me // step) % 2
        both = [jnp.concatenate(pair, 0) for pair in ((value, other), (other, value))]
        return jnp.where(bit == 0, *both)

    masks = frame_mask.astype(BF)[:, None, None]
    chores = [
        lambda: ffn_own.append(pack_ffn(now(w_gate), w_up, w_down, 0)),
        lambda: x.append(split_sets(now(layer_input), sets)[0]),
        lambda: ffn_own.append(pack_ffn(now(w_gate), w_up, w_down, 1)),
        lambda: x.append(split_sets(now(layer_input), sets)[1]),
        lambda: g.append(split_sets(now(cotangent) * masks, sets)[0]),
        lambda: g.append(split_sets(now(cotangent) * masks, sets)[1]),
    ]
    attn = Gather(rounds, ring, attn_own)
    for k in range(max(far, 3)):
        moved = attn.step() if rings else ()
        if rings and k == far - 1:
            rows = [Gather(rounds, ring, shard) for shard in ffn_own]
            moved += rows[0].step()
        for chore in chores[:2]:
            chore()
        del chores[:2]
        if steps and k != 2:
            small = gain_step(small)
        close(small, *moved, *[v[-1] for v in (ffn_own, x, g) if v])
    while steps:
        small = gain_step(small)
    gains = small.transpose(1, 0, 2).reshape(2 * sets, width)
    g_attn, g_ffn = [[gains[k * sets + c][None] for c in range(sets)] for k in range(2)]
    if rings:
        w_attn = [attn.entries(c, sets) for c in range(sets)]
    else:
        both = gather(attn_own).reshape(n, sets, own, -1)
        w_attn = [([(both[:, c].reshape(width, -1), None, 0, 0, width)], width) for c in range(sets)]

    def move(c):
        return rows[c].step() if rings else ()

    def weights(c):
        if rings:
            return rows[c].entries()
        return [(gather(ffn_own[c]), None, 0, 0, width)], width

    h1, qkv, mixed, heads = [None] * 2, [None] * 2, [None] * 2, [None] * 2
    moved = move(0)
    h1[0], qkv[0], mixed[0], part = attend(now(places), x[0], g_attn[0], None, w_attn[0], each)
    heads[0] = HeadSum(rounds, part)
    close(*moved, part[0])
    moved = move(0)
    heads[0].near()
    got = heads[0].far()
    h1[1], qkv[1], mixed[1], part = attend(now(places), x[1], g_attn[1], qkv[0], w_attn[1], each)
    heads[1] = HeadSum(rounds, part)
    held, rounds.done = rounds.done, (*rounds.done, part[0])
    moved += move(0)
    rounds.done = held
    close(*moved, part[0], got)
    moved = move(1)
    close(heads[1].near(), heads[0].last())

    def grads_of(c, out):
        columns = [(out[0], out[2]), (g[c], out[1])]
        return weight_grads(now(places), [columns], far)

    dh, mlp, grads, dm, d_gain_ffn = ([None] * 2 for _ in range(5))
    got = heads[1].far(0.5)
    ffn = (x[0], heads[0].sum, g[0], g_ffn[0], weights(0))
    out, dh_other, mlp_other = hidden_units(now(places), *ffn, half=1)
    close(*moved, dh_other, got)
    moved = move(1)
    got = heads[1].far(0.5)
    dh[0] = HeadSum(rounds, (None, dh_other))
    mlp[0] = HeadSum(rounds, (None, mlp_other))
    near = dh[0].near_start(), mlp[0].near_start()
    out, dh_mine, mlp_mine = hidden_units(now(places), *ffn, half=0, filled=out)
    close(*moved, dh_mine, got, *near)
    dh[0].near_add(dh_mine)
    mlp[0].near_add(mlp_mine)
    moved = move(1)
    got = dh[0].far(0.5)
    grads[0] = grads_of(0, out)
    close(*moved, grads[0][0], got, heads[1].last())
    att = [head.sum for head in heads]
    sums = [Scatter(rounds, ring, grads[0])] if rings else []
    add = lambda k: sums[k].step() if rings else ()
    close(*move(1), *add(0), dh[0].far(0.5))

    moved = (*add(0), dh[0].last())
    got = mlp[0].far(0.5)
    ffn = (x[1], att[1], g[1], g_ffn[1], weights(1))
    out, dh_other, mlp_other = hidden_units(now(places), *ffn, half=1)
    close(*moved, dh_other, got)
    moved = add(0)
    got = mlp[0].far(0.5)
    dh[1] = HeadSum(rounds, (None, dh_other))
    mlp[1] = HeadSum(rounds, (None, mlp_other))
    near = dh[1].near_start(), mlp[1].near_start()
    out, dh_mine, mlp_mine = hidden_units(now(places), *ffn, half=0, filled=out)
    close(*moved, dh_mine, got, *near)
    dh[1].near_add(dh_mine)
    mlp[1].near_add(mlp_mine)
    moved = add(0)
    got = dh[1].far()
    grads[1] = grads_of(1, out)
    if rings:
        sums.append(Scatter(rounds, ring, grads[1]))
        moved += add(1)
    dm[0], d_gain_ffn[0] = middle_back(now(places), x[0], att[0], g[0], dh[0].sum, g_ffn[0])
    close(*moved, grads[1][0], dm[0], got)
    close(dh[1].last(), mlp[0].last())

    moved = add(1)
    got = mlp[1].far(0.75)
    backward = (x, g[1], dm[0], att[1], dh[1].sum, g_ffn[1], qkv, w_attn)
    found, part, d_gain0 = attend_back(now(places), *backward, 0, (), each)
    back = [HeadSum(rounds, part)]
    close(*moved, part[0], got)
    moved = (*add(1), back[0].near(), mlp[1].far(0.25))
    (*d_qkv, dm[1]), part, d_gain1 = attend_back(now(places), *backward, 1, found, each)
    back.append(HeadSum(rounds, part))
    close(*moved, part[0])

    shared = lax.axis_size("mp")
    d_gain_attn, d_gain_ffn[1] = (one + two for one, two in zip(d_gain0, d_gain1))
    d_gains = jnp.concatenate([d_gain_attn, *[d / shared for d in d_gain_ffn]], 0)
    steps = list(exchange_steps(("mp", "dp")))

    def sum_step(value, *earlier):
        axis, moves, _ = steps.pop(0)
        got = lax.ppermute(now(value), axis, moves)
        return value + lax.optimization_barrier((got, *earlier))[0]

    moved = (*add(1), back[1].near())
    got = back[0].far(0.75)
    d_gains = sum_step(sum_step(d_gains))
    runs = [[(h1[c], d_qkv[c]), (dm[c], mixed[c])] for c in range(sets)]
    if rings:
        blocks = weight_grads(now(places), runs, far)
        sums.append(Scatter(rounds, ring, blocks))
    else:
        blocks = [weight_grads(now(places), [run], far)[0] for run in runs]
    close(*moved, blocks[0], got, d_gains)
    moved = (*add(2), mlp[1].last())
    got = back[0].far(0.25)
    d_gains = sum_step(d_gains)
    if rings:
        ffn_sums = [([now(t) for t in s.terms()], 0) for s in sums[:2]]
    else:
        ffn_sums = [([scatter(b[0])], 0) for b in grads]
    d_gate_w, d_up_w, d_down_w = finish(ffn_sums, 3, own)
    close(*moved, d_gains, d_gate_w, got)
    moved = (*add(2), back[0].last())
    d_gains = sum_step(d_gains)
    got = back[1].far(0.5)
    output = output_of(now(places), x, att, [m.sum for m in mlp], shape)
    close(*moved, d_gains, got, output)
    moved = add(2)
    while steps:
        d_gains = sum_step(d_gains)
    got = back[1].far(0.5)
    grad_input = input_back(now(places), x, dm, back[0].sum, gains[:sets], 0, None, shape)
    close(*moved, grad_input, d_gains, got)
    moved = add(2)
    back[1].last()
    grad_input = input_back(now(places), x, dm, back[1].sum, gains[:sets], 1, grad_input, shape)
    close(*moved, grad_input)
    if rings:
        terms = [now(t) for t in sums[2].terms()]
        attn_sums = [(terms, c * own) for c in range(sets)]
    else:
        attn_sums = [([scatter(b)], 0) for b in blocks]
    d_query, d_key, d_value, d_out = finish(attn_sums, 4, own)
    d_gains = lax.dynamic_slice_in_dim(d_gains, ring.me * own, own, 1)
    return (
        output, grad_input, d_gains[:sets], d_query, d_key, d_value, d_out,
        d_gains[sets:], d_gate_w, d_up_w, d_down_w,
    )


def solution(mesh):
    rows = P("dp", None, None)
    gain = P(None, "dp")
    into = P(None, "dp", "mp")
    back = P(None, "mp", "dp")
    weights = (gain, into, into, into, back, gain, into, into, back)
    return jax.shard_map(
        on_device,
        mesh=mesh,
        in_specs=(rows, P("dp"), *weights, rows),
        out_specs=(rows, rows, *weights),
        check_vma=False,
    )
```

```python
import functools

import jax
import jax.numpy as jnp
from jax import lax
from jax.experimental import pallas as pl
from jax.experimental.pallas import tpu as pltpu
from jax.sharding import PartitionSpec as P

HDIM = 64
EPS = 1e-05
NEG = -1e30
BF = jnp.bfloat16
F32 = jnp.float32
NN = (((1,), (0,)), ((), ()))
NT = (((1,), (1,)), ((), ()))
TN = (((0,), (0,)), ((), ()))
MIB = 1024 * 1024
SUB = 128
PAIR = 2 * HDIM
ROWS = 256
HBM = pl.BlockSpec(memory_space=pl.ANY)


def mm(left, right, dims=NN):
    return lax.dot_general(left, right, dims, preferred_element_type=F32)


def kernel_call(body, grid, ins, in_specs, outs, out_specs, flops, scratch=(), scalars=None, alias=None):
    moved = sum(a.size * a.dtype.itemsize for a in ins) + sum(
        o.size * jnp.dtype(o.dtype).itemsize for o in outs
    )
    spec = pltpu.PrefetchScalarGridSpec(
        num_scalar_prefetch=0 if scalars is None else 1,
        grid=grid,
        in_specs=in_specs,
        out_specs=out_specs,
        scratch_shapes=scratch,
    )
    args = ins if scalars is None else (scalars, *ins)
    return pl.pallas_call(
        body,
        grid_spec=spec,
        out_shape=outs,
        input_output_aliases=alias or {},
        compiler_params=pltpu.CompilerParams(vmem_limit_bytes=56 * MIB),
        cost_estimate=pl.CostEstimate(flops=500000000, bytes_accessed=1, transcendentals=0),
    )(*args)


def whole(shape):
    return pl.BlockSpec(shape, lambda *i: (0,) * len(shape))


def rows_of(rows, width, start=0):
    return pl.BlockSpec((rows, width), lambda i, *_: (i + start, 0))


def out_of(shape, kind=BF):
    return jax.ShapeDtypeStruct(shape, kind)


class Halves:
    def __init__(self, tokens):
        self.count = tokens // 2 // ROWS
        self.grid = (2 * self.count,)

    def block(self, i, places):
        half = (1 - i // self.count + places[places.shape[0] - 1]) % 2
        return half * self.count + i % self.count

    def both(self, width):
        return pl.BlockSpec((ROWS, width), lambda i, p: (self.block(i, p), 0))

    def pair(self, width):
        return [
            pl.BlockSpec((ROWS, width), lambda i, p: (jnp.maximum(i - self.count, 0), 0)),
            pl.BlockSpec((ROWS, width), lambda i, p: (jnp.minimum(i, self.count - 1), 0)),
        ]

    def pick(self, pair):
        return jnp.where(pl.program_id(0) < self.count, pair[1][...], pair[0][...])

    def one(self, width, half):
        shift = 0 if half else self.count
        return pl.BlockSpec((ROWS, width), lambda i, p: (self.block(i + shift, p), 0))

    def put(self, pair, value):
        pair[0][...] = value

        @pl.when(pl.program_id(0) < self.count)
        def _():
            pair[1][...] = pair[0][...]


def split_sets(value, sets):
    frames, steps, width = value.shape
    parts = value.reshape(frames, sets, steps // sets, width)
    return [parts[:, c].reshape(-1, width) for c in range(sets)]


def pack_attn_body(wq, wk, wv, wo, out):
    own, hw = wq.shape[1:]
    for c in range(2):
        rows = slice(c * own, (c + 1) * own)
        for t, w in enumerate((wq, wk, wv)):
            out[rows, t * hw : (t + 1) * hw] = w[c]
        out[rows, 3 * hw :] = wo[c].T


def pack_attn(wq, wk, wv, wo):
    sets, own, hw = wq.shape
    piece = (sets * own, 4 * hw)
    return kernel_call(
        pack_attn_body,
        (1,),
        (wq, wk, wv, wo),
        [whole(w.shape) for w in (wq, wk, wv, wo)],
        [out_of(piece)],
        [whole(piece)],
        0,
    )[0]


def pack_ffn_body(wg, wu, wd, out):
    units = wg.shape[2]
    out[:, :units] = wg[0]
    out[:, units : 2 * units] = wu[0]
    out[:, 2 * units :] = wd[0].T


def pack_ffn(wg, wu, wd, c):
    own, units = wg.shape[1:]
    piece = (own, 3 * units)
    into = pl.BlockSpec((1, own, units), lambda i: (c, 0, 0))
    back = pl.BlockSpec((1, units, own), lambda i: (c, 0, 0))
    return kernel_call(
        pack_ffn_body,
        (1,),
        (wg, wu, wd),
        [into, into, back],
        [out_of(piece)],
        [whole(piece)],
        0,
    )[0]


def norm(value):
    scale = lax.rsqrt(jnp.mean(value * value, axis=-1, keepdims=True) + EPS)
    return value * scale, scale


def lanes_low(shape):
    return lax.broadcasted_iota(jnp.int32, shape, 1) < HDIM


def stack_heads(pair):
    low = lanes_low(pair.shape)
    zero = jnp.zeros_like(pair)
    return jnp.concatenate([jnp.where(low, pair, zero), jnp.where(low, zero, pair)], axis=0)


def pick_heads(stacked):
    half = stacked.shape[0] // 2
    low = lanes_low((half, stacked.shape[1]))
    return jnp.where(low, stacked[:half], stacked[half:])


def hidden_keys(rows, keys, steps, turned=False):
    shape, axis = ((keys, rows), 1) if turned else ((rows, keys), 0)
    row = lax.broadcasted_iota(jnp.int32, shape, axis) & (SUB - 1)
    spot = lax.broadcasted_iota(jnp.int32, shape, 1 - axis)
    key = spot & (SUB - 1)
    shift = steps.bit_length() - 1
    seen = lax.shift_right_logical(row, shift) == lax.shift_right_logical(key, shift)
    own = spot >= keys - SUB
    seen = seen & ((row >= key) | jnp.logical_not(own))
    return jnp.where(seen, 0.0, NEG)


def softmax(query, keys, hidden):
    raw = mm(query, keys, NT) + hidden
    power = jnp.exp(raw - jnp.max(raw, axis=-1, keepdims=True))
    return power * (1.0 / jnp.sum(power, axis=-1, keepdims=True))


def softmax_turned(query, keys, hidden):
    raw = mm(keys, query, NT) + hidden
    power = jnp.exp(raw - jnp.max(raw, axis=0, keepdims=True))
    return power * (1.0 / jnp.sum(power, axis=0, keepdims=True))


class Pieces:
    def __init__(self, entries, own, groups):
        self.entries = entries
        self.own = own
        self.groups = groups
        self.arrays = []
        for array, *_ in entries:
            if not any(array is a for a in self.arrays):
                self.arrays.append(array)
        self.count = len(self.arrays)
        self.shape = (sum(e[4] for e in entries), entries[0][0].shape[1])
        self.scratch = [pltpu.VMEM(self.shape, BF), pltpu.SemaphoreType.DMA((groups, len(entries)))]

    def copies(self, refs, places, memory, sems, group):
        wide = self.shape[1] // self.groups
        cols = pl.ds(group * wide, wide)
        for k, (array, slot, row, first, rows) in enumerate(self.entries):
            ref = [r for r, a in zip(refs, self.arrays) if a is array][0]
            start = row if slot is None else pl.multiple_of(places[slot] * self.own + row, rows)
            source = ref.at[pl.ds(first, rows), cols]
            yield pltpu.make_async_copy(source, memory.at[pl.ds(start, rows), cols], sems.at[group, k])

    def start(self, refs, places, memory, sems, order):
        @pl.when(pl.program_id(0) == 0)
        def _():
            for group in order:
                for copy in self.copies(refs, places, memory, sems, group):
                    copy.start()

    def wait(self, refs, places, memory, sems, group):
        @pl.when(pl.program_id(0) == 0)
        def _():
            for copy in self.copies(refs, places, memory, sems, group):
                copy.wait()


def attend_body(pieces, halves, steps, hw, later, filled, places, *refs):
    x_ref, gain_ref, *refs = refs
    if later:
        before_ref, *refs = refs
    w_refs, refs = refs[: pieces.count], refs[pieces.count :]
    h_ref, qkv_ref, mixed_ref, *part_refs, w_ref, sems = refs[filled:]
    pieces.start(w_refs, places, w_ref, sems, range(1))
    normed, _ = norm(x_ref[...].astype(F32))
    hidden = (normed * gain_ref[...]).astype(BF)
    h_ref[...] = hidden
    pieces.wait(w_refs, places, w_ref, sems, 0)
    qkv = mm(hidden, w_ref[:, : 3 * hw]).astype(BF)
    qkv_ref[...] = qkv
    scale = jnp.asarray(HDIM ** (-0.5), BF)
    hidden_scores = hidden_keys(2 * SUB, 2 * SUB if later else SUB, steps)
    for s in range(x_ref.shape[0] // SUB):
        rows = slice(s * SUB, (s + 1) * SUB)
        for j in range(hw // PAIR):
            q, k, v = (qkv[rows, t * hw + j * PAIR : t * hw + (j + 1) * PAIR] for t in range(3))
            if later:
                k_old, v_old = (
                    before_ref[rows, t * hw + j * PAIR : t * hw + (j + 1) * PAIR] for t in (1, 2)
                )
                k = jnp.concatenate([k_old, k], axis=0)
                v = jnp.concatenate([v_old, v], axis=0)
            probs = softmax(stack_heads(q) * scale, k, hidden_scores).astype(BF)
            mixed_ref[rows, j * PAIR : (j + 1) * PAIR] = pick_heads(mm(probs, v)).astype(BF)
    part = mm(mixed_ref[...], w_ref[:, 3 * hw :], NT).astype(BF)
    if len(part_refs) == 2:
        halves.put(part_refs, part)
    else:
        part_refs[0][...] = part


def attend(places, x, gain, before, w, steps, half=None, filled=()):
    tokens, width = x.shape
    pieces, halves = Pieces(*w, 1), Halves(tokens)
    hw = pieces.shape[1] // 4
    spec = halves.both if half is None else functools.partial(halves.one, half=half)
    ins = [x, gain]
    specs = [spec(width), whole(gain.shape)]
    if before is not None:
        ins.append(before)
        specs.append(spec(3 * hw))
    ins += [*pieces.arrays, *filled]
    specs += [HBM] * (pieces.count + len(filled))
    widths = (width, 3 * hw, hw)
    *out, part = kernel_call(
        functools.partial(attend_body, pieces, halves, steps, hw, before is not None, len(filled)),
        halves.grid if half is None else (halves.count,),
        ins,
        specs,
        [out_of((tokens, n)) for n in widths] + [out_of((tokens // 2, width))] * (2 if half is None else 1),
        [spec(n) for n in widths] + (halves.pair(width) if half is None else [rows_of(ROWS, width)]),
        2 * tokens * width * 4 * hw,
        pieces.scratch,
        places,
        {len(ins) - len(filled) + 1 + k: k for k in range(len(filled))},
    )
    if half is None:
        return *out[:3], (out[3], part)
    return *out, part


def units_body(pieces, halves, units, half, filled, places, x_ref, *refs):
    if half is None:
        att0, att1, *refs = refs
        att = halves.pick((att0, att1))
    else:
        att_ref, *refs = refs
        att = att_ref[...]
    g_ref, gain_ref, *refs = refs
    w_refs, refs = refs[: pieces.count], refs[pieces.count + filled :]
    h_ref, inner_ref, dboth_ref, *sum_refs, w_ref, sems = refs
    pieces.start(w_refs, places, w_ref, sems, (2, 0, 1))
    normed, _ = norm(x_ref[...].astype(F32) + att.astype(F32))
    hidden = (normed * gain_ref[...]).astype(BF)
    h_ref[...] = hidden
    cut = 256
    cols = [
        [slice(t * units + u * cut, t * units + (u + 1) * cut) for t in range(3)] for u in range(units // cut)
    ]
    pieces.wait(w_refs, places, w_ref, sems, 2)
    d_inners = [mm(g_ref[...], w_ref[:, c[2]]) for c in cols]
    pieces.wait(w_refs, places, w_ref, sems, 0)
    pieces.wait(w_refs, places, w_ref, sems, 1)
    for c, d_inner in zip(cols, d_inners):
        gate = mm(hidden, w_ref[:, c[0]])
        up = mm(hidden, w_ref[:, c[1]])
        sigma = 1.0 / (1.0 + jnp.exp(-gate))
        active = gate * sigma
        inner_ref[:, c[0]] = (active * up).astype(BF)
        dboth_ref[:, c[1]] = (d_inner * active).astype(BF)
        dboth_ref[:, c[0]] = (d_inner * up * (sigma + active * (1.0 - sigma))).astype(BF)
    d_hidden = mm(dboth_ref[...], w_ref[:, : 2 * units], NT).astype(BF)
    if half is None:
        halves.put(sum_refs[:2], d_hidden)
        halves.put(sum_refs[2:], mm(inner_ref[...], w_ref[:, 2 * units :], NT).astype(BF))
    else:
        sum_refs[0][0] = d_hidden
        sum_refs[0][1] = mm(inner_ref[...], w_ref[:, 2 * units :], NT).astype(BF)


def hidden_units(places, x, att, g, gain, w, half=None, filled=()):
    tokens, width = x.shape
    pieces, halves = Pieces(*w, 3), Halves(tokens)
    units = pieces.shape[1] // 3
    spec = halves.both if half is None else functools.partial(halves.one, half=half)
    part = spec(width)
    widths = (width, units, 2 * units)
    sides = [*att, g, gain] if half is None else [att[half], g, gain]
    side_specs = halves.pair(width) if half is None else [rows_of(ROWS, width)]
    ins = [x, *sides, *pieces.arrays, *filled]
    out = kernel_call(
        functools.partial(units_body, pieces, halves, units, half, len(filled)),
        halves.grid if half is None else (halves.count,),
        ins,
        [part, *side_specs, part, whole(gain.shape)] + [HBM] * (pieces.count + len(filled)),
        [out_of((tokens, n)) for n in widths]
        + ([out_of((tokens // 2, width))] * 4 if half is None else [out_of((2, tokens // 2, width))]),
        [spec(n) for n in widths] + (halves.pair(width) * 2 if half is None else [pl.BlockSpec((2, ROWS, width), lambda i, p: (0, i, 0))]),
        12 * tokens * width * units,
        pieces.scratch,
        places,
        {len(ins) - len(filled) + 1 + k: k for k in range(len(filled))},
    )
    if half is None:
        return *out[:3], tuple(out[3:5]), tuple(out[5:])
    return out[:3], *out[3:]


def grads_body(runs, cut, steps, places, *refs):
    inputs = max(right for columns in runs for _, right in columns) + 1
    ins, outs = refs[:inputs], refs[inputs:]
    values = []
    for columns in runs:
        values.append([])
        for slots, k in columns:
            rows = [ins[s][...] for s in slots]
            rows = jnp.concatenate(rows, axis=1) if len(rows) > 1 else rows[0]
            values[-1].append(mm(rows, ins[k][...], TN).astype(BF))
    if not cut:
        at = 0
        for value in values[0]:
            outs[0][:, at : at + value.shape[1]] = value
            at += value.shape[1]
        return
    *outs, buffer, sems = outs
    height = outs[0].shape[0]
    own = height // len(runs)
    slots = ROWS // own

    def copies(block):
        at = 0
        for k in range(slots):
            t = block * slots + k
            for ref in outs[t : t + 1] if t < cut else outs[t : t + 2] if t == cut else outs[t + 1 : t + 2]:
                rows = buffer.at[block % 2, pl.ds(at, ref.shape[0])]
                yield pltpu.make_async_copy(rows, ref, sems.at[block % 2, at // (height // 2)])
                at += ref.shape[0]

    for block in range(steps):

        @pl.when(pl.program_id(0) == block)
        def _():
            if block >= 2:
                for copy in copies(block - 2):
                    copy.wait()
            for k in range(slots):
                for r, columns in enumerate(values):
                    at = 0
                    first = (k * len(runs) + r) * own
                    for value in columns:
                        cols = slice(at, at + value.shape[1])
                        buffer[block % 2, first : first + own, cols] = value[k * own : (k + 1) * own]
                        at += value.shape[1]
            for copy in copies(block):
                copy.start()
            if block == steps - 1:
                for last in range(max(0, steps - 2), steps):
                    for copy in copies(last):
                        copy.wait()


def weight_grads(places, runs, cut):
    count = places.shape[0] - 1
    tokens, width = runs[0][0][0].shape
    own = width // count
    steps = width // ROWS
    slots = ROWS // own if cut else 1
    ins, specs, marks = [], [], []
    for columns in runs:
        for left, _ in columns:
            mark = []
            for k in range(slots):
                place = (lambda i, p, k=k: (0, p[i * slots + k])) if cut else (lambda i, p: (0, i))
                ins.append(left)
                specs.append(pl.BlockSpec((tokens, ROWS // slots), place))
                mark.append(len(ins) - 1)
            marks.append(tuple(mark))
    pairs = []
    for columns in runs:
        pairs.append([])
        for _, right in columns:
            ins.append(right)
            specs.append(whole(right.shape))
            pairs[-1].append((marks.pop(0), len(ins) - 1))
    total = sum(right.shape[1] for _, right in runs[0])
    if cut:
        height = own * len(runs)
        heights = [height] * cut + [height // 2] * 2 + [height] * (count - cut - 1)
        outs = [out_of((h, total)) for h in heights]
        out_specs = [HBM] * len(outs)
        scratch = [
            pltpu.VMEM((2, slots * height, total), BF),
            pltpu.SemaphoreType.DMA((2, 2 * slots)),
        ]
    else:
        outs, out_specs, scratch = [out_of((width, total))], [rows_of(ROWS, total)], []
    return kernel_call(
        functools.partial(grads_body, pairs, cut, steps),
        (steps,),
        ins,
        specs,
        outs,
        out_specs,
        2 * tokens * width * total,
        scratch,
        places,
    )


def norm_back(grad_hidden, value, gain):
    normed, scale = norm(value)
    scaled = grad_hidden * gain
    back = scale * (scaled - normed * jnp.mean(scaled * normed, axis=-1, keepdims=True))
    return back, jnp.sum(grad_hidden * normed, axis=0, keepdims=True)


def add_up(ref, value):
    @pl.when(pl.program_id(0) == 0)
    def _():
        ref[...] = jnp.zeros_like(ref)

    ref[...] += value


def middle_body(halves, _, x_ref, att0, att1, g_ref, dh0, dh1, gain_ref, dm_ref, dgain_ref):
    value = x_ref[...].astype(F32) + halves.pick((att0, att1)).astype(F32)
    back, d_gain = norm_back(halves.pick((dh0, dh1)).astype(F32), value, gain_ref[...])
    dm_ref[...] = (g_ref[...].astype(F32) + back).astype(BF)
    add_up(dgain_ref, d_gain)


def middle_back(places, x, att, g, dh, gain):
    tokens, width = x.shape
    halves = Halves(tokens)
    part, pair = halves.both(width), halves.pair(width)
    return kernel_call(
        functools.partial(middle_body, halves),
        halves.grid,
        (x, *att, g, *dh, gain),
        [part, *pair, part, *pair, whole(gain.shape)],
        [out_of((tokens, width)), out_of((1, width), F32)],
        [part, whole((1, width))],
        0,
        (),
        places,
    )


def attend_back_body(pieces, shared, steps, hw, places, x0, x1, g1, dm0, att0, att1, dh0, dh1, gain, qkv0, qkv1, *refs):
    sides = [
        [r for a in p.arrays for r, b in zip(refs, shared.arrays) if a is b] for p in pieces
    ]
    dqkv0, dqkv1, dm1, mine, other, dgain, dgain_ffn, w0, sems0, w1, sems1, d_hidden = refs[-12:]
    for p, s, w, sems in zip(pieces, sides, (w0, w1), (sems0, sems1)):
        p.start(s, places, w, sems, range(1))
    first = pl.program_id(0) == 0
    value = x1[...].astype(F32) + jnp.where(first, att1[...], att0[...]).astype(F32)
    back, d_gain = norm_back(jnp.where(first, dh1[...], dh0[...]).astype(F32), value, gain[...])
    dm1[...] = (g1[...].astype(F32) + back).astype(BF)
    add_up(dgain_ffn, d_gain)
    normed = [norm(x[...].astype(F32))[0] for x in (x0, x1)]
    for p, s, w, sems in zip(pieces, sides, (w0, w1), (sems0, sems1)):
        p.wait(s, places, w, sems, 0)
    scale = HDIM ** (-0.5)
    low_scale = jnp.asarray(scale, BF)
    hidden = [hidden_keys(2 * SUB, (1 + c) * SUB, steps, True) for c in range(2)]
    d_mixed = [mm(d[...], w[:, 3 * hw :]).astype(BF) for d, w in ((dm0, w0), (dm1, w1))]
    for s in range(dm0.shape[0] // SUB):
        rows = slice(s * SUB, (s + 1) * SUB)
        for j in range(hw // PAIR):
            cols = [slice(t * hw + j * PAIR, t * hw + (j + 1) * PAIR) for t in range(3)]
            q0, k0, v0 = (qkv0[rows, c] for c in cols)
            q1, k1, v1 = (qkv1[rows, c] for c in cols)
            keys = (k0, jnp.concatenate([k0, k1], axis=0))
            values = (v0, jnp.concatenate([v0, v1], axis=0))
            d_k, d_v = [], []
            for c, (q, out_ref) in enumerate(((q0, dqkv0), (q1, dqkv1))):
                q_two = stack_heads(q) * low_scale
                d_two = stack_heads(d_mixed[c][rows, cols[0]])
                soft = softmax_turned(q_two, keys[c], hidden[c])
                d_probs = mm(values[c], d_two, NT)
                inside = jnp.sum(soft * d_probs, axis=0, keepdims=True)
                d_scores = (soft * (d_probs - inside)).astype(BF)
                d_q = pick_heads(mm(d_scores, keys[c], TN)) * scale
                out_ref[rows, cols[0]] = d_q.astype(BF)
                d_k.append(mm(d_scores, q_two))
                d_v.append(mm(soft.astype(BF), d_two))
            dqkv0[rows, cols[1]] = (d_k[0] + d_k[1][:SUB]).astype(BF)
            dqkv1[rows, cols[1]] = d_k[1][SUB:].astype(BF)
            dqkv0[rows, cols[2]] = (d_v[0] + d_v[1][:SUB]).astype(BF)
            dqkv1[rows, cols[2]] = d_v[1][SUB:].astype(BF)
    gains = []
    for c, (d, w) in enumerate(((dqkv0, w0), (dqkv1, w1))):
        grad = mm(d[...], w[:, : 3 * hw], NT)
        gains.append(jnp.sum(grad * normed[c], axis=0, keepdims=True))
        d_hidden[c] = grad.astype(BF)

    for k, ref in enumerate((other, mine)):

        @pl.when(pl.program_id(0) == k)
        def _():
            ref[...] = d_hidden[...]

    add_up(dgain, jnp.concatenate(gains, axis=0))


def attend_back(places, x, g1, dm0, att1, dh1, gain, qkv, w, part, before, steps):
    tokens, width = dm0.shape
    halves = Halves(tokens)
    pieces = [Pieces(*side, 1) for side in w]
    shared = Pieces(w[0][0] + w[1][0], w[0][1], 1)
    hw = pieces[0].shape[1] // 4
    spot = lambda i, p: (halves.block(i * halves.count, p) + part, 0)
    flat, thin = pl.BlockSpec((ROWS, width), spot), pl.BlockSpec((ROWS, 3 * hw), spot)
    sums = pl.BlockSpec((ROWS, width), lambda i, p: (part, 0))
    block = (2, ROWS, width)
    ins = [*x, g1, dm0, *att1, *dh1, gain, *qkv, *shared.arrays, *before]
    specs = [flat] * 4 + [sums] * 4 + [whole(gain.shape)] + [thin] * 2
    d0, d1, dm1, mine, other, d_gain, d_gain_ffn = kernel_call(
        functools.partial(attend_back_body, pieces, shared, steps, hw),
        (2,),
        ins,
        specs + [HBM] * (len(ins) - len(specs)),
        [out_of((tokens, 3 * hw))] * 2
        + [out_of((tokens, width))]
        + [out_of(block)] * 2
        + [out_of((2, width), F32), out_of((1, width), F32)],
        [thin] * 2 + [flat] + [whole(block)] * 2 + [whole((2, width)), whole((1, width))],
        8 * ROWS * width * 4 * hw,
        pieces[0].scratch + pieces[1].scratch + [pltpu.VMEM(block, BF)],
        places,
        {len(ins) - len(before) + 1 + k: k for k in range(len(before))},
    )
    return (d0, d1, dm1), [part.reshape(-1, width) for part in (mine, other)], (d_gain, d_gain_ffn)


def store_frames(out_ref, sums):
    frames, _, width = out_ref.shape
    both = [p.reshape(frames, 1, p.shape[0] // frames, width) for p in sums]
    out_ref[...] = jnp.concatenate(both, axis=1).reshape(frames, -1, width).astype(BF)


def output_body(halves, _, x0, x1, *refs):
    *refs, out_ref = refs
    pairs = [halves.pick(refs[k : k + 2]).astype(F32) for k in range(0, 8, 2)]
    sums = [x[...].astype(F32) + pairs[2 * c] + pairs[2 * c + 1] for c, x in enumerate((x0, x1))]
    store_frames(out_ref, sums)


def output_of(places, x, att, mlp, shape):
    frames, steps, width = shape
    halves = Halves(x[0].shape[0])
    sides = [a for c in range(2) for pair in (att[c], mlp[c]) for a in pair]
    cube = pl.BlockSpec((2 * ROWS // steps, steps, width), lambda i, p: (halves.block(i, p), 0, 0))
    return kernel_call(
        functools.partial(output_body, halves),
        halves.grid,
        [*x, *sides],
        [halves.both(width)] * 2 + halves.pair(width) * 4,
        [out_of(shape)],
        [cube],
        0,
        (),
        places,
    )[0]


def input_body(_, x0, x1, dm0, dm1, mine, other, gain_ref, *refs):
    sums = []
    dh = jnp.where(pl.program_id(0) == 0, other[...], mine[...]).astype(F32)
    for c, (x, dm) in enumerate(((x0, dm0), (x1, dm1))):
        rows = slice(c * ROWS, (c + 1) * ROWS)
        back, _ = norm_back(dh[rows], x[...].astype(F32), gain_ref[c : c + 1])
        sums.append(dm[...].astype(F32) + back)
    store_frames(refs[-1], sums)


def input_back(places, x, dm, dh, gain, part, before, shape):
    frames, steps, width = shape
    halves = Halves(x[0].shape[0])
    block = lambda i, p: halves.block(i * halves.count, p) + part
    flat = pl.BlockSpec((ROWS, width), lambda i, p: (block(i, p), 0))
    cube = pl.BlockSpec((2 * ROWS // steps, steps, width), lambda i, p: (block(i, p), 0, 0))
    ins = [*x, *dm, *dh, gain]
    specs = [flat] * 4 + [whole(d.shape) for d in dh] + [whole(gain.shape)]
    alias = {}
    if before is not None:
        ins.append(before)
        specs.append(HBM)
        alias = {len(ins): 0}
    return kernel_call(input_body, (2,), ins, specs, [out_of(shape)], [cube], 0, (), places, alias)[0]


def finish_body(layout, turned, *refs):
    count = 1 + max(k for terms, _ in layout for k in terms)
    ins, outs = refs[:count], refs[count:]
    own, wide = outs[0].shape[1:]
    for c, (terms, first) in enumerate(layout):
        rows = slice(first, first + own)
        for t, ref in enumerate(outs):
            cols = slice(t * wide, (t + 1) * wide)
            total = ins[terms[0]][rows, cols].astype(F32)
            for k in terms[1:]:
                total = total + ins[k][rows, cols].astype(F32)
            ref[c] = total.T if t == turned else total


def finish(sides, kinds, own):
    arrays, layout = [], []
    for terms, first in sides:
        spots = []
        for term in terms:
            found = [k for k, a in enumerate(arrays) if a is term]
            if not found:
                arrays.append(term)
            spots.append(found[0] if found else len(arrays) - 1)
        layout.append((spots, first))
    wide = arrays[0].shape[1] // kinds
    shapes = [(len(sides), own, wide)] * (kinds - 1) + [(len(sides), wide, own)]
    return kernel_call(
        functools.partial(finish_body, layout, kinds - 1),
        (1,),
        arrays,
        [whole(a.shape) for a in arrays],
        [out_of(s, F32) for s in shapes],
        [whole(s) for s in shapes],
        0,
    )


def add_body(one, a, two, b, one_out, two_out):
    one_out[...] = (one[...].astype(F32) + a[...].astype(F32)).astype(BF)
    two_out[...] = (two[...].astype(F32) + b[...].astype(F32)).astype(BF)


def add_ends(one, a, two, b):
    rows, width = a.shape
    first = pl.BlockSpec((rows, width), lambda i: (0, 0))
    last = pl.BlockSpec((rows, width), lambda i: (one.shape[0] // rows - 1, 0))
    return kernel_call(
        add_body,
        (1,),
        (one, a, two, b),
        [first, first, last, first],
        [out_of(one.shape)] * 2,
        [first, last],
        0,
        alias={0: 0, 2: 1},
    )


class Ring:
    def __init__(self, size):
        self.size = size
        self.rings = size <= 16
        half = size // 2
        order = [2 * q for q in range(half)] + [2 * (size - 1 - q) + 1 for q in range(half, size)]
        self.ahead = [(order[q], order[(q + 1) % size]) for q in range(size)]
        self.behind = [(b, a) for a, b in self.ahead]
        self.me = lax.axis_index("dp")
        place = jnp.where(self.me % 2 == 0, self.me // 2, size - 1 - self.me // 2)
        q = lax.rem(place + jnp.arange(size, dtype=jnp.int32), size)
        self.order = jnp.where(q < half, 2 * q, 2 * (size - 1 - q) + 1).astype(jnp.int32)


class Rounds:
    def __init__(self):
        self.done = ()

    def now(self, value):
        return lax.optimization_barrier((value, *self.done))[0] if self.done else value

    def close(self, *arrays):
        self.done = arrays


class Gather:
    def __init__(self, rounds, ring, shard):
        self.rounds, self.ring = rounds, ring
        self.a, self.b = [shard], [shard]

    def step(self):
        a, b = self.a[-1], self.b[-1]
        if len(self.a) == self.ring.size // 2:
            half = a.shape[0] // 2
            a, b = a[:half], b[half:]
        self.a.append(lax.ppermute(self.rounds.now(a), "dp", self.ring.ahead))
        self.b.append(lax.ppermute(self.rounds.now(b), "dp", self.ring.behind))
        return self.a[-1], self.b[-1]

    def entries(self, part=0, parts=1):
        n = self.ring.size
        own = self.a[0].shape[0] // parts
        found = []
        for t in range(n):
            if t != n // 2:
                found.append((self.b[t] if t < n // 2 else self.a[n - t], t, 0, part * own, own))
            elif parts == 1:
                found.append((self.a[t], t, 0, 0, own // 2))
                found.append((self.b[t], t, own // 2, 0, own // 2))
            else:
                found.append(((self.a[t], self.b[t])[part], t, 0, 0, own))
        return found, own


class Scatter:
    def __init__(self, rounds, ring, blocks):
        self.rounds, self.ring = rounds, ring
        far = ring.size // 2
        self.a, self.b = blocks[far], blocks[far + 1]
        self.blocks = [*blocks[:far], None, *blocks[far + 2 :]]
        self.k = far

    def step(self):
        n = self.ring.size
        if self.k < n // 2:
            one, two = self.blocks[self.k], self.blocks[n - self.k]
            if self.k == n // 2 - 1:
                self.a, self.b = add_ends(one, self.a, two, self.b)
            else:
                self.a = (one.astype(F32) + self.a.astype(F32)).astype(BF)
                self.b = (two.astype(F32) + self.b.astype(F32)).astype(BF)
        self.k -= 1
        self.a = lax.ppermute(self.rounds.now(self.a), "dp", self.ring.ahead)
        self.b = lax.ppermute(self.rounds.now(self.b), "dp", self.ring.behind)
        return self.a, self.b

    def terms(self):
        return [self.blocks[0], self.a, self.b]


class HeadSum:
    def __init__(self, rounds, pair):
        size = lax.axis_size("mp")
        self.rounds, self.pair, self.got = rounds, pair, []
        self.near_moves = [(i, i ^ 1) for i in range(size)]
        self.far_moves = [(i, i ^ 2) for i in range(size)]

    def add(self, one, two):
        return (one.astype(F32) + two.astype(F32)).astype(BF)

    def near_start(self):
        self.near_got = lax.ppermute(self.rounds.now(self.pair[1]), "mp", self.near_moves)
        return self.near_got

    def near_add(self, mine):
        self.mine = self.add(mine, self.near_got)
        return self.mine

    def near(self):
        self.near_start()
        return self.near_add(self.pair[0])

    def far(self, part=1.0):
        start = sum(got.shape[0] for got in self.got)
        rows = int(self.mine.shape[0] * part)
        moved = self.rounds.now(self.mine[start : start + rows])
        self.got.append(lax.ppermute(moved, "mp", self.far_moves))
        return self.got[-1]

    def last(self):
        got = [self.rounds.now(got) for got in self.got]
        self.mine = self.add(self.mine, jnp.concatenate(got, 0))
        self.sum = (self.mine, lax.ppermute(self.mine, "mp", self.near_moves))
        return self.sum[1]


def exchange_steps(axes):
    for axis in axes:
        size, step = lax.axis_size(axis), 1
        while step < size:
            yield axis, [(i, i ^ step) for i in range(size)], step
            step *= 2


def on_device(
    layer_input, frame_mask, gain_attn, w_query, w_key, w_value, w_out, gain_ffn, w_gate, w_up,
    w_down, cotangent,
):
    sets, width = gain_attn.shape[0], layer_input.shape[2]
    shape = layer_input.shape
    each = shape[1] // sets
    ring = Ring(lax.axis_size("dp"))
    rings, n = ring.rings, ring.size
    far = n // 2 if rings else 0
    own = width // n
    places = jnp.concatenate([ring.order, (lax.axis_index("mp") % 2).astype(jnp.int32)[None]])
    gather = lambda value: lax.all_gather(value, "dp", tiled=True)
    scatter = lambda value: lax.psum_scatter(value, "dp", scatter_dimension=0, tiled=True)
    rounds = Rounds()
    now, close = rounds.now, rounds.close

    attn_own = pack_attn(w_query, w_key, w_value, w_out)
    small = jnp.concatenate([gain_attn, gain_ffn], 0).astype(F32)[None]
    steps = list(exchange_steps(("dp",)))
    ffn_own, x, g = [], [], []

    def gain_step(value):
        axis, moves, step = steps.pop(0)
        other = lax.ppermute(now(value), axis, moves)
        bit = (ring.me // step) % 2
        both = [jnp.concatenate(pair, 0) for pair in ((value, other), (other, value))]
        return jnp.where(bit == 0, *both)

    masks = frame_mask.astype(BF)[:, None, None]
    chores = [
        lambda: ffn_own.append(pack_ffn(now(w_gate), w_up, w_down, 0)),
        lambda: x.append(split_sets(now(layer_input), sets)[0]),
        lambda: ffn_own.append(pack_ffn(now(w_gate), w_up, w_down, 1)),
        lambda: x.append(split_sets(now(layer_input), sets)[1]),
        lambda: g.append(split_sets(now(cotangent) * masks, sets)[0]),
        lambda: g.append(split_sets(now(cotangent) * masks, sets)[1]),
    ]
    attn = Gather(rounds, ring, attn_own)
    for k in range(max(far, 3)):
        moved = attn.step() if rings else ()
        if rings and k == far - 1:
            rows = [Gather(rounds, ring, shard) for shard in ffn_own]
            moved += rows[0].step()
        for chore in chores[:2]:
            chore()
        del chores[:2]
        if steps and k != 2:
            small = gain_step(small)
        close(small, *moved, *[v[-1] for v in (ffn_own, x, g) if v])
    while steps:
        small = gain_step(small)
    gains = small.transpose(1, 0, 2).reshape(2 * sets, width)
    g_attn, g_ffn = [[gains[k * sets + c][None] for c in range(sets)] for k in range(2)]
    if rings:
        w_attn = [attn.entries(c, sets) for c in range(sets)]
    else:
        both = gather(attn_own).reshape(n, sets, own, -1)
        w_attn = [([(both[:, c].reshape(width, -1), None, 0, 0, width)], width) for c in range(sets)]

    def move(c):
        return rows[c].step() if rings else ()

    def weights(c):
        if rings:
            return rows[c].entries()
        return [(gather(ffn_own[c]), None, 0, 0, width)], width

    h1, qkv, mixed, heads = [None] * 2, [None] * 2, [None] * 2, [None] * 2
    moved = move(0)
    h1[0], qkv[0], mixed[0], part = attend(now(places), x[0], g_attn[0], None, w_attn[0], each)
    heads[0] = HeadSum(rounds, part)
    close(*moved, part[0])
    moved = move(0)
    heads[0].near()
    got = heads[0].far()
    h1[1], qkv[1], mixed[1], part = attend(now(places), x[1], g_attn[1], qkv[0], w_attn[1], each)
    heads[1] = HeadSum(rounds, part)
    held, rounds.done = rounds.done, (*rounds.done, part[0])
    moved += move(0)
    rounds.done = held
    close(*moved, part[0], got)
    moved = move(1)
    close(heads[1].near(), heads[0].last())

    def grads_of(c, out):
        columns = [(out[0], out[2]), (g[c], out[1])]
        return weight_grads(now(places), [columns], far)

    dh, mlp, grads, dm, d_gain_ffn = ([None] * 2 for _ in range(5))
    got = heads[1].far(0.5)
    ffn = (x[0], heads[0].sum, g[0], g_ffn[0], weights(0))
    out, other = hidden_units(now(places), *ffn, half=1)
    close(*moved, other, got)
    moved = move(1)
    got = heads[1].far(0.5)
    dh[0], mlp[0] = HeadSum(rounds, (None, other)), HeadSum(rounds, None)
    near = dh[0].near_start()
    out, mine = hidden_units(now(places), *ffn, half=0, filled=out)
    close(*moved, mine, got, near)
    dh[0].near_got, mlp[0].near_got = near[0], near[1]
    dh[0].near_add(mine[0])
    mlp[0].near_add(mine[1])
    moved = move(1)
    got = dh[0].far(0.5)
    grads[0] = grads_of(0, out)
    close(*moved, grads[0][0], got, heads[1].last())
    att = [head.sum for head in heads]
    sums = [Scatter(rounds, ring, grads[0])] if rings else []
    add = lambda k: sums[k].step() if rings else ()
    close(*move(1), *add(0), dh[0].far(0.5))

    moved = (*add(0), dh[0].last())
    got = mlp[0].far(0.5)
    ffn = (x[1], att[1], g[1], g_ffn[1], weights(1))
    out, other = hidden_units(now(places), *ffn, half=1)
    close(*moved, other, got)
    moved = add(0)
    got = mlp[0].far(0.5)
    dh[1], mlp[1] = HeadSum(rounds, (None, other)), HeadSum(rounds, None)
    near = dh[1].near_start()
    out, mine = hidden_units(now(places), *ffn, half=0, filled=out)
    close(*moved, mine, got, near)
    dh[1].near_got, mlp[1].near_got = near[0], near[1]
    dh[1].near_add(mine[0])
    mlp[1].near_add(mine[1])
    moved = add(0)
    got = dh[1].far()
    grads[1] = grads_of(1, out)
    if rings:
        sums.append(Scatter(rounds, ring, grads[1]))
        moved += add(1)
    dm[0], d_gain_ffn[0] = middle_back(now(places), x[0], att[0], g[0], dh[0].sum, g_ffn[0])
    close(*moved, grads[1][0], dm[0], got)
    close(dh[1].last(), mlp[0].last())

    moved = add(1)
    got = mlp[1].far(0.75)
    backward = (x, g[1], dm[0], att[1], dh[1].sum, g_ffn[1], qkv, w_attn)
    found, part, d_gain0 = attend_back(now(places), *backward, 0, (), each)
    back = [HeadSum(rounds, part)]
    close(*moved, part[0], got)
    moved = (*add(1), back[0].near(), mlp[1].far(0.25))
    (*d_qkv, dm[1]), part, d_gain1 = attend_back(now(places), *backward, 1, found, each)
    back.append(HeadSum(rounds, part))
    close(*moved, part[0])

    shared = lax.axis_size("mp")
    d_gain_attn, d_gain_ffn[1] = (one + two for one, two in zip(d_gain0, d_gain1))
    d_gains = jnp.concatenate([d_gain_attn, *[d / shared for d in d_gain_ffn]], 0)
    steps = list(exchange_steps(("mp", "dp")))

    def sum_step(value, *earlier):
        axis, moves, _ = steps.pop(0)
        got = lax.ppermute(now(value), axis, moves)
        return value + lax.optimization_barrier((got, *earlier))[0]

    moved = (*add(1), back[1].near())
    got = back[0].far(0.75)
    d_gains = sum_step(sum_step(d_gains))
    runs = [[(h1[c], d_qkv[c]), (dm[c], mixed[c])] for c in range(sets)]
    if rings:
        blocks = weight_grads(now(places), runs, far)
        sums.append(Scatter(rounds, ring, blocks))
    else:
        blocks = [weight_grads(now(places), [run], far)[0] for run in runs]
    close(*moved, blocks[0], got, d_gains)
    moved = (*add(2), mlp[1].last())
    got = back[0].far(0.25)
    d_gains = sum_step(d_gains)
    if rings:
        ffn_sums = [([now(t) for t in s.terms()], 0) for s in sums[:2]]
    else:
        ffn_sums = [([scatter(b[0])], 0) for b in grads]
    d_gate_w, d_up_w, d_down_w = finish(ffn_sums, 3, own)
    close(*moved, d_gains, d_gate_w, got)
    moved = (*add(2), back[0].last())
    d_gains = sum_step(d_gains)
    got = back[1].far(0.5)
    output = output_of(now(places), x, att, [m.sum for m in mlp], shape)
    close(*moved, d_gains, got, output)
    moved = add(2)
    while steps:
        d_gains = sum_step(d_gains)
    got = back[1].far(0.5)
    grad_input = input_back(now(places), x, dm, back[0].sum, gains[:sets], 0, None, shape)
    close(*moved, grad_input, d_gains, got)
    moved = add(2)
    back[1].last()
    grad_input = input_back(now(places), x, dm, back[1].sum, gains[:sets], 1, grad_input, shape)
    close(*moved, grad_input)
    if rings:
        terms = [now(t) for t in sums[2].terms()]
        attn_sums = [(terms, c * own) for c in range(sets)]
    else:
        attn_sums = [([scatter(b)], 0) for b in blocks]
    d_query, d_key, d_value, d_out = finish(attn_sums, 4, own)
    d_gains = lax.dynamic_slice_in_dim(d_gains, ring.me * own, own, 1)
    return (
        output, grad_input, d_gains[:sets], d_query, d_key, d_value, d_out,
        d_gains[sets:], d_gate_w, d_up_w, d_down_w,
    )


def solution(mesh):
    rows = P("dp", None, None)
    gain = P(None, "dp")
    into = P(None, "dp", "mp")
    back = P(None, "mp", "dp")
    weights = (gain, into, into, into, back, gain, into, into, back)
    return jax.shard_map(
        on_device,
        mesh=mesh,
        in_specs=(rows, P("dp"), *weights, rows),
        out_specs=(rows, rows, *weights),
        check_vma=False,
    )
```
